32 devices in a mesh: gx: 4 (over x, core), gy: 4 (over z), gz: 2 (over y).
Axes of the slice: x: 2, y: 2, z: 4, core: 2. Of those that a mesh axis runs over, the one named last changes fastest.
Arguments:
- offsets: float32 [3, 131072], P(None, ('gx', 'gy', 'gz')), may hold values from -0.5 to 0.5
- velocity: float32 [3, 131072], P(None, ('gx', 'gy', 'gz')), may hold values from -6 to 6
- affine: float32 [9, 131072], P(None, ('gx', 'gy', 'gz')), may hold values from -6 to 6
- volume: float32 [131072], P(('gx', 'gy', 'gz')), may hold values from 0.8 to 1.2
- cot_velocity: float32 [3, 131072], P(None, ('gx', 'gy', 'gz')), may hold values from -6 to 6
- cot_affine: float32 [9, 131072], P(None, ('gx', 'gy', 'gz')), may hold values from -3 to 3
- block_cells: int32 [1024], P(('gx', 'gy', 'gz')), may hold values from 0 to 511
- fill_counts: int32 [32], P(('gx', 'gy', 'gz')), may hold values from 2 to 32, as said below
- baffle_top: int32 [128, 128], P('gx', 'gy'), may hold values from 0 to 16
- drag: float32 [128, 128, 16], P('gx', 'gy', 'gz'), may hold values from 0.2 to 0.9
Outputs:
- grad_velocity: float32 [3, 131072], P(None, ('gx', 'gy', 'gz'))
- grad_affine: float32 [9, 131072], P(None, ('gx', 'gy', 'gz'))
- grad_volume: float32 [131072], P(('gx', 'gy', 'gz'))
- grad_drag: float32 [128, 128, 16], P('gx', 'gy', 'gz')
The draws below stay inside these ranges and needn't reach their ends.
Inputs may be any that keep to these rules, and one draw needn't show every extreme that they name: Blocks 0 to fill_counts - 1 of a device are live, its other slots are padding; in every draw some device has all 32 blocks live.
All inputs are finite; a program needn't handle non-finite values.
Results may differ from the reference program's by a relative error of at most 0.00011.
Values sent between devices are 32-bit elements; how exact they have to be, the bound alone decides.
No kernel may reach another device: no remote copies, remote signals or barrier semaphores. Data moves between devices by JAX's collectives and lax.ppermute only.
A program may use at most 64 MiB of HBM per device.

```python
import jax
import jax.numpy as jnp
from jax import lax

CX = 32
CY = 32
CZ = 8
BLOCKS = 32
PER_BLOCK = 128
NX = 128
NY = 128
NZ = 16
NBLK = 1024
P_TOTAL = 131072
N_GX = 4
N_GY = 4
N_GZ = 2
DEVICES = 32


def draw_fill_counts(key, part):
    key = jax.random.fold_in(key, 7)
    first_key, second_key, third_key = jax.random.split(key, 3)
    lowest = BLOCKS // 16
    first_draw = jax.random.randint(first_key, (DEVICES,), lowest, BLOCKS + 1)
    second_draw = jax.random.randint(second_key, (DEVICES,), lowest, BLOCKS + 1)
    counts = jnp.minimum(first_draw, second_draw)
    fullest = jax.random.randint(third_key, (), 0, DEVICES)
    return counts.at[fullest].set(BLOCKS).astype(jnp.int32)


def touch_ends(result, rng, least, top_value):
    dims = result.shape
    place = [jax.random.randint(jax.random.fold_in(rng, axis), (), 0, dims[axis]) for axis in range(len(dims))]
    result = result.at[tuple(place)].set(least)
    longest = dims.index(max(dims))
    place[longest] = (place[longest] + 1) % dims[longest]
    return result.at[tuple(place)].set(top_value)


def steps_of(own_key, extent, shards, least, top_value):
    factor_of = 1.0
    for dim, parts in shards:
        steps = jax.random.uniform(jax.random.fold_in(jax.random.fold_in(own_key, 6), dim), (parts,), jnp.float32, least / len(shards), top_value / len(shards))
        factor_of = factor_of * jnp.repeat(jnp.exp(steps), extent[dim] // parts).reshape((-1,) + (1,) * (len(extent) - 1 - dim))
    return factor_of


def gaussian(own_key, extent, scale, limit, cuts=(), held_as=jnp.bfloat16):
    loudness = steps_of(own_key, extent, cuts, -0.22, 0.18) if cuts else 1.0
    values = jax.random.normal(own_key, extent, jnp.float32) * scale * loudness
    return jnp.minimum(jnp.maximum(values, -limit), limit).astype(held_as)


def setup_inputs(seed: int = 0) -> dict:
    seeds = jax.random.split(jax.random.key(seed), 11)
    return {
        "offsets": jnp.clip(jax.random.uniform(seeds[0], (3, P_TOTAL), jnp.float32, -0.5, 0.5) * steps_of(seeds[0], (3, P_TOTAL), ((1, 32),), -0.4, 0.0), -0.5, 0.5),
        "velocity": gaussian(seeds[1], (3, P_TOTAL), 1.0, 6.0, ((1, 32),), jnp.float32),
        "affine": gaussian(seeds[2], (9, P_TOTAL), 1.0, 6.0, ((1, 32),), jnp.float32),
        "volume": jnp.clip(0.8 + 0.40000004 * jax.random.uniform(seeds[3], (P_TOTAL,), jnp.float32) ** steps_of(seeds[3], (P_TOTAL,), ((0, 32),), -0.2, 0.2), 0.8, 1.2),
        "cot_velocity": gaussian(seeds[4], (3, P_TOTAL), 1.0, 6.0, ((1, 32),), jnp.float32),
        "cot_affine": gaussian(seeds[5], (9, P_TOTAL), 0.5, 3.0, ((1, 32),), jnp.float32),
        "block_cells": touch_ends(jax.random.randint(seeds[6], (NBLK,), 0, CX * CY * CZ // 16), jax.random.fold_in(seeds[6], 1), 0, (CX * CY * CZ // 16) - 1).astype(jnp.int32),
        "fill_counts": draw_fill_counts(jax.random.fold_in(seeds[10], 71), 0),
        "baffle_top": touch_ends(jax.random.randint(seeds[8], (NX, NY), 0, NZ + 1), jax.random.fold_in(seeds[8], 1), 0, NZ).astype(jnp.int32),
        "drag": jnp.clip(0.2 + 0.7 * jax.random.uniform(seeds[9], (NX, NY, NZ), jnp.float32) ** steps_of(seeds[9], (NX, NY, NZ), ((0, 4), (1, 4), (2, 2)), -0.2, 0.2), 0.2, 0.9),
    }


stiffness = 2.0
gravity_step = 0.3


def node_window():
    node_ids = jnp.arange(96, dtype=jnp.int32)
    return jnp.stack([node_ids // 24 - 1, (node_ids // 6) % 4 - 1, node_ids % 6 - 1])


def local_cells(per_rows):
    cell_ids = jnp.arange(per_rows, dtype=jnp.int32) // 8
    return jnp.stack([cell_ids // 8, (cell_ids // 4) % 2, cell_ids % 4])


def axis_weights(frac, local, span):
    spline = jnp.stack([0.5 * (0.5 - frac) ** 2, 0.75 - frac * frac, 0.5 * (0.5 + frac) ** 2])
    window_ids = jnp.arange(span, dtype=jnp.int32)[:, None, None]
    targets = local[None, None, :] + jnp.arange(3, dtype=jnp.int32)[None, :, None]
    hits = (window_ids == targets).astype(jnp.float32)
    return jnp.sum(hits[:, :, None, :] * spline[None], axis=1)


def block_weights(position):
    local = local_cells(position.shape[2])
    weight_x = axis_weights(position[0], local[0], 4)
    weight_y = axis_weights(position[1], local[1], 4)
    weight_z = axis_weights(position[2], local[2], 6)
    product = weight_x[:, None, None] * weight_y[None, :, None] * weight_z[None, None, :]
    return product.reshape((96,) + position.shape[1:])


def shifted(position):
    return position + local_cells(position.shape[2]).astype(jnp.float32)[:, None, :]


def forward_terms(position, speeds, matrices, ratios, alive):
    block_count, per_rows = position.shape[1], position.shape[2]
    weight = block_weights(position)
    placed = shifted(position)
    alive_rows = alive[:, None]
    identity = jnp.eye(3, dtype=jnp.float32).reshape(9)[:, None, None]
    stress = alive_rows * (matrices - stiffness * (ratios - 1.0) * identity)
    linear = alive_rows * speeds - jnp.sum(stress.reshape(3, 3, block_count, per_rows) * placed[None], axis=1)
    masses = jnp.broadcast_to(alive_rows[None], (1, block_count, per_rows))
    stacked = jnp.concatenate([masses, linear, stress], axis=0)
    node_sums = jnp.einsum("nkp,ckp->ckn", weight, stacked, precision=lax.Precision.HIGHEST)
    offset_table = node_window().astype(jnp.float32)
    momentum = node_sums[1:4] + jnp.einsum("abkn,bn->akn", node_sums[4:].reshape(3, 3, block_count, 96), offset_table, precision=lax.Precision.HIGHEST)
    return jnp.concatenate([node_sums[:1], momentum], axis=0)


def adjoint_terms(position, cot_speeds, cot_matrices, alive):
    block_count, per_rows = position.shape[1], position.shape[2]
    weight = block_weights(position)
    placed = shifted(position)
    alive_rows = alive[:, None]
    linear = alive_rows * (cot_speeds - 4.0 * jnp.sum(cot_matrices.reshape(3, 3, block_count, per_rows) * placed[None], axis=1))
    scaled = 4.0 * alive_rows * cot_matrices
    stacked = jnp.concatenate([linear, scaled], axis=0)
    node_sums = jnp.einsum("nkp,ckp->ckn", weight, stacked, precision=lax.Precision.HIGHEST)
    offset_table = node_window().astype(jnp.float32)
    return node_sums[:3] + jnp.einsum("abkn,bn->akn", node_sums[3:].reshape(3, 3, block_count, 96), offset_table, precision=lax.Precision.HIGHEST)


def pull_back(position, gathered, alive):
    block_count, per_rows = position.shape[1], position.shape[2]
    weight = block_weights(position)
    placed = shifted(position)
    alive_rows = alive[:, None]
    offset_table = node_window().astype(jnp.float32)
    spread = (gathered[:, None] * offset_table[None, :, None, :]).reshape(9, block_count, 96)
    stacked = jnp.concatenate([gathered, spread], axis=0)
    pulled = jnp.einsum("nkp,ckn->ckp", weight, stacked, precision=lax.Precision.HIGHEST)
    speed_grad = alive_rows * pulled[:3]
    matrix_grad = (alive_rows * (pulled[3:].reshape(3, 3, block_count, per_rows) - pulled[:3][:, None] * placed[None])).reshape(9, block_count, per_rows)
    ratio_grad = -stiffness * (matrix_grad[0] + matrix_grad[4] + matrix_grad[8])
    return jnp.concatenate([speed_grad, matrix_grad, ratio_grad[None]], axis=0)


def reference(offsets, velocity, affine, volume, cot_velocity, cot_affine, block_cells, fill_counts, baffle_top, drag):
    devices = N_GX * N_GY * N_GZ

    def split_devices(array, channels):
        return jnp.moveaxis(array.reshape(channels, devices, BLOCKS, PER_BLOCK), 1, 0)

    positions = split_devices(offsets, 3)
    speeds = split_devices(velocity, 3)
    matrices = split_devices(affine, 9)
    ratios = split_devices(volume[None], 1)
    cot_speeds = split_devices(cot_velocity, 3)
    cot_matrices = split_devices(cot_affine, 9)
    slot_index = jnp.arange(BLOCKS, dtype=jnp.int32)
    live_blocks = (slot_index[None, :] < fill_counts[:, None]).astype(jnp.float32)

    def deposit(pieces):
        position, speed, matrix, ratio, cot_speed, cot_matrix, alive = pieces
        return jnp.concatenate([forward_terms(position, speed, matrix, ratio[0], alive), adjoint_terms(position, cot_speed, cot_matrix, alive)], axis=0)

    node_terms = lax.map(deposit, (positions, speeds, matrices, ratios, cot_speeds, cot_matrices, live_blocks))
    node_terms = jnp.moveaxis(node_terms, 1, 0).reshape(7, -1)

    block_ids = jnp.arange(NBLK, dtype=jnp.int32)
    device = block_ids // BLOCKS
    tiles_y = CY // 2
    tiles_z = CZ // 4
    glob_x = (device // (N_GY * N_GZ)) * CX + 2 * (block_cells // (tiles_y * tiles_z))
    glob_y = ((device // N_GZ) % N_GY) * CY + 2 * ((block_cells // tiles_z) % tiles_y)
    glob_z = (device % N_GZ) * CZ + 4 * (block_cells % tiles_z)
    node_steps = node_window()
    node_x = glob_x[:, None] + node_steps[0][None, :]
    node_y = glob_y[:, None] + node_steps[1][None, :]
    node_z = glob_z[:, None] + node_steps[2][None, :]
    inside = (node_x >= 0) & (node_x < NX) & (node_y >= 0) & (node_y < NY) & (node_z >= 0) & (node_z < NZ)
    cell_total = NX * NY * NZ
    flat_index = jnp.where(inside, (node_x * NY + node_y) * NZ + node_z, cell_total).reshape(-1).astype(jnp.int32)
    entries = flat_index.shape[0]
    sort_order = jnp.argsort(flat_index, stable=True).astype(jnp.int32)
    ordered = flat_index[sort_order]
    new_segment = jnp.concatenate([jnp.zeros((1,), jnp.int32), (ordered[1:] != ordered[:-1]).astype(jnp.int32)])
    segment_sorted = jnp.cumsum(new_segment).astype(jnp.int32)
    segment = jnp.zeros((entries,), jnp.int32).at[sort_order].set(segment_sorted)
    segment_sums = jax.ops.segment_sum(node_terms.T, segment, num_segments=entries)
    cell_index = jnp.full((entries,), cell_total, jnp.int32).at[segment].min(flat_index)
    inside_cell = (cell_index < cell_total).astype(jnp.float32)
    safe_cell = jnp.minimum(cell_index, cell_total - 1).astype(jnp.int32)
    cell_x = safe_cell // (NY * NZ)
    cell_y = (safe_cell // NZ) % NY
    cell_z = safe_cell % NZ
    baffle = (cell_z < baffle_top[cell_x, cell_y]).astype(jnp.float32) * inside_cell
    drag_at = drag.reshape(-1)[safe_cell]
    mass_floor = jnp.maximum(segment_sums[:, 0], 1.0)
    gravity = jnp.array([0.0, 0.0, -gravity_step], dtype=jnp.float32)
    grid_velocity = segment_sums[:, 1:4] / mass_floor[:, None] + gravity[None, :]
    node_adjoint = segment_sums[:, 4:7]
    grad_cell = -baffle * jnp.sum(node_adjoint * grid_velocity, axis=1)
    grad_drag = jnp.zeros((cell_total,), jnp.float32).at[cell_index].set(grad_cell, mode="drop").reshape(NX, NY, NZ)
    node_grad = inside_cell[:, None] * node_adjoint * (1.0 - baffle * drag_at)[:, None] / mass_floor[:, None]
    per_entry = node_grad[segment].reshape(devices, BLOCKS, 96, 3)
    per_entry = jnp.transpose(per_entry, (0, 3, 1, 2))

    def collect(pieces):
        position, gathered, alive = pieces
        return pull_back(position, gathered, alive)

    particle_grads = lax.map(collect, (positions, per_entry, live_blocks))
    particle_grads = jnp.moveaxis(particle_grads, 0, 1).reshape(13, -1)
    return particle_grads[:3], particle_grads[3:12], particle_grads[12], grad_drag
```

```python
import functools

import jax
import jax.numpy as jnp
from jax import lax
from jax.experimental import pallas as pl
from jax.experimental.pallas import tpu as pltpu
from jax.sharding import PartitionSpec as P

stiffness = 2.0
gravity_step = 0.3

LANES = 128
SLABS = 4
ZROWS = 10
CHANNELS = 8
ROWS = ZROWS * CHANNELS
F32 = jnp.float32
BF16 = jnp.bfloat16


def iota(shape, dim):
    return lax.broadcasted_iota(jnp.int32, shape, dim)


def tile_nodes(tile, rows, brick):
    lane = iota((rows, LANES), 1)
    if tile < 2:
        x, y = lane >> 1, (lane & 1) + tile * brick
        valid = lane < 2 * (brick + 2)
    else:
        x = (lane >> 5) + ((0, brick)[tile - 2] if tile < SLABS else 4 * (tile - SLABS) + 1)
        y = (lane & 31) + 1
        valid = (y >= 2) & (y < brick)
        valid = valid & ((lane < 64) if tile < SLABS else ((x >= 2) & (x < brick)))
    return x, y, valid


def tile_code(tile, rows, brick):
    x, y, valid = tile_nodes(tile, rows, brick)
    return jnp.where(valid, x * 64 + y, -1)


def block_columns(cells_ref, blocks):
    row = iota((blocks, LANES), 0)
    cells = jnp.zeros((blocks, LANES), jnp.int32)
    for b in range(blocks):
        cells = jnp.where(row == b, cells_ref[b], cells)
    code = (cells >> 5) * 128 + ((cells >> 1) & 15) * 2
    return code, cells & 1


def fill_one_hot(hot_ref, code, blocks, tiles, brick):
    for tile in range(tiles):
        lane_code = tile_code(tile, blocks, brick) - code
        for node in range(16):
            hit = lane_code == (node // 4) * 64 + node % 4
            hot_ref[pl.ds(node * blocks, blocks), pl.ds(tile * LANES, LANES)] = jnp.where(hit, 1.0, 0.0).astype(BF16)


def spline(frac):
    return [0.5 * (0.5 - frac) ** 2, 0.75 - frac * frac, 0.5 * (0.5 + frac) ** 2]


def split(value):
    high = value.astype(BF16)
    return high, (value - high.astype(F32)).astype(BF16)


def is_even(axis):
    return lax.rem(lax.axis_index(axis), 2) == 0


def low_high(even, odd, axis):
    here = is_even(axis)
    return jnp.where(here, odd, even), jnp.where(here, even, odd)


def to_rows(flat_ref, first, array_ref, blocks):
    channels = array_ref.shape[0]
    for b in range(blocks):
        flat_ref[pl.ds(first * blocks + b, channels, stride=blocks), :] = array_ref[:, pl.ds(b * LANES, LANES)]


def from_rows(array_ref, flat_ref, first, blocks):
    channels = array_ref.shape[0]
    for b in range(blocks):
        array_ref[:, pl.ds(b * LANES, LANES)] = flat_ref[pl.ds(first * blocks + b, channels, stride=blocks), :]


def corners(low, high):
    lane = iota(low.shape, 1)
    first, last = lane < 4, (lane >= 64) & (lane < 68)
    zero = jnp.zeros_like(low)
    lower = jnp.where(first, pltpu.roll(low, 64, 1), jnp.where(last, high, zero))
    upper = jnp.where(first, pltpu.roll(low, 60, 1), jnp.where(last, pltpu.roll(high, 124, 1), zero))
    return lower, upper


def deposit_kernel(
    cells_ref, count_ref, pos_ref, vel_ref, aff_ref, vol_ref, cvel_ref, caff_ref, top_ref, drag_ref,
    grid_ref, even_ref, odd_ref,
    flat_ref, terms_ref, spread_ref, sums_ref, window_ref, hot_ref, all_ref,
):
    blocks = vol_ref.shape[0]
    brick = drag_ref.shape[0]
    size_z = drag_ref.shape[1]
    tiles = grid_ref.shape[0]
    for first, ref in ((0, pos_ref), (3, vel_ref), (6, aff_ref), (15, cvel_ref), (18, caff_ref)):
        to_rows(flat_ref, first, ref, blocks)

    def channel(c):
        return flat_ref[pl.ds(c * blocks, blocks), :]

    code, upper_tile = block_columns(cells_ref, blocks)
    live = (iota((blocks, LANES), 0) < count_ref[0]).astype(F32)
    frac = [channel(k) for k in range(3)]
    weight = [spline(f) for f in frac]
    stretch = stiffness * (vol_ref[...] - 1.0)
    linear, matrix = [live], [None]
    for a in range(3):
        row = [live * (channel(6 + 3 * a + b) - (stretch if a == b else 0.0)) for b in range(3)]
        matrix.append(row)
        linear.append(live * channel(3 + a) - sum(row[b] * frac[b] for b in range(3)))
    for a in range(3):
        row = [(4.0 * live) * channel(18 + 3 * a + b) for b in range(3)]
        matrix.append(row)
        linear.append(live * channel(15 + a) - sum(row[b] * frac[b] for b in range(3)))

    def put(row, slot, value):
        high, low = split(value)
        lanes = pl.ds(slot * LANES, LANES)
        terms_ref[pl.ds(row * blocks, blocks), lanes] = high
        terms_ref[pl.ds((9 + row) * blocks, blocks), lanes] = low

    for ox in range(3):
        for oy in range(3):
            planar = weight[0][ox] * weight[1][oy]
            weights = [planar * weight[2][oz] for oz in range(3)]
            for c in range(7):
                base = linear[c]
                if c:
                    if ox != 1:
                        base = base + matrix[c][0] if ox else base - matrix[c][0]
                    if oy != 1:
                        base = base + matrix[c][1] if oy else base - matrix[c][1]
                for oz in range(3):
                    value = base
                    if c and oz != 1:
                        value = base + matrix[c][2] if oz else base - matrix[c][2]
                    put(3 * ox + oy, 3 * c + oz, weights[oz] * value)

    particle = iota((LANES, 2 * LANES), 0)
    shift = iota((LANES, 2 * LANES), 1) - ((particle >> 5) * 64 + ((particle >> 3) & 3) * 8)
    for c in range(7):
        for oz in range(3):
            hit = shift == oz * 8 + c
            spread_ref[pl.ds((3 * c + oz) * LANES, LANES), :] = jnp.where(hit, 1.0, 0.0).astype(BF16)
    sums_ref[...] = jnp.dot(terms_ref[...], spread_ref[...], preferred_element_type=F32)

    fill_one_hot(hot_ref, code, blocks, tiles, brick)

    lane = iota((blocks, LANES), 1)
    low_half = lane < 64
    own_half = low_half == (upper_tile == 0)

    def partial(wx, oy):
        total = None
        for cx in range(2):
            ox = wx - cx
            if 0 <= ox < 3:
                lanes = pl.ds(cx * LANES, LANES)
                row = 3 * ox + oy
                piece = sums_ref[pl.ds(row * blocks, blocks), lanes] + sums_ref[pl.ds((9 + row) * blocks, blocks), lanes]
                total = piece if total is None else total + piece
        return total

    for wx in range(4):
        columns = [partial(wx, oy) for oy in range(3)]
        zero = jnp.zeros_like(columns[0])
        for wy in range(4):
            both = jnp.where(low_half, columns[wy] if wy < 3 else zero, columns[wy - 1] if wy else zero)
            node = jnp.where(own_half, both + pltpu.roll(both, 64, 1), 0.0)
            high, low = split(node)
            rows = pl.ds((4 * wx + wy) * blocks, blocks)
            window_ref[rows, pl.ds(0, LANES)] = high
            window_ref[rows, pl.ds(LANES, LANES)] = low

    all_ref[...] = lax.dot_general(
        window_ref[...], hot_ref[...], (((0,), (0,)), ((), ())), preferred_element_type=F32
    )
    for z in range(ZROWS):
        piece = None
        for tz in range(2):
            wz = z - 4 * tz
            if 0 <= wz < 6:
                row = 64 * tz + 8 * wz
                part = all_ref[pl.ds(row, 8), :] + all_ref[pl.ds(128 + row, 8), :]
                piece = part if piece is None else piece + part
        for tile in range(tiles):
            grid_ref[tile, pl.ds(8 * z, 8), :] = piece[:, tile * LANES : (tile + 1) * LANES]

    depth = iota((size_z, brick), 0) + lax.axis_index("gz") * size_z
    lane = iota((size_z, LANES), 1)
    zero = jnp.zeros((size_z, LANES), F32)
    ends = [zero, zero]
    layers = []
    for x in range(brick):
        layer = jnp.where(depth < top_ref[pl.ds(x, 1), :], drag_ref[x], 0.0)
        layers.append(layer)
        ends[0] = jnp.where(lane == 2 * (x + 1) + 1, layer[:, 0:1], ends[0])
        ends[1] = jnp.where(lane == 2 * (x + 1), layer[:, brick - 1 : brick], ends[1])
    blank = jnp.zeros((size_z, 32), F32)
    planes = ends + [
        jnp.concatenate([blank, layers[0], blank, blank], axis=1),
        jnp.concatenate([layers[-1], blank, blank, blank], axis=1),
    ]
    for t in range(brick // 4):
        planes.append(jnp.concatenate(layers[4 * t : 4 * t + 4], axis=1))
    for tile, plane in enumerate(planes):
        grid_ref[tile, pl.ds(8 + 7, size_z, stride=8), :] = plane

    lane = iota((ROWS, LANES), 1)
    slab = [grid_ref[t] for t in range(SLABS)]
    low = jnp.where(lane < 64, slab[2], jnp.where(lane < 68, pltpu.roll(slab[0], 64, 1), pltpu.roll(slab[1], 68, 1)))
    high = jnp.where(lane < 64, slab[3], jnp.where(lane < 68, slab[0], pltpu.roll(slab[1], 4, 1)))
    here = is_even("gx")
    even_ref[...] = jnp.where(here, high, low)
    odd_ref[...] = jnp.where(here, low, high)


def pack_y_kernel(slab_ref, xe_ref, xo_ref, even_ref, odd_ref):
    low, high = low_high(xe_ref[...], xo_ref[...], "gx")
    lower, upper = corners(low, high)
    lower = slab_ref[0] + lower
    upper = slab_ref[1] + upper
    here = is_even("gy")
    even_ref[...] = jnp.where(here, upper, lower)
    odd_ref[...] = jnp.where(here, lower, upper)


def slab_additions(xe, xo, ye, yo):
    low_x, high_x = low_high(xe, xo, "gx")
    low_y, high_y = low_high(ye, yo, "gy")
    lower, upper = corners(low_x, high_x)
    planar = iota(low_x.shape, 1) < 64
    return [low_y + lower, high_y + upper, jnp.where(planar, low_x, 0.0), jnp.where(planar, high_x, 0.0)]


def pack_z_kernel(grid_ref, xe_ref, xo_ref, ye_ref, yo_ref, even_ref, *odd_refs):
    here = is_even("gz")
    ends = []
    for first in (0, ROWS - 16):
        rows = pl.ds(first, 16)
        extra = slab_additions(xe_ref[rows, :], xo_ref[rows, :], ye_ref[rows, :], yo_ref[rows, :])
        ends.append([grid_ref[t, rows, :] + (extra[t] if t < SLABS else 0.0) for t in range(grid_ref.shape[0])])
    for tile, (lower, upper) in enumerate(zip(*ends)):
        even_ref[tile] = jnp.where(here, upper, lower)
        for odd_ref in odd_refs:
            odd_ref[tile] = jnp.where(here, lower, upper)


def collect_kernel(counts, cells_ref, count_ref, pos_ref, top_ref, grid_ref, xe_ref, xo_ref, ye_ref, yo_ref, *refs):
    received_z = refs[: -11]
    gvel_ref, gaff_ref, gvol_ref, gdrag_ref = refs[-11:-7]
    total_ref, push_ref, hot_ref, take_ref, spread_ref, pulled_ref, flat_ref = refs[-7:]
    blocks = gvol_ref.shape[0]
    brick, size_z = gdrag_ref.shape[0], gdrag_ref.shape[1]
    tiles = grid_ref.shape[0]
    to_rows(flat_ref, 0, pos_ref, blocks)
    frac = [flat_ref[pl.ds(k * blocks, blocks), :] for k in range(3)]
    weight = [spline(f) for f in frac]
    code, upper_tile = block_columns(cells_ref, blocks)
    fill_one_hot(hot_ref, code, blocks, tiles, brick)

    here = is_even("gz")
    extra = slab_additions(xe_ref[...], xo_ref[...], ye_ref[...], yo_ref[...])
    for tile in range(tiles):
        even = received_z[0][tile]
        odd = received_z[1][tile] if len(received_z) > 1 else jnp.zeros_like(even)
        total_ref[tile, pl.ds(0, ROWS), :] = grid_ref[tile] + extra[tile] if tile < SLABS else grid_ref[tile]
        total_ref[tile, pl.ds(ROWS, 16), :] = jnp.zeros((16, LANES), F32)
        total_ref[tile, pl.ds(0, 16), :] += jnp.where(here, odd, even)
        total_ref[tile, pl.ds(ROWS - 16, 16), :] += jnp.where(here, even, odd)

    place = [lax.axis_index(axis) for axis in ("gx", "gy", "gz")]
    edges = []
    row = iota((8, LANES), 0)
    blank = jnp.zeros((8, LANES), F32)
    for tile in range(tiles):
        lanes = pl.ds(tile * LANES, LANES)
        node_x, node_y, _ = tile_nodes(tile, 8, brick)
        node_x = node_x + (place[0] * brick - 1)
        node_y = node_y + (place[1] * brick - 1)
        drags = []
        for side in range(2):
            c = [total_ref[tile, pl.ds(32 * side + k, 8, stride=8), :] for k in range(CHANNELS)]
            node_z = row + (4 * side - 1) + place[2] * size_z
            inside = (node_z >= 0) & (node_z < counts[2] * size_z)
            if tile < SLABS:
                inside = inside & (node_x >= 0) & (node_x < counts[0] * brick)
                inside = inside & (node_y >= 0) & (node_y < counts[1] * brick)
            inverse = 1.0 / jnp.maximum(c[0], 1.0)
            scale = jnp.where(inside, (1.0 - c[7]) * inverse, 0.0)
            high, low = split(jnp.concatenate([c[4 + a] * scale for a in range(3)] + [blank], axis=0))
            push_ref[pl.ds(64 * side, 32), lanes] = high
            push_ref[pl.ds(64 * side + 32, 32), lanes] = low
            drags.append(
                c[4] * (c[1] * inverse) + c[5] * (c[2] * inverse) + c[6] * (c[3] * inverse - gravity_step)
            )
        edges.append(jnp.where(row < 7, pltpu.roll(drags[0], 7, 0), pltpu.roll(drags[1], 3, 0)))

    depth = iota((size_z, brick), 0) + place[2] * size_z
    lane = iota((size_z, LANES), 1)
    for x in range(brick):
        if x == 0:
            plane = pltpu.roll(edges[2], 96, 1)
        elif x == brick - 1:
            plane = edges[3]
        else:
            plane = edges[SLABS + x // 4]
            if x % 4:
                plane = pltpu.roll(plane, LANES - 32 * (x % 4), 1)
        at = 2 * (x + 1)
        plane = jnp.where(lane == 0, edges[0][:, at + 1 : at + 2], plane)
        plane = jnp.where(lane == brick - 1, edges[1][:, at : at + 1], plane)
        gdrag_ref[x] = jnp.where(depth < top_ref[pl.ds(x, 1), :], -plane[:, :brick], 0.0)

    gathered = lax.dot_general(hot_ref[...], push_ref[...], (((1,), (1,)), ((), ())), preferred_element_type=F32)
    lane = iota((blocks, LANES), 1)
    low_half = lane < 64
    upper = upper_tile == 1
    lows, highs = [], []
    for node in range(16):
        value = gathered[node * blocks : (node + 1) * blocks]
        rolled = pltpu.roll(value, 64, 1)
        lows.append(jnp.where(upper, rolled, value))
        highs.append(jnp.where(upper, value, rolled))
    for ox in range(3):
        for oy in range(3):
            for cx in range(2):
                value = jnp.where(low_half, lows[4 * (cx + ox) + oy], highs[4 * (cx + ox) + oy + 1])
                take_ref[pl.ds((3 * ox + oy) * blocks, blocks), pl.ds(cx * LANES, LANES)] = value.astype(BF16)

    key = iota((2 * LANES, LANES), 0)
    particle = iota((2 * LANES, LANES), 1)
    shift = jnp.where((key >> 6) == (particle >> 5), (key & 31) - ((particle >> 3) & 3), -64)
    for a in range(3):
        for oz in range(3):
            hit = shift == 8 * a + oz
            spread_ref[:, pl.ds((3 * a + oz) * LANES, LANES)] = jnp.where(hit, 1.0, 0.0).astype(BF16)
    pulled_ref[...] = jnp.dot(take_ref[...], spread_ref[...], preferred_element_type=F32)

    live = (iota((blocks, LANES), 0) < count_ref[0]).astype(F32)
    planar = [[live * weight[0][ox] * weight[1][oy] for oy in range(3)] for ox in range(3)]
    trace = None
    for a in range(3):
        sums_x, sums_y, sums_z = [], [None] * 3, None
        for ox in range(3):
            column = None
            for oy in range(3):
                rows = pl.ds((3 * ox + oy) * blocks, blocks)
                g = [pulled_ref[rows, pl.ds((3 * a + oz) * LANES, LANES)] for oz in range(3)]
                below, above = weight[2][0] * g[0], weight[2][2] * g[2]
                sum_z = planar[ox][oy] * (weight[2][1] * g[1] + (below + above))
                slope = planar[ox][oy] * (above - below)
                column = sum_z if column is None else column + sum_z
                sums_y[oy] = sum_z if sums_y[oy] is None else sums_y[oy] + sum_z
                sums_z = slope if sums_z is None else sums_z + slope
            sums_x.append(column)
        whole = sums_x[0] + sums_x[1] + sums_x[2]
        moments = [sums_x[2] - sums_x[0], sums_y[2] - sums_y[0], sums_z]
        flat_ref[pl.ds((3 + a) * blocks, blocks), :] = whole
        for b in range(3):
            value = moments[b] - frac[b] * whole
            flat_ref[pl.ds((6 + 3 * a + b) * blocks, blocks), :] = value
            if a == b:
                trace = value if trace is None else trace + value
    gvol_ref[...] = -stiffness * trace
    from_rows(gvel_ref, flat_ref, 3, blocks)
    from_rows(gaff_ref, flat_ref, 6, blocks)


def swap(array, axis, first):
    count = lax.axis_size(axis)
    pairs = [(i + k, i + 1 - k) for i in range(first, count - 1, 2) for k in range(2)]
    return lax.ppermute(array, axis, pairs) if pairs else jnp.zeros_like(array)


def shards(
    offsets, velocity, affine, volume, cot_velocity, cot_affine, block_cells, fill_counts, baffle_top, drag
):
    brick, _, size_z = drag.shape
    blocks = block_cells.shape[0]
    counts = tuple(lax.axis_size(axis) for axis in ("gx", "gy", "gz"))
    tiles = SLABS + brick // 4
    width = tiles * LANES
    smem = pl.BlockSpec(memory_space=pltpu.SMEM)
    vmem = pl.BlockSpec(memory_space=pltpu.VMEM)

    def f32(*shape):
        return jax.ShapeDtypeStruct(shape, F32)

    params = pltpu.CompilerParams(vmem_limit_bytes=40 * 1024 * 1024)
    slab = f32(ROWS, LANES)
    grid, send_xe, send_xo = pl.pallas_call(
        deposit_kernel,
        out_shape=(f32(tiles, ROWS, LANES), slab, slab),
        in_specs=[smem, smem] + [vmem] * 8,
        out_specs=(vmem,) * 3,
        scratch_shapes=[
            pltpu.VMEM((27 * blocks, LANES), F32),
            pltpu.VMEM((18 * blocks, 21 * LANES), BF16),
            pltpu.VMEM((21 * LANES, 2 * LANES), BF16),
            pltpu.VMEM((18 * blocks, 2 * LANES), F32),
            pltpu.VMEM((16 * blocks, 2 * LANES), BF16),
            pltpu.VMEM((16 * blocks, width), BF16),
            pltpu.VMEM((2 * LANES, width), F32),
        ],
        compiler_params=params,
        name="deposit",
    )(
        block_cells, fill_counts, offsets, velocity, affine, volume.reshape(blocks, LANES), cot_velocity, cot_affine,
        baffle_top, drag.transpose(0, 2, 1),
    )
    xo = swap(send_xo, "gx", 1)
    xe = swap(send_xe, "gx", 0)
    send_ye, send_yo = pl.pallas_call(
        pack_y_kernel,
        grid=(1,),
        out_shape=(slab, slab),
        in_specs=[pl.BlockSpec((2, ROWS, LANES), lambda i: (0, 0, 0))] + [pl.BlockSpec((ROWS, LANES), lambda i: (0, 0))] * 2,
        out_specs=(pl.BlockSpec((ROWS, LANES), lambda i: (0, 0)),) * 2,
        name="pack_y",
    )(grid, xe, xo)
    yo = swap(send_yo, "gy", 1)
    ye = swap(send_ye, "gy", 0)
    ends_z = 2 if counts[2] > 2 else 1
    send_z = pl.pallas_call(
        pack_z_kernel,
        out_shape=(f32(tiles, 16, LANES),) * ends_z,
        in_specs=[vmem] * 5,
        out_specs=(vmem,) * ends_z,
        name="pack_z",
    )(grid, xe, xo, ye, yo)
    received_z = [swap(array, "gz", first) for first, array in enumerate(send_z)]
    grad_velocity, grad_affine, grad_volume, grad_drag = pl.pallas_call(
        functools.partial(collect_kernel, counts),
        out_shape=(f32(3, blocks * LANES), f32(9, blocks * LANES), f32(blocks, LANES), f32(brick, size_z, brick)),
        in_specs=[smem, smem] + [vmem] * (7 + ends_z),
        out_specs=(vmem,) * 4,
        scratch_shapes=[
            pltpu.VMEM((tiles, ROWS + 16, LANES), F32),
            pltpu.VMEM((LANES, width), BF16),
            pltpu.VMEM((16 * blocks, width), BF16),
            pltpu.VMEM((9 * blocks, 2 * LANES), BF16),
            pltpu.VMEM((2 * LANES, 9 * LANES), BF16),
            pltpu.VMEM((9 * blocks, 9 * LANES), F32),
            pltpu.VMEM((15 * blocks, LANES), F32),
        ],
        compiler_params=params,
        name="collect",
    )(block_cells, fill_counts, offsets, baffle_top, grid, xe, xo, ye, yo, *received_z)
    return grad_velocity, grad_affine, grad_volume.reshape(-1), grad_drag.transpose(0, 2, 1)


def solution(mesh):
    everywhere = ("gx", "gy", "gz")
    rows, flat = P(None, everywhere), P(everywhere)
    in_specs = (rows, rows, rows, flat, rows, rows, flat, flat, P("gx", "gy"), P("gx", "gy", "gz"))
    out_specs = (rows, rows, flat, P("gx", "gy", "gz"))
    return jax.shard_map(shards, mesh=mesh, in_specs=in_specs, out_specs=out_specs, check_vma=False)
```

```python
import functools

import jax
import jax.numpy as jnp
from jax import lax
from jax.experimental import pallas as pl
from jax.experimental.pallas import tpu as pltpu
from jax.sharding import PartitionSpec as P

stiffness = 2.0
gravity_step = 0.3

LANES = 128
SLABS = 4
ZROWS = 10
CHANNELS = 8
ROWS = ZROWS * CHANNELS
F32 = jnp.float32
BF16 = jnp.bfloat16


def iota(shape, dim):
    return lax.broadcasted_iota(jnp.int32, shape, dim)


def tile_nodes(tile, rows, brick):
    lane = iota((rows, LANES), 1)
    if tile < 2:
        x, y = lane >> 1, (lane & 1) + tile * brick
        valid = lane < 2 * (brick + 2)
    else:
        x = (lane >> 5) + ((0, brick)[tile - 2] if tile < SLABS else 4 * (tile - SLABS) + 1)
        y = (lane & 31) + 1
        valid = (y >= 2) & (y < brick)
        valid = valid & ((lane < 64) if tile < SLABS else ((x >= 2) & (x < brick)))
    return x, y, valid


def tile_code(tile, rows, brick):
    x, y, valid = tile_nodes(tile, rows, brick)
    return jnp.where(valid, x * 64 + y, -1)


def block_columns(cells_ref, blocks):
    row = iota((blocks, LANES), 0)
    cells = jnp.zeros((blocks, LANES), jnp.int32)
    for b in range(blocks):
        cells = jnp.where(row == b, cells_ref[b], cells)
    code = (cells >> 5) * 128 + ((cells >> 1) & 15) * 2
    return code, cells & 1


def fill_one_hot(hot_ref, code, first_tile, brick):
    blocks = code.shape[0]
    for at in range(hot_ref.shape[1] // LANES):
        lane_code = tile_code(first_tile + at, blocks, brick) - code
        for node in range(16):
            hit = lane_code == (node // 4) * 64 + node % 4
            hot_ref[pl.ds(node * blocks, blocks), pl.ds(at * LANES, LANES)] = jnp.where(hit, 1.0, 0.0).astype(BF16)


def deposit_windows(grid_ref, window_ref, hot_ref, all_ref):
    all_ref[...] = lax.dot_general(
        window_ref[...], hot_ref[...], (((0,), (0,)), ((), ())), preferred_element_type=F32
    )
    for z in range(ZROWS):
        piece = None
        for tz in range(2):
            wz = z - 4 * tz
            if 0 <= wz < 6:
                row = 64 * tz + 8 * wz
                part = all_ref[pl.ds(row, 8), :] + all_ref[pl.ds(128 + row, 8), :]
                piece = part if piece is None else piece + part
        for tile in range(grid_ref.shape[0]):
            grid_ref[tile, pl.ds(8 * z, 8), :] = piece[:, tile * LANES : (tile + 1) * LANES]


def spline(frac):
    return [0.5 * (0.5 - frac) ** 2, 0.75 - frac * frac, 0.5 * (0.5 + frac) ** 2]


def split(value):
    high = value.astype(BF16)
    return high, (value - high.astype(F32)).astype(BF16)


def is_even(axis):
    return lax.rem(lax.axis_index(axis), 2) == 0


def low_high(even, odd, axis):
    here = is_even(axis)
    place = lax.axis_index(axis)
    low, high = jnp.where(here, odd, even), jnp.where(here, even, odd)
    return jnp.where(place > 0, low, 0.0), jnp.where(place < lax.axis_size(axis) - 1, high, 0.0)


def diagonal_rows(ends):
    even = ends[0]
    low, high = low_high(even, ends[1] if len(ends) > 1 else jnp.zeros_like(even), "gz")
    return jnp.concatenate([low, jnp.zeros((ROWS - 32, LANES), F32), high], axis=0)


def to_rows(flat_ref, first, array_ref, blocks):
    channels = array_ref.shape[0]
    for b in range(blocks):
        flat_ref[pl.ds(first * blocks + b, channels, stride=blocks), :] = array_ref[:, pl.ds(b * LANES, LANES)]


def from_rows(array_ref, flat_ref, first, blocks):
    channels = array_ref.shape[0]
    for b in range(blocks):
        array_ref[:, pl.ds(b * LANES, LANES)] = flat_ref[pl.ds(first * blocks + b, channels, stride=blocks), :]


def corners(low, high):
    lane = iota(low.shape, 1)
    first, last = lane < 4, (lane >= 64) & (lane < 68)
    zero = jnp.zeros_like(low)
    lower = jnp.where(first, pltpu.roll(low, 64, 1), jnp.where(last, high, zero))
    upper = jnp.where(first, pltpu.roll(low, 60, 1), jnp.where(last, pltpu.roll(high, 124, 1), zero))
    return lower, upper


def spread_kernel(spread_ref, take_ref):
    particle = iota((LANES, 2 * LANES), 0)
    shift = iota((LANES, 2 * LANES), 1) - ((particle >> 5) * 64 + ((particle >> 3) & 3) * 8)
    for c in range(7):
        for oz in range(3):
            hit = shift == oz * 8 + c
            spread_ref[pl.ds((3 * c + oz) * LANES, LANES), :] = jnp.where(hit, 1.0, 0.0).astype(BF16)
    key = iota((2 * LANES, LANES), 0)
    particle = iota((2 * LANES, LANES), 1)
    shift = jnp.where((key >> 6) == (particle >> 5), (key & 31) - ((particle >> 3) & 3), -64)
    for a in range(3):
        for oz in range(3):
            hit = shift == 8 * a + oz
            take_ref[:, pl.ds((3 * a + oz) * LANES, LANES)] = jnp.where(hit, 1.0, 0.0).astype(BF16)


def deposit_kernel(*refs):
    cells_ref, count_ref, pos_ref, vel_ref, aff_ref, vol_ref, cvel_ref, caff_ref, top_ref, drag_ref = refs[:10]
    spread_ref, refs = refs[10], refs[11:]
    grid_ref, even_ref, odd_ref, diagonal_ref, meta_ref, shape_ref, window_ref, hot_ref, planes_ref = refs[:9]
    flat_ref, terms_ref, sums_ref, all_ref = refs[9:]
    blocks = vol_ref.shape[0]
    brick = drag_ref.shape[0]
    size_z = drag_ref.shape[1]
    code, upper_tile = block_columns(cells_ref, blocks)
    live_rows = iota((blocks, LANES), 0) < count_ref[0]
    meta_ref[0], meta_ref[1], meta_ref[2] = code, upper_tile, live_rows.astype(jnp.int32)
    fill_one_hot(hot_ref, code, 0, brick)
    for first, ref in ((0, pos_ref), (3, vel_ref), (6, aff_ref), (15, cvel_ref), (18, caff_ref)):
        to_rows(flat_ref, first, ref, blocks)

    def channel(c):
        return flat_ref[pl.ds(c * blocks, blocks), :]

    live = live_rows.astype(F32)
    frac = [channel(k) for k in range(3)]
    weight = [spline(f) for f in frac]
    for k, value in enumerate(weight[0] + weight[1] + weight[2] + frac):
        shape_ref[pl.ds(k * blocks, blocks), :] = value
    stretch = stiffness * (vol_ref[...] - 1.0)
    linear, matrix = [live], [None]
    for a in range(3):
        row = [live * (channel(6 + 3 * a + b) - (stretch if a == b else 0.0)) for b in range(3)]
        matrix.append(row)
        linear.append(live * channel(3 + a) - sum(row[b] * frac[b] for b in range(3)))
    for a in range(3):
        row = [(4.0 * live) * channel(18 + 3 * a + b) for b in range(3)]
        matrix.append(row)
        linear.append(live * channel(15 + a) - sum(row[b] * frac[b] for b in range(3)))

    def put(row, slot, value):
        high, low = split(value)
        lanes = pl.ds(slot * LANES, LANES)
        terms_ref[pl.ds(row * blocks, blocks), lanes] = high
        terms_ref[pl.ds((9 + row) * blocks, blocks), lanes] = low

    for ox in range(3):
        for oy in range(3):
            planar = weight[0][ox] * weight[1][oy]
            weights = [planar * weight[2][oz] for oz in range(3)]
            for c in range(7):
                base = linear[c]
                if c:
                    if ox != 1:
                        base = base + matrix[c][0] if ox else base - matrix[c][0]
                    if oy != 1:
                        base = base + matrix[c][1] if oy else base - matrix[c][1]
                for oz in range(3):
                    value = base
                    if c and oz != 1:
                        value = base + matrix[c][2] if oz else base - matrix[c][2]
                    put(3 * ox + oy, 3 * c + oz, weights[oz] * value)

    sums_ref[...] = jnp.dot(terms_ref[...], spread_ref[...], preferred_element_type=F32)

    lane = iota((blocks, LANES), 1)
    low_half = lane < 64
    own_half = low_half == (upper_tile == 0)

    def partial(wx, oy):
        total = None
        for cx in range(2):
            ox = wx - cx
            if 0 <= ox < 3:
                lanes = pl.ds(cx * LANES, LANES)
                row = 3 * ox + oy
                piece = sums_ref[pl.ds(row * blocks, blocks), lanes] + sums_ref[pl.ds((9 + row) * blocks, blocks), lanes]
                total = piece if total is None else total + piece
        return total

    for wx in range(4):
        columns = [partial(wx, oy) for oy in range(3)]
        zero = jnp.zeros_like(columns[0])
        for wy in range(4):
            both = jnp.where(low_half, columns[wy] if wy < 3 else zero, columns[wy - 1] if wy else zero)
            node = jnp.where(own_half, both + pltpu.roll(both, 64, 1), 0.0)
            high, low = split(node)
            rows = pl.ds((4 * wx + wy) * blocks, blocks)
            window_ref[rows, pl.ds(0, LANES)] = high
            window_ref[rows, pl.ds(LANES, LANES)] = low

    deposit_windows(grid_ref, window_ref, hot_ref, all_ref)

    depth = iota((size_z, brick), 0) + lax.axis_index("gz") * size_z
    lane = iota((size_z, LANES), 1)
    zero = jnp.zeros((size_z, LANES), F32)
    ends = [zero, zero]
    layers = []
    for x in range(brick):
        layer = jnp.where(depth < top_ref[pl.ds(x, 1), :], drag_ref[x], 0.0)
        layers.append(layer)
        ends[0] = jnp.where(lane == 2 * (x + 1) + 1, layer[:, 0:1], ends[0])
        ends[1] = jnp.where(lane == 2 * (x + 1), layer[:, brick - 1 : brick], ends[1])
    blank = jnp.zeros((size_z, 32), F32)
    planes = ends + [
        jnp.concatenate([blank, layers[0], blank, blank], axis=1),
        jnp.concatenate([layers[-1], blank, blank, blank], axis=1),
    ]
    for t in range(brick // 4):
        planes_ref[t] = jnp.concatenate(layers[4 * t : 4 * t + 4], axis=1)
    for tile, plane in enumerate(planes):
        grid_ref[tile, pl.ds(8 + 7, size_z, stride=8), :] = plane

    lane = iota((ROWS, LANES), 1)
    slab = [grid_ref[t] for t in range(SLABS)]
    low = jnp.where(lane < 64, slab[2], jnp.where(lane < 68, pltpu.roll(slab[0], 64, 1), pltpu.roll(slab[1], 68, 1)))
    high = jnp.where(lane < 64, slab[3], jnp.where(lane < 68, slab[0], pltpu.roll(slab[1], 4, 1)))
    here = is_even("gx")
    even_ref[...] = jnp.where(here, high, low)
    odd_ref[...] = jnp.where(here, low, high)
    here = is_even("gz")
    lower, upper = odd_ref[pl.ds(0, 16), :], odd_ref[pl.ds(ROWS - 16, 16), :]
    diagonal_ref[0] = jnp.where(here, upper, lower)
    if diagonal_ref.shape[0] > 1:
        diagonal_ref[1] = jnp.where(here, lower, upper)


def interior_kernel(brick, window_ref, meta_ref, planes_ref, grid_ref, hot_ref, all_ref):
    fill_one_hot(hot_ref, meta_ref[0], SLABS, brick)
    deposit_windows(grid_ref, window_ref, hot_ref, all_ref)
    for tile in range(grid_ref.shape[0]):
        grid_ref[tile, pl.ds(8 + 7, planes_ref.shape[1], stride=8), :] = planes_ref[tile]


def pack_z_kernel(slab_ref, grid_ref, xe_ref, even_ref, *odd_refs):
    here = is_even("gz")
    ends = []
    for first in (0, ROWS - 16):
        rows = pl.ds(first, 16)
        received = xe_ref[rows, :]
        extra = x_additions(*low_high(received, jnp.zeros_like(received), "gx"))
        ends.append([slab_ref[t, rows, :] + extra[t] for t in range(SLABS)])
        ends[-1] += [grid_ref[t, rows, :] for t in range(grid_ref.shape[0])]
    for tile, (lower, upper) in enumerate(zip(*ends)):
        even_ref[tile] = jnp.where(here, upper, lower)
        for odd_ref in odd_refs:
            odd_ref[tile] = jnp.where(here, lower, upper)


def x_additions(low, high):
    lower, upper = corners(low, high)
    planar = iota(low.shape, 1) < 64
    return [lower, upper, jnp.where(planar, low, 0.0), jnp.where(planar, high, 0.0)]


def xz_additions(xe_ref, xo_ref, diagonals, layers, tiles):
    odd = xo_ref[...] + diagonal_rows([ref[...] for ref in diagonals])
    extra = x_additions(*low_high(xe_ref[...], odd, "gx"))
    return [extra[t] + diagonal_rows([ref[t] for ref in layers]) for t in range(tiles)]


def pack_y_kernel(ends, *refs):
    slab_ref, xe_ref, xo_ref, *received = refs[:-2]
    even_ref, odd_ref = refs[-2:]
    extra = xz_additions(xe_ref, xo_ref, received[:ends], received[ends:], 2)
    lower, upper = slab_ref[0] + extra[0], slab_ref[1] + extra[1]
    here = is_even("gy")
    even_ref[...] = jnp.where(here, upper, lower)
    odd_ref[...] = jnp.where(here, lower, upper)


def collect_kernel(counts, ends, *refs):
    inputs, refs = refs[:-10], refs[-10:]
    meta_ref, shape_ref, hot_slab_ref, hot_ref, spread_ref, top_ref, slab_ref, grid_ref = inputs[:8]
    xe_ref, xo_ref, ye_ref, yo_ref, *received = inputs[8:]
    gvel_ref, gaff_ref, gvol_ref, gdrag_ref = refs[:4]
    total_ref, push_slab_ref, push_ref, take_ref, pulled_ref, flat_ref = refs[4:]
    blocks = gvol_ref.shape[0]
    brick, size_z = gdrag_ref.shape[0], gdrag_ref.shape[1]
    tiles = SLABS + grid_ref.shape[0]
    saved = [shape_ref[pl.ds(k * blocks, blocks), :] for k in range(12)]
    weight, frac = [saved[3 * k : 3 * k + 3] for k in range(3)], saved[9:]

    extra = xz_additions(xe_ref, xo_ref, received[:ends], received[ends:], SLABS)
    low, high = low_high(ye_ref[...], yo_ref[...], "gy")
    extra[0], extra[1] = extra[0] + low, extra[1] + high
    for tile in range(tiles):
        if tile < SLABS:
            total_ref[tile, pl.ds(0, ROWS), :] = slab_ref[tile] + extra[tile]
        else:
            more = diagonal_rows([ref[tile] for ref in received[ends:]])
            total_ref[tile, pl.ds(0, ROWS), :] = grid_ref[tile - SLABS] + more
        total_ref[tile, pl.ds(ROWS, 16), :] = jnp.zeros((16, LANES), F32)

    place = [lax.axis_index(axis) for axis in ("gx", "gy", "gz")]
    edges = []
    row = iota((8, LANES), 0)
    blank = jnp.zeros((8, LANES), F32)
    for tile in range(tiles):
        at = tile if tile < SLABS else tile - SLABS
        lanes = pl.ds(at * LANES, LANES)
        target_ref = push_slab_ref if tile < SLABS else push_ref
        node_x, node_y, _ = tile_nodes(tile, 8, brick)
        node_x = node_x + (place[0] * brick - 1)
        node_y = node_y + (place[1] * brick - 1)
        drags = []
        for side in range(2):
            c = [total_ref[tile, pl.ds(32 * side + k, 8, stride=8), :] for k in range(CHANNELS)]
            node_z = row + (4 * side - 1) + place[2] * size_z
            inside = (node_z >= 0) & (node_z < counts[2] * size_z)
            if tile < SLABS:
                inside = inside & (node_x >= 0) & (node_x < counts[0] * brick)
                inside = inside & (node_y >= 0) & (node_y < counts[1] * brick)
            inverse = 1.0 / jnp.maximum(c[0], 1.0)
            scale = jnp.where(inside, (1.0 - c[7]) * inverse, 0.0)
            high, low = split(jnp.concatenate([c[4 + a] * scale for a in range(3)] + [blank], axis=0))
            target_ref[pl.ds(64 * side, 32), lanes] = high
            target_ref[pl.ds(64 * side + 32, 32), lanes] = low
            drags.append(
                c[4] * (c[1] * inverse) + c[5] * (c[2] * inverse) + c[6] * (c[3] * inverse - gravity_step)
            )
        edges.append(jnp.where(row < 7, pltpu.roll(drags[0], 7, 0), pltpu.roll(drags[1], 3, 0)))

    depth = iota((size_z, brick), 0) + place[2] * size_z
    lane = iota((size_z, LANES), 1)
    for x in range(brick):
        if x == 0:
            plane = pltpu.roll(edges[2], 96, 1)
        elif x == brick - 1:
            plane = edges[3]
        else:
            plane = edges[SLABS + x // 4]
            if x % 4:
                plane = pltpu.roll(plane, LANES - 32 * (x % 4), 1)
        at = 2 * (x + 1)
        plane = jnp.where(lane == 0, edges[0][:, at + 1 : at + 2], plane)
        plane = jnp.where(lane == brick - 1, edges[1][:, at : at + 1], plane)
        gdrag_ref[x] = jnp.where(depth < top_ref[pl.ds(x, 1), :], -plane[:, :brick], 0.0)

    gathered = sum(
        lax.dot_general(hot[...], push[...], (((1,), (1,)), ((), ())), preferred_element_type=F32)
        for hot, push in ((hot_slab_ref, push_slab_ref), (hot_ref, push_ref))
    )
    lane = iota((blocks, LANES), 1)
    low_half = lane < 64
    upper = meta_ref[1] == 1
    lows, highs = [], []
    for node in range(16):
        value = gathered[node * blocks : (node + 1) * blocks]
        rolled = pltpu.roll(value, 64, 1)
        lows.append(jnp.where(upper, rolled, value))
        highs.append(jnp.where(upper, value, rolled))
    for ox in range(3):
        for oy in range(3):
            for cx in range(2):
                value = jnp.where(low_half, lows[4 * (cx + ox) + oy], highs[4 * (cx + ox) + oy + 1])
                take_ref[pl.ds((3 * ox + oy) * blocks, blocks), pl.ds(cx * LANES, LANES)] = value.astype(BF16)

    pulled_ref[...] = jnp.dot(take_ref[...], spread_ref[...], preferred_element_type=F32)

    live = meta_ref[2].astype(F32)
    planar = [[live * weight[0][ox] * weight[1][oy] for oy in range(3)] for ox in range(3)]
    trace = None
    for a in range(3):
        sums_x, sums_y, sums_z = [], [None] * 3, None
        for ox in range(3):
            column = None
            for oy in range(3):
                rows = pl.ds((3 * ox + oy) * blocks, blocks)
                g = [pulled_ref[rows, pl.ds((3 * a + oz) * LANES, LANES)] for oz in range(3)]
                below, above = weight[2][0] * g[0], weight[2][2] * g[2]
                sum_z = planar[ox][oy] * (weight[2][1] * g[1] + (below + above))
                slope = planar[ox][oy] * (above - below)
                column = sum_z if column is None else column + sum_z
                sums_y[oy] = sum_z if sums_y[oy] is None else sums_y[oy] + sum_z
                sums_z = slope if sums_z is None else sums_z + slope
            sums_x.append(column)
        whole = sums_x[0] + sums_x[1] + sums_x[2]
        moments = [sums_x[2] - sums_x[0], sums_y[2] - sums_y[0], sums_z]
        flat_ref[pl.ds(a * blocks, blocks), :] = whole
        for b in range(3):
            value = moments[b] - frac[b] * whole
            flat_ref[pl.ds((3 + 3 * a + b) * blocks, blocks), :] = value
            if a == b:
                trace = value if trace is None else trace + value
    gvol_ref[...] = -stiffness * trace
    from_rows(gvel_ref, flat_ref, 0, blocks)
    from_rows(gaff_ref, flat_ref, 3, blocks)


def paired(index, count, first):
    partner = index + 1 if (index - first) % 2 == 0 else index - 1
    return partner if 0 <= partner < count else None


def exchange(array, counts, pair):
    names = ("gx", "gy", "gz")
    links = []
    for x in range(counts[0]):
        for y in range(counts[1]):
            for z in range(counts[2]):
                target = pair(x, y, z)
                if None not in target:
                    links.append(((x * counts[1] + y) * counts[2] + z, (target[0] * counts[1] + target[1]) * counts[2] + target[2]))
    return lax.ppermute(array, names, links) if links else jnp.zeros_like(array)


def shards(
    offsets, velocity, affine, volume, cot_velocity, cot_affine, block_cells, fill_counts, baffle_top, drag
):
    brick, _, size_z = drag.shape
    blocks = block_cells.shape[0]
    counts = tuple(lax.axis_size(axis) for axis in ("gx", "gy", "gz"))
    interior = brick // 4
    smem = pl.BlockSpec(memory_space=pltpu.SMEM)
    vmem = pl.BlockSpec(memory_space=pltpu.VMEM)

    def f32(*shape):
        return jax.ShapeDtypeStruct(shape, F32)

    def bf16(*shape):
        return jax.ShapeDtypeStruct(shape, BF16)

    def call(kernel, name, out_shape, operands, in_specs=None, scratch=(), megabytes=4, flops=0):
        return pl.pallas_call(
            kernel,
            out_shape=out_shape,
            in_specs=in_specs or [vmem] * len(operands),
            out_specs=(vmem,) * len(out_shape),
            scratch_shapes=scratch,
            compiler_params=pltpu.CompilerParams(vmem_limit_bytes=megabytes * 1024 * 1024),
            cost_estimate=pl.CostEstimate(flops=flops, bytes_accessed=1024, transcendentals=0),
            name=name,
        )(*operands)

    operands = (
        block_cells, fill_counts, offsets, velocity, affine, volume.reshape(blocks, LANES), cot_velocity, cot_affine,
        baffle_top, drag.transpose(0, 2, 1),
    )
    slab = f32(ROWS, LANES)
    ends = 2 if counts[2] > 2 else 1
    spread, take = call(
        spread_kernel, "spread", (bf16(21 * LANES, 2 * LANES), bf16(2 * LANES, 9 * LANES)), (), flops=20_000_000_000
    )
    edge, send_xe, send_xo, send_xz, meta, shape, window, hot_edge, planes = call(
        deposit_kernel,
        "deposit",
        (
            f32(SLABS, ROWS, LANES), slab, slab, f32(ends, 16, LANES),
            jax.ShapeDtypeStruct((3, blocks, LANES), jnp.int32), f32(12 * blocks, LANES),
            bf16(16 * blocks, 2 * LANES), bf16(16 * blocks, SLABS * LANES), f32(interior, size_z, LANES),
        ),
        operands + (spread,),
        in_specs=[smem, smem] + [vmem] * 9,
        scratch=[
            pltpu.VMEM((27 * blocks, LANES), F32),
            pltpu.VMEM((18 * blocks, 21 * LANES), BF16),
            pltpu.VMEM((18 * blocks, 2 * LANES), F32),
            pltpu.VMEM((2 * LANES, SLABS * LANES), F32),
        ],
        megabytes=16,
    )

    def even_x(x):
        return paired(x, counts[0], 0)

    def odd_x(x):
        partner = paired(x, counts[0], 1)
        return counts[0] - 1 - x if partner is None and counts[0] % 2 == 0 else partner

    def odd_y(x, y, z):
        partner = paired(y, counts[1], 1)
        return (even_x(x), y, z) if partner is None else (x, partner, z)

    xe = exchange(send_xe, counts, lambda x, y, z: (even_x(x), y, z))
    xo = exchange(send_xo, counts, lambda x, y, z: (odd_x(x), y, z))
    xz = [
        exchange(send_xz[first], counts, lambda x, y, z: (odd_x(x), y, paired(z, counts[2], first)))
        for first in range(ends)
    ]
    grid, hot = call(
        functools.partial(interior_kernel, brick),
        "interior",
        (f32(interior, ROWS, LANES), bf16(16 * blocks, interior * LANES)),
        (window, meta, planes),
        scratch=[pltpu.VMEM((2 * LANES, interior * LANES), F32)],
        megabytes=8,
        flops=1_000_000_000,
    )
    send_z = call(pack_z_kernel, "pack_z", (f32(SLABS + interior, 16, LANES),) * ends, (edge, grid, xe))
    layers = [
        exchange(array, counts, lambda x, y, z: (x, y, paired(z, counts[2], first)))
        for first, array in enumerate(send_z)
    ]
    send_ye, send_yo = call(
        functools.partial(pack_y_kernel, ends), "pack_y", (slab, slab), (edge, xe, xo, *xz, *layers)
    )
    yo = exchange(send_yo, counts, odd_y)
    ye = exchange(send_ye, counts, lambda x, y, z: (x, paired(y, counts[1], 0), z))
    grad_velocity, grad_affine, grad_volume, grad_drag = call(
        functools.partial(collect_kernel, counts, ends),
        "collect",
        (f32(3, blocks * LANES), f32(9, blocks * LANES), f32(blocks, LANES), f32(brick, size_z, brick)),
        (meta, shape, hot_edge, hot, take, baffle_top, edge, grid, xe, xo, ye, yo, *xz, *layers),
        scratch=[
            pltpu.VMEM((SLABS + interior, ROWS + 16, LANES), F32),
            pltpu.VMEM((LANES, SLABS * LANES), BF16),
            pltpu.VMEM((LANES, interior * LANES), BF16),
            pltpu.VMEM((9 * blocks, 2 * LANES), BF16),
            pltpu.VMEM((9 * blocks, 9 * LANES), F32),
            pltpu.VMEM((12 * blocks, LANES), F32),
        ],
        megabytes=16,
    )
    return grad_velocity, grad_affine, grad_volume.reshape(-1), grad_drag.transpose(0, 2, 1)


def solution(mesh):
    everywhere = ("gx", "gy", "gz")
    rows, flat = P(None, everywhere), P(everywhere)
    in_specs = (rows, rows, rows, flat, rows, rows, flat, flat, P("gx", "gy"), P("gx", "gy", "gz"))
    out_specs = (rows, rows, flat, P("gx", "gy", "gz"))
    return jax.shard_map(shards, mesh=mesh, in_specs=in_specs, out_specs=out_specs, check_vma=False)
```

```python
import functools

import jax
import jax.numpy as jnp
from jax import lax
from jax.experimental import pallas as pl
from jax.experimental.pallas import tpu as pltpu
from jax.sharding import PartitionSpec as P

stiffness = 2.0
gravity_step = 0.3

LANES = 128
SLABS = 4
ZROWS = 10
CHANNELS = 8
ROWS = ZROWS * CHANNELS
F32 = jnp.float32
BF16 = jnp.bfloat16


def iota(shape, dim):
    return lax.broadcasted_iota(jnp.int32, shape, dim)


def tile_nodes(tile, rows, brick):
    lane = iota((rows, LANES), 1)
    if tile < 2:
        x, y = lane >> 1, (lane & 1) + tile * brick
        valid = lane < 2 * (brick + 2)
    else:
        x = (lane >> 5) + ((0, brick)[tile - 2] if tile < SLABS else 4 * (tile - SLABS) + 1)
        y = (lane & 31) + 1
        valid = (y >= 2) & (y < brick)
        valid = valid & ((lane < 64) if tile < SLABS else ((x >= 2) & (x < brick)))
    return x, y, valid


def tile_code(tile, rows, brick):
    x, y, valid = tile_nodes(tile, rows, brick)
    return jnp.where(valid, x * 64 + y, -1)


def block_columns(cells_ref):
    blocks = cells_ref.shape[1]
    same = iota((blocks, blocks), 0) == iota((blocks, blocks), 1)
    column = jnp.sum(jnp.where(same, cells_ref[...].astype(F32), 0.0), axis=1, keepdims=True)
    cells = jnp.broadcast_to(column, (blocks, LANES)).astype(jnp.int32)
    return (cells >> 5) * 128 + ((cells >> 1) & 15) * 2, cells & 1


def fill_one_hot(hot_ref, code, first_tile, brick):
    blocks = code.shape[0]
    for at in range(hot_ref.shape[1] // LANES):
        lane_code = tile_code(first_tile + at, blocks, brick) - code
        for node in range(16):
            hit = lane_code == (node // 4) * 64 + node % 4
            hot_ref[pl.ds(node * blocks, blocks), pl.ds(at * LANES, LANES)] = jnp.where(hit, 1.0, 0.0).astype(BF16)


def deposit_windows(grid_ref, window_ref, hot_ref, all_ref):
    all_ref[...] = lax.dot_general(
        window_ref[...], hot_ref[...], (((0,), (0,)), ((), ())), preferred_element_type=F32
    )
    for z in range(ZROWS):
        piece = None
        for tz in range(2):
            wz = z - 4 * tz
            if 0 <= wz < 6:
                row = 64 * tz + 8 * wz
                part = all_ref[pl.ds(row, 8), :] + all_ref[pl.ds(128 + row, 8), :]
                piece = part if piece is None else piece + part
        for tile in range(grid_ref.shape[0]):
            grid_ref[tile, pl.ds(8 * z, 8), :] = piece[:, tile * LANES : (tile + 1) * LANES]


def spline(frac):
    return [0.5 * (0.5 - frac) ** 2, 0.75 - frac * frac, 0.5 * (0.5 + frac) ** 2]


def split(value):
    high = value.astype(BF16)
    return high, (value - high.astype(F32)).astype(BF16)


def is_even(axis):
    return lax.rem(lax.axis_index(axis), 2) == 0


def low_high(even, odd, axis):
    here = is_even(axis)
    place = lax.axis_index(axis)
    low, high = jnp.where(here, odd, even), jnp.where(here, even, odd)
    return jnp.where(place > 0, low, 0.0), jnp.where(place < lax.axis_size(axis) - 1, high, 0.0)


def diagonal_rows(ends):
    even = ends[0]
    low, high = low_high(even, ends[1] if len(ends) > 1 else jnp.zeros_like(even), "gz")
    return jnp.concatenate([low, jnp.zeros((ROWS - 32, LANES), F32), high], axis=0)


def to_rows(flat_ref, first, array_ref, blocks):
    channels = array_ref.shape[0]
    for b in range(blocks):
        flat_ref[pl.ds(first * blocks + b, channels, stride=blocks), :] = array_ref[:, pl.ds(b * LANES, LANES)]


def from_rows(array_ref, flat_ref, first, blocks):
    channels = array_ref.shape[0]
    for b in range(blocks):
        array_ref[:, pl.ds(b * LANES, LANES)] = flat_ref[pl.ds(first * blocks + b, channels, stride=blocks), :]


def corners(low, high):
    lane = iota(low.shape, 1)
    first, last = lane < 4, (lane >= 64) & (lane < 68)
    zero = jnp.zeros_like(low)
    lower = jnp.where(first, pltpu.roll(low, 64, 1), jnp.where(last, high, zero))
    upper = jnp.where(first, pltpu.roll(low, 60, 1), jnp.where(last, pltpu.roll(high, 124, 1), zero))
    return lower, upper


def spread_kernel(spread_ref, take_ref):
    particle = iota((LANES, 2 * LANES), 0)
    shift = iota((LANES, 2 * LANES), 1) - ((particle >> 5) * 64 + ((particle >> 3) & 3) * 8)
    for c in range(7):
        for oz in range(3):
            hit = shift == oz * 8 + c
            spread_ref[pl.ds((3 * c + oz) * LANES, LANES), :] = jnp.where(hit, 1.0, 0.0).astype(BF16)
    key = iota((2 * LANES, LANES), 0)
    particle = iota((2 * LANES, LANES), 1)
    shift = jnp.where((key >> 6) == (particle >> 5), (key & 31) - ((particle >> 3) & 3), -64)
    for a in range(3):
        for oz in range(3):
            hit = shift == 8 * a + oz
            take_ref[:, pl.ds((3 * a + oz) * LANES, LANES)] = jnp.where(hit, 1.0, 0.0).astype(BF16)


def deposit_kernel(*refs):
    cells_ref, count_ref, pos_ref, vel_ref, aff_ref, vol_ref, cvel_ref, caff_ref, top_ref, drag_ref = refs[:10]
    spread_ref, refs = refs[10], refs[11:]
    grid_ref, even_ref, odd_ref, diagonal_ref, meta_ref, shape_ref, window_ref, hot_ref, planes_ref = refs[:9]
    flat_ref, terms_ref, sums_ref, all_ref = refs[9:]
    blocks = vol_ref.shape[0]
    brick = drag_ref.shape[0]
    size_z = drag_ref.shape[1]
    code, upper_tile = block_columns(cells_ref)
    live_rows = iota((blocks, LANES), 0) < count_ref[...]
    meta_ref[0], meta_ref[1], meta_ref[2] = code, upper_tile, live_rows.astype(jnp.int32)
    fill_one_hot(hot_ref, code, 0, brick)
    for first, ref in ((0, pos_ref), (3, vel_ref), (6, aff_ref), (15, cvel_ref), (18, caff_ref)):
        to_rows(flat_ref, first, ref, blocks)

    def channel(c):
        return flat_ref[pl.ds(c * blocks, blocks), :]

    live = live_rows.astype(F32)
    frac = [channel(k) for k in range(3)]
    weight = [spline(f) for f in frac]
    for k, value in enumerate(weight[0] + weight[1] + weight[2] + frac):
        shape_ref[pl.ds(k * blocks, blocks), :] = value
    stretch = stiffness * (vol_ref[...] - 1.0)
    linear, matrix = [live], [None]
    for a in range(3):
        row = [live * (channel(6 + 3 * a + b) - (stretch if a == b else 0.0)) for b in range(3)]
        matrix.append(row)
        linear.append(live * channel(3 + a) - sum(row[b] * frac[b] for b in range(3)))
    for a in range(3):
        row = [(4.0 * live) * channel(18 + 3 * a + b) for b in range(3)]
        matrix.append(row)
        linear.append(live * channel(15 + a) - sum(row[b] * frac[b] for b in range(3)))

    def put(row, slot, value):
        high, low = split(value)
        lanes = pl.ds(slot * LANES, LANES)
        terms_ref[pl.ds(row * blocks, blocks), lanes] = high
        terms_ref[pl.ds((9 + row) * blocks, blocks), lanes] = low

    for ox in range(3):
        for oy in range(3):
            planar = weight[0][ox] * weight[1][oy]
            weights = [planar * weight[2][oz] for oz in range(3)]
            for c in range(7):
                base = linear[c]
                if c:
                    if ox != 1:
                        base = base + matrix[c][0] if ox else base - matrix[c][0]
                    if oy != 1:
                        base = base + matrix[c][1] if oy else base - matrix[c][1]
                for oz in range(3):
                    value = base
                    if c and oz != 1:
                        value = base + matrix[c][2] if oz else base - matrix[c][2]
                    put(3 * ox + oy, 3 * c + oz, weights[oz] * value)

    sums_ref[...] = jnp.dot(terms_ref[...], spread_ref[...], preferred_element_type=F32)

    lane = iota((blocks, LANES), 1)
    low_half = lane < 64
    own_half = low_half == (upper_tile == 0)

    def partial(wx, oy):
        total = None
        for cx in range(2):
            ox = wx - cx
            if 0 <= ox < 3:
                lanes = pl.ds(cx * LANES, LANES)
                row = 3 * ox + oy
                piece = sums_ref[pl.ds(row * blocks, blocks), lanes] + sums_ref[pl.ds((9 + row) * blocks, blocks), lanes]
                total = piece if total is None else total + piece
        return total

    for wx in range(4):
        columns = [partial(wx, oy) for oy in range(3)]
        zero = jnp.zeros_like(columns[0])
        for wy in range(4):
            both = jnp.where(low_half, columns[wy] if wy < 3 else zero, columns[wy - 1] if wy else zero)
            node = jnp.where(own_half, both + pltpu.roll(both, 64, 1), 0.0)
            high, low = split(node)
            rows = pl.ds((4 * wx + wy) * blocks, blocks)
            window_ref[rows, pl.ds(0, LANES)] = high
            window_ref[rows, pl.ds(LANES, LANES)] = low

    deposit_windows(grid_ref, window_ref, hot_ref, all_ref)

    depth = iota((size_z, brick), 0) + lax.axis_index("gz") * size_z
    lane = iota((size_z, LANES), 1)
    zero = jnp.zeros((size_z, LANES), F32)
    ends = [zero, zero]
    layers = []
    for x in range(brick):
        layer = jnp.where(depth < top_ref[pl.ds(x, 1), :], drag_ref[x], 0.0)
        layers.append(layer)
        ends[0] = jnp.where(lane == 2 * (x + 1) + 1, layer[:, 0:1], ends[0])
        ends[1] = jnp.where(lane == 2 * (x + 1), layer[:, brick - 1 : brick], ends[1])
    blank = jnp.zeros((size_z, 32), F32)
    planes = ends + [
        jnp.concatenate([blank, layers[0], blank, blank], axis=1),
        jnp.concatenate([layers[-1], blank, blank, blank], axis=1),
    ]
    for t in range(brick // 4):
        planes_ref[t] = jnp.concatenate(layers[4 * t : 4 * t + 4], axis=1)
    for tile, plane in enumerate(planes):
        grid_ref[tile, pl.ds(8 + 7, size_z, stride=8), :] = plane

    lane = iota((ROWS, LANES), 1)
    slab = [grid_ref[t] for t in range(SLABS)]
    low = jnp.where(lane < 64, slab[2], jnp.where(lane < 68, pltpu.roll(slab[0], 64, 1), pltpu.roll(slab[1], 68, 1)))
    high = jnp.where(lane < 64, slab[3], jnp.where(lane < 68, slab[0], pltpu.roll(slab[1], 4, 1)))
    here = is_even("gx")
    even_ref[...] = jnp.where(here, high, low)
    odd_ref[...] = jnp.where(here, low, high)
    here = is_even("gz")
    lower, upper = odd_ref[pl.ds(0, 16), :], odd_ref[pl.ds(ROWS - 16, 16), :]
    diagonal_ref[0] = jnp.where(here, upper, lower)
    if diagonal_ref.shape[0] > 1:
        diagonal_ref[1] = jnp.where(here, lower, upper)


def interior_kernel(brick, window_ref, meta_ref, planes_ref, grid_ref, hot_ref, all_ref):
    fill_one_hot(hot_ref, meta_ref[0], SLABS, brick)
    deposit_windows(grid_ref, window_ref, hot_ref, all_ref)
    for tile in range(grid_ref.shape[0]):
        grid_ref[tile, pl.ds(8 + 7, planes_ref.shape[1], stride=8), :] = planes_ref[tile]


def pack_z_kernel(slab_ref, grid_ref, xe_ref, even_ref, *odd_refs):
    here = is_even("gz")
    ends = []
    for first in (0, ROWS - 16):
        rows = pl.ds(first, 16)
        received = xe_ref[rows, :]
        extra = x_additions(*low_high(received, jnp.zeros_like(received), "gx"))
        ends.append([slab_ref[t, rows, :] + extra[t] for t in range(SLABS)])
        ends[-1] += [grid_ref[t, rows, :] for t in range(grid_ref.shape[0])]
    for tile, (lower, upper) in enumerate(zip(*ends)):
        even_ref[tile] = jnp.where(here, upper, lower)
        for odd_ref in odd_refs:
            odd_ref[tile] = jnp.where(here, lower, upper)


def x_additions(low, high):
    lower, upper = corners(low, high)
    planar = iota(low.shape, 1) < 64
    return [lower, upper, jnp.where(planar, low, 0.0), jnp.where(planar, high, 0.0)]


def xz_additions(xe_ref, xo_ref, diagonals, layers, tiles):
    odd = xo_ref[...] + diagonal_rows([ref[...] for ref in diagonals])
    extra = x_additions(*low_high(xe_ref[...], odd, "gx"))
    return [extra[t] + diagonal_rows([ref[t] for ref in layers]) for t in range(tiles)]


def pack_y_kernel(ends, *refs):
    slab_ref, xe_ref, xo_ref, *received = refs[:-2]
    even_ref, odd_ref = refs[-2:]
    extra = xz_additions(xe_ref, xo_ref, received[:ends], received[ends:], 2)
    lower, upper = slab_ref[0] + extra[0], slab_ref[1] + extra[1]
    here = is_even("gy")
    even_ref[...] = jnp.where(here, upper, lower)
    odd_ref[...] = jnp.where(here, lower, upper)


def node_gradients(counts, brick, size_z, tiles, totals, total_ref, push_ref, drag_ref):
    place = [lax.axis_index(axis) for axis in ("gx", "gy", "gz")]
    row = iota((8, LANES), 0)
    blank = jnp.zeros((8, LANES), F32)
    for at, (tile, total) in enumerate(zip(tiles, totals)):
        total_ref[at, pl.ds(0, ROWS), :] = total
        total_ref[at, pl.ds(ROWS, 16), :] = jnp.zeros((16, LANES), F32)
        lanes = pl.ds(at * LANES, LANES)
        node_x, node_y, _ = tile_nodes(tile, 8, brick)
        node_x = node_x + (place[0] * brick - 1)
        node_y = node_y + (place[1] * brick - 1)
        drags = []
        for side in range(2):
            c = [total_ref[at, pl.ds(32 * side + k, 8, stride=8), :] for k in range(CHANNELS)]
            node_z = row + (4 * side - 1) + place[2] * size_z
            inside = (node_z >= 0) & (node_z < counts[2] * size_z)
            if tile < SLABS:
                inside = inside & (node_x >= 0) & (node_x < counts[0] * brick)
                inside = inside & (node_y >= 0) & (node_y < counts[1] * brick)
            inverse = 1.0 / jnp.maximum(c[0], 1.0)
            scale = jnp.where(inside, (1.0 - c[7]) * inverse, 0.0)
            high, low = split(jnp.concatenate([c[4 + a] * scale for a in range(3)] + [blank], axis=0))
            push_ref[pl.ds(64 * side, 32), lanes] = high
            push_ref[pl.ds(64 * side + 32, 32), lanes] = low
            drags.append(
                c[4] * (c[1] * inverse) + c[5] * (c[2] * inverse) + c[6] * (c[3] * inverse - gravity_step)
            )
        drag_ref[at] = jnp.where(row < 7, pltpu.roll(drags[0], 7, 0), pltpu.roll(drags[1], 3, 0))


def gather(hot, push_ref):
    return lax.dot_general(hot, push_ref[...], (((1,), (1,)), ((), ())), preferred_element_type=F32)


def early_kernel(counts, ends, size_z, *refs):
    inputs, refs = refs[:-7], refs[-7:]
    hot_slab_ref, hot_ref, slab_ref, grid_ref, xe_ref, xo_ref, *received = inputs
    gathered_ref, drag_slab_ref, drag_ref, total_ref, push_slab_ref, push_ref, _ = refs
    brick = 4 * grid_ref.shape[0]
    extra = xz_additions(xe_ref, xo_ref, received[:ends], received[ends:], SLABS)
    totals = [slab_ref[tile] + extra[tile] for tile in (2, 3)]
    node_gradients(counts, brick, size_z, (2, 3), totals, total_ref, push_slab_ref, drag_slab_ref)
    tiles = range(SLABS, SLABS + grid_ref.shape[0])
    totals = [grid_ref[t - SLABS] + diagonal_rows([ref[t] for ref in received[ends:]]) for t in tiles]
    node_gradients(counts, brick, size_z, tiles, totals, total_ref, push_ref, drag_ref)
    gathered_ref[...] = gather(hot_slab_ref[:, pl.ds(2 * LANES, 2 * LANES)], push_slab_ref) + gather(hot_ref[...], push_ref)


def collect_kernel(counts, ends, *refs):
    inputs, refs = refs[:-10], refs[-10:]
    meta_ref, shape_ref, hot_slab_ref, take_spread_ref, top_ref, gathered_ref, drag_slab_ref, drag_ref = inputs[:8]
    slab_ref, xe_ref, xo_ref, ye_ref, yo_ref, *received = inputs[8:]
    gvel_ref, gaff_ref, gvol_ref, gdrag_ref = refs[:4]
    total_ref, push_ref, drag_ends_ref, take_ref, pulled_ref, flat_ref = refs[4:]
    blocks = gvol_ref.shape[0]
    brick, size_z = gdrag_ref.shape[0], gdrag_ref.shape[1]
    saved = [shape_ref[pl.ds(k * blocks, blocks), :] for k in range(12)]
    weight, frac = [saved[3 * k : 3 * k + 3] for k in range(3)], saved[9:]

    extra = xz_additions(xe_ref, xo_ref, received[:ends], received[ends:], 2)
    low, high = low_high(ye_ref[...], yo_ref[...], "gy")
    totals = [slab_ref[0] + extra[0] + low, slab_ref[1] + extra[1] + high]
    node_gradients(counts, brick, size_z, (0, 1), totals, total_ref, push_ref, drag_ends_ref)
    gathered = gathered_ref[...] + gather(hot_slab_ref[:, pl.ds(0, 2 * LANES)], push_ref)

    edges = [drag_ends_ref[t] for t in range(2)]
    depth = iota((size_z, brick), 0) + lax.axis_index("gz") * size_z
    lane = iota((size_z, LANES), 1)
    for x in range(brick):
        if x == 0:
            plane = pltpu.roll(drag_slab_ref[0], 96, 1)
        elif x == brick - 1:
            plane = drag_slab_ref[1]
        else:
            plane = drag_ref[x // 4]
            if x % 4:
                plane = pltpu.roll(plane, LANES - 32 * (x % 4), 1)
        at = 2 * (x + 1)
        plane = jnp.where(lane == 0, edges[0][:, at + 1 : at + 2], plane)
        plane = jnp.where(lane == brick - 1, edges[1][:, at : at + 1], plane)
        gdrag_ref[x] = jnp.where(depth < top_ref[pl.ds(x, 1), :], -plane[:, :brick], 0.0)

    lane = iota((blocks, LANES), 1)
    low_half = lane < 64
    upper = meta_ref[1] == 1
    lows, highs = [], []
    for node in range(16):
        value = gathered[node * blocks : (node + 1) * blocks]
        rolled = pltpu.roll(value, 64, 1)
        lows.append(jnp.where(upper, rolled, value))
        highs.append(jnp.where(upper, value, rolled))
    for ox in range(3):
        for oy in range(3):
            for cx in range(2):
                value = jnp.where(low_half, lows[4 * (cx + ox) + oy], highs[4 * (cx + ox) + oy + 1])
                take_ref[pl.ds((3 * ox + oy) * blocks, blocks), pl.ds(cx * LANES, LANES)] = value.astype(BF16)

    pulled_ref[...] = jnp.dot(take_ref[...], take_spread_ref[...], preferred_element_type=F32)

    live = meta_ref[2].astype(F32)
    planar = [[live * weight[0][ox] * weight[1][oy] for oy in range(3)] for ox in range(3)]
    trace = None
    for a in range(3):
        sums_x, sums_y, sums_z = [], [None] * 3, None
        for ox in range(3):
            column = None
            for oy in range(3):
                rows = pl.ds((3 * ox + oy) * blocks, blocks)
                g = [pulled_ref[rows, pl.ds((3 * a + oz) * LANES, LANES)] for oz in range(3)]
                below, above = weight[2][0] * g[0], weight[2][2] * g[2]
                sum_z = planar[ox][oy] * (weight[2][1] * g[1] + (below + above))
                slope = planar[ox][oy] * (above - below)
                column = sum_z if column is None else column + sum_z
                sums_y[oy] = sum_z if sums_y[oy] is None else sums_y[oy] + sum_z
                sums_z = slope if sums_z is None else sums_z + slope
            sums_x.append(column)
        whole = sums_x[0] + sums_x[1] + sums_x[2]
        moments = [sums_x[2] - sums_x[0], sums_y[2] - sums_y[0], sums_z]
        flat_ref[pl.ds(a * blocks, blocks), :] = whole
        for b in range(3):
            value = moments[b] - frac[b] * whole
            flat_ref[pl.ds((3 + 3 * a + b) * blocks, blocks), :] = value
            if a == b:
                trace = value if trace is None else trace + value
    gvol_ref[...] = -stiffness * trace
    from_rows(gvel_ref, flat_ref, 0, blocks)
    from_rows(gaff_ref, flat_ref, 3, blocks)


def paired(index, count, first):
    partner = index + 1 if (index - first) % 2 == 0 else index - 1
    return partner if 0 <= partner < count else None


def exchange(array, counts, pair):
    names = ("gx", "gy", "gz")
    links = []
    for x in range(counts[0]):
        for y in range(counts[1]):
            for z in range(counts[2]):
                target = pair(x, y, z)
                if None not in target:
                    links.append(((x * counts[1] + y) * counts[2] + z, (target[0] * counts[1] + target[1]) * counts[2] + target[2]))
    return lax.ppermute(array, names, links) if links else jnp.zeros_like(array)


def shards(
    offsets, velocity, affine, volume, cot_velocity, cot_affine, block_cells, fill_counts, baffle_top, drag
):
    brick, _, size_z = drag.shape
    blocks = block_cells.shape[0]
    counts = tuple(lax.axis_size(axis) for axis in ("gx", "gy", "gz"))
    interior = brick // 4
    vmem = pl.BlockSpec(memory_space=pltpu.VMEM)

    def f32(*shape):
        return jax.ShapeDtypeStruct(shape, F32)

    def bf16(*shape):
        return jax.ShapeDtypeStruct(shape, BF16)

    def call(kernel, name, out_shape, operands, scratch=(), megabytes=4, flops=0):
        return pl.pallas_call(
            kernel,
            out_shape=out_shape,
            in_specs=[vmem] * len(operands),
            out_specs=(vmem,) * len(out_shape),
            scratch_shapes=scratch,
            compiler_params=pltpu.CompilerParams(vmem_limit_bytes=megabytes * 1024 * 1024),
            cost_estimate=pl.CostEstimate(flops=flops, bytes_accessed=1024, transcendentals=0),
            name=name,
        )(*operands)

    operands = (
        block_cells.reshape(1, blocks), fill_counts.reshape(1, 1), offsets, velocity, affine, volume.reshape(blocks, LANES), cot_velocity, cot_affine,
        baffle_top, drag.transpose(0, 2, 1),
    )
    slab = f32(ROWS, LANES)
    ends = 2 if counts[2] > 2 else 1
    spread, take = call(
        spread_kernel, "spread", (bf16(21 * LANES, 2 * LANES), bf16(2 * LANES, 9 * LANES)), (), flops=20_000_000_000
    )
    edge, send_xe, send_xo, send_xz, meta, shape, window, hot_edge, planes = call(
        deposit_kernel,
        "deposit",
        (
            f32(SLABS, ROWS, LANES), slab, slab, f32(ends, 16, LANES),
            jax.ShapeDtypeStruct((3, blocks, LANES), jnp.int32), f32(12 * blocks, LANES),
            bf16(16 * blocks, 2 * LANES), bf16(16 * blocks, SLABS * LANES), f32(interior, size_z, LANES),
        ),
        operands + (spread,),
        scratch=[
            pltpu.VMEM((27 * blocks, LANES), F32),
            pltpu.VMEM((18 * blocks, 21 * LANES), BF16),
            pltpu.VMEM((18 * blocks, 2 * LANES), F32),
            pltpu.VMEM((2 * LANES, SLABS * LANES), F32),
        ],
        megabytes=16,
    )

    def even_x(x):
        return paired(x, counts[0], 0)

    def odd_x(x):
        partner = paired(x, counts[0], 1)
        return counts[0] - 1 - x if partner is None and counts[0] % 2 == 0 else partner

    def odd_y(x, y, z):
        partner = paired(y, counts[1], 1)
        return (even_x(x), y, z) if partner is None else (x, partner, z)

    xe = exchange(send_xe, counts, lambda x, y, z: (even_x(x), y, z))
    xo = exchange(send_xo, counts, lambda x, y, z: (odd_x(x), y, z))
    xz = [
        exchange(send_xz[first], counts, lambda x, y, z: (odd_x(x), y, paired(z, counts[2], first)))
        for first in range(ends)
    ]
    grid, hot = call(
        functools.partial(interior_kernel, brick),
        "interior",
        (f32(interior, ROWS, LANES), bf16(16 * blocks, interior * LANES)),
        (window, meta, planes),
        scratch=[pltpu.VMEM((2 * LANES, interior * LANES), F32)],
        megabytes=8,
        flops=1_000_000_000,
    )
    send_z = call(pack_z_kernel, "pack_z", (f32(SLABS + interior, 16, LANES),) * ends, (edge, grid, xe))
    layers = [
        exchange(array, counts, lambda x, y, z: (x, y, paired(z, counts[2], first)))
        for first, array in enumerate(send_z)
    ]
    send_ye, send_yo = call(
        functools.partial(pack_y_kernel, ends), "pack_y", (slab, slab), (edge, xe, xo, *xz, *layers)
    )
    yo = exchange(send_yo, counts, odd_y)
    ye = exchange(send_ye, counts, lambda x, y, z: (x, paired(y, counts[1], 0), z))
    gathered, drag_slab, drag_rows = call(
        functools.partial(early_kernel, counts, ends, size_z),
        "early",
        (f32(16 * blocks, LANES), f32(2, size_z, LANES), f32(interior, size_z, LANES)),
        (hot_edge, hot, edge, grid, xe, xo, *xz, *layers),
        scratch=[
            pltpu.VMEM((interior, ROWS + 16, LANES), F32),
            pltpu.VMEM((LANES, 2 * LANES), BF16),
            pltpu.VMEM((LANES, interior * LANES), BF16),
            pltpu.VMEM((8, LANES), F32),
        ],
        megabytes=8,
        flops=1_000_000_000,
    )
    grad_velocity, grad_affine, grad_volume, grad_drag = call(
        functools.partial(collect_kernel, counts, ends),
        "collect",
        (f32(3, blocks * LANES), f32(9, blocks * LANES), f32(blocks, LANES), f32(brick, size_z, brick)),
        (meta, shape, hot_edge, take, baffle_top, gathered, drag_slab, drag_rows, edge, xe, xo, ye, yo, *xz, *layers),
        scratch=[
            pltpu.VMEM((2, ROWS + 16, LANES), F32),
            pltpu.VMEM((LANES, 2 * LANES), BF16),
            pltpu.VMEM((2, size_z, LANES), F32),
            pltpu.VMEM((9 * blocks, 2 * LANES), BF16),
            pltpu.VMEM((9 * blocks, 9 * LANES), F32),
            pltpu.VMEM((12 * blocks, LANES), F32),
        ],
        megabytes=12,
    )
    return grad_velocity, grad_affine, grad_volume.reshape(-1), grad_drag.transpose(0, 2, 1)


def solution(mesh):
    everywhere = ("gx", "gy", "gz")
    rows, flat = P(None, everywhere), P(everywhere)
    in_specs = (rows, rows, rows, flat, rows, rows, flat, flat, P("gx", "gy"), P("gx", "gy", "gz"))
    out_specs = (rows, rows, flat, P("gx", "gy", "gz"))
    return jax.shard_map(shards, mesh=mesh, in_specs=in_specs, out_specs=out_specs, check_vma=False)
```

```python
import functools

import jax
import jax.numpy as jnp
from jax import lax
from jax.experimental import pallas as pl
from jax.experimental.pallas import tpu as pltpu
from jax.sharding import PartitionSpec as P

stiffness = 2.0
gravity_step = 0.3

LANES = 128
SLABS = 4
ZROWS = 10
CHANNELS = 8
ROWS = ZROWS * CHANNELS
F32 = jnp.float32
BF16 = jnp.bfloat16


def iota(shape, dim):
    return lax.broadcasted_iota(jnp.int32, shape, dim)


def tile_nodes(tile, rows, brick):
    lane = iota((rows, LANES), 1)
    if tile < 2:
        x, y = lane >> 1, (lane & 1) + tile * brick
        valid = lane < 2 * (brick + 2)
    elif tile < SLABS:
        plane, corner = lane < 64, lane - 64
        x = jnp.where(plane, lane >> 5, (corner & 3) >> 1) + (tile - 2) * brick
        y = jnp.where(plane, (lane & 31) + 1, (corner >> 2) * brick + (corner & 1))
        valid = jnp.where(plane, ((y >= 2) & (y < brick)).astype(jnp.int32), (corner < 8).astype(jnp.int32)) == 1
    else:
        x = (lane >> 5) + 4 * (tile - SLABS) + 1
        y = (lane & 31) + 1
        valid = (x >= 2) & (x < brick) & (y >= 2) & (y < brick)
    return x, y, valid


def tile_code(tile, rows, brick):
    x, y, valid = tile_nodes(tile, rows, brick)
    return jnp.where(valid, x * 64 + y, -1)


def block_columns(cells_ref):
    blocks = cells_ref.shape[1]
    same = iota((blocks, blocks), 0) == iota((blocks, blocks), 1)
    column = jnp.sum(jnp.where(same, cells_ref[...].astype(F32), 0.0), axis=1, keepdims=True)
    cells = jnp.broadcast_to(column, (blocks, LANES)).astype(jnp.int32)
    return (cells >> 5) * 128 + ((cells >> 1) & 15) * 2, cells & 1


def fill_one_hot(hot_ref, code, tiles, brick):
    blocks = code.shape[0]
    for at, tile in enumerate(tiles):
        lane_code = tile_code(tile, blocks, brick) - code
        for node in range(16):
            hit = lane_code == (node // 4) * 64 + node % 4
            hot_ref[pl.ds(node * blocks, blocks), pl.ds(at * LANES, LANES)] = jnp.where(hit, 1.0, 0.0).astype(BF16)


def deposit_windows(grid_ref, window_ref, hot_ref, all_ref):
    all_ref[...] = lax.dot_general(
        window_ref[...], hot_ref[...], (((0,), (0,)), ((), ())), preferred_element_type=F32
    )
    for z in range(ZROWS):
        piece = None
        for tz in range(2):
            wz = z - 4 * tz
            if 0 <= wz < 6:
                row = 64 * tz + 8 * wz
                part = all_ref[pl.ds(row, 8), :] + all_ref[pl.ds(128 + row, 8), :]
                piece = part if piece is None else piece + part
        for tile in range(grid_ref.shape[0]):
            grid_ref[tile, pl.ds(8 * z, 8), :] = piece[:, tile * LANES : (tile + 1) * LANES]


def inner_tiles(brick):
    return (0, 1) + tuple(range(SLABS, SLABS + brick // 4))


def spline(frac):
    return [0.5 * (0.5 - frac) ** 2, 0.75 - frac * frac, 0.5 * (0.5 + frac) ** 2]


def split(value):
    high = value.astype(BF16)
    return high, (value - high.astype(F32)).astype(BF16)


def is_even(axis):
    return lax.rem(lax.axis_index(axis), 2) == 0


def low_high(even, odd, axis):
    here = is_even(axis)
    place = lax.axis_index(axis)
    low, high = jnp.where(here, odd, even), jnp.where(here, even, odd)
    return jnp.where(place > 0, low, 0.0), jnp.where(place < lax.axis_size(axis) - 1, high, 0.0)


def diagonal_rows(ends):
    even = ends[0]
    low, high = low_high(even, ends[1] if len(ends) > 1 else jnp.zeros_like(even), "gz")
    return jnp.concatenate([low, jnp.zeros((ROWS - 32, LANES), F32), high], axis=0)


def to_rows(flat_ref, first, array_ref, blocks):
    channels = array_ref.shape[0]
    if channels > 8:
        tiles = jnp.stack([array_ref[pl.ds(0, 8), pl.ds(b * LANES, LANES)] for b in range(blocks)])
        flat_ref[pl.ds(first * blocks, 8 * blocks), :] = jnp.swapaxes(tiles, 0, 1).reshape(8 * blocks, LANES)
        for b in range(blocks):
            flat_ref[pl.ds((first + 8) * blocks + b, 1), :] = array_ref[pl.ds(8, 1), pl.ds(b * LANES, LANES)]
        return
    for b in range(blocks):
        flat_ref[pl.ds(first * blocks + b, channels, stride=blocks), :] = array_ref[:, pl.ds(b * LANES, LANES)]


def from_rows(array_ref, flat_ref, first, blocks):
    channels = array_ref.shape[0]
    for b in range(blocks):
        array_ref[:, pl.ds(b * LANES, LANES)] = flat_ref[pl.ds(first * blocks + b, channels, stride=blocks), :]


def corners(low, high):
    lane = iota(low.shape, 1)
    first, last = lane < 4, (lane >= 64) & (lane < 68)
    zero = jnp.zeros_like(low)
    lower = jnp.where(first, pltpu.roll(low, 64, 1), jnp.where(last, high, zero))
    upper = jnp.where(first, pltpu.roll(low, 60, 1), jnp.where(last, pltpu.roll(high, 124, 1), zero))
    return lower, upper


def spread_kernel(spread_ref, take_ref):
    particle = iota((LANES, 2 * LANES), 0)
    shift = iota((LANES, 2 * LANES), 1) - ((particle >> 5) * 64 + ((particle >> 3) & 3) * 8)
    for c in range(7):
        for oz in range(3):
            hit = shift == oz * 8 + c
            spread_ref[pl.ds((3 * c + oz) * LANES, LANES), :] = jnp.where(hit, 1.0, 0.0).astype(BF16)
    key = iota((2 * LANES, LANES), 0)
    particle = iota((2 * LANES, LANES), 1)
    shift = jnp.where((key >> 6) == (particle >> 5), (key & 31) - ((particle >> 3) & 3), -64)
    for a in range(3):
        for oz in range(3):
            hit = shift == 8 * a + oz
            take_ref[:, pl.ds((3 * a + oz) * LANES, LANES)] = jnp.where(hit, 1.0, 0.0).astype(BF16)


def deposit_kernel(*refs):
    cells_ref, count_ref, pos_ref, vel_ref, aff_ref, vol_ref, cvel_ref, caff_ref, top_ref, drag_ref = refs[:10]
    spread_ref, refs = refs[10], refs[11:]
    grid_ref, even_ref, odd_ref, diagonal_ref, meta_ref, shape_ref, window_ref, hot_ref = refs[:8]
    flat_ref, terms_ref, sums_ref, all_ref = refs[8:]
    blocks = vol_ref.shape[0]
    brick = drag_ref.shape[0]
    size_z = drag_ref.shape[1]
    code, upper_tile = block_columns(cells_ref)
    live_rows = iota((blocks, LANES), 0) < count_ref[...]
    meta_ref[0], meta_ref[1], meta_ref[2] = code, upper_tile, live_rows.astype(jnp.int32)
    fill_one_hot(hot_ref, code, (2, 3), brick)
    for first, ref in ((0, pos_ref), (3, vel_ref), (6, aff_ref), (15, cvel_ref), (18, caff_ref)):
        to_rows(flat_ref, first, ref, blocks)

    def channel(c):
        return flat_ref[pl.ds(c * blocks, blocks), :]

    live = live_rows.astype(F32)
    frac = [channel(k) for k in range(3)]
    weight = [spline(f) for f in frac]
    for k, value in enumerate(weight[0] + weight[1] + weight[2] + frac):
        shape_ref[pl.ds(k * blocks, blocks), :] = value
    stretch = stiffness * (vol_ref[...] - 1.0)
    linear, matrix = [live], [None]
    for a in range(3):
        row = [live * (channel(6 + 3 * a + b) - (stretch if a == b else 0.0)) for b in range(3)]
        matrix.append(row)
        linear.append(live * channel(3 + a) - sum(row[b] * frac[b] for b in range(3)))
    for a in range(3):
        row = [(4.0 * live) * channel(18 + 3 * a + b) for b in range(3)]
        matrix.append(row)
        linear.append(live * channel(15 + a) - sum(row[b] * frac[b] for b in range(3)))

    def put(row, slot, value):
        high, low = split(value)
        lanes = pl.ds(slot * LANES, LANES)
        terms_ref[pl.ds(row * blocks, blocks), lanes] = high
        terms_ref[pl.ds((9 + row) * blocks, blocks), lanes] = low

    for ox in range(3):
        for oy in range(3):
            planar = weight[0][ox] * weight[1][oy]
            weights = [planar * weight[2][oz] for oz in range(3)]
            for c in range(7):
                base = linear[c]
                if c:
                    if ox != 1:
                        base = base + matrix[c][0] if ox else base - matrix[c][0]
                    if oy != 1:
                        base = base + matrix[c][1] if oy else base - matrix[c][1]
                for oz in range(3):
                    value = base
                    if c and oz != 1:
                        value = base + matrix[c][2] if oz else base - matrix[c][2]
                    put(3 * ox + oy, 3 * c + oz, weights[oz] * value)

    sums_ref[...] = jnp.dot(terms_ref[...], spread_ref[...], preferred_element_type=F32)

    lane = iota((blocks, LANES), 1)
    low_half = lane < 64
    own_half = low_half == (upper_tile == 0)

    def partial(wx, oy):
        total = None
        for cx in range(2):
            ox = wx - cx
            if 0 <= ox < 3:
                lanes = pl.ds(cx * LANES, LANES)
                row = 3 * ox + oy
                piece = sums_ref[pl.ds(row * blocks, blocks), lanes] + sums_ref[pl.ds((9 + row) * blocks, blocks), lanes]
                total = piece if total is None else total + piece
        return total

    for wx in range(4):
        columns = [partial(wx, oy) for oy in range(3)]
        zero = jnp.zeros_like(columns[0])
        for wy in range(4):
            both = jnp.where(low_half, columns[wy] if wy < 3 else zero, columns[wy - 1] if wy else zero)
            node = jnp.where(own_half, both + pltpu.roll(both, 64, 1), 0.0)
            high, low = split(node)
            rows = pl.ds((4 * wx + wy) * blocks, blocks)
            window_ref[rows, pl.ds(0, LANES)] = high
            window_ref[rows, pl.ds(LANES, LANES)] = low

    deposit_windows(grid_ref, window_ref, hot_ref, all_ref)

    depth = iota((size_z, brick), 0) + lax.axis_index("gz") * size_z
    lane = iota((size_z, LANES), 1)
    blank = jnp.zeros((size_z, 32), F32)
    for side, x in enumerate((0, brick - 1)):
        layer = jnp.where(depth < top_ref[pl.ds(x, 1), :], drag_ref[x], 0.0)
        plane = jnp.concatenate([blank, layer, blank, blank] if side == 0 else [layer, blank, blank, blank], axis=1)
        plane = jnp.where(lane == 67 - 2 * side, layer[:, 0:1], plane)
        plane = jnp.where(lane == 70 - 2 * side, layer[:, brick - 1 : brick], plane)
        grid_ref[side, pl.ds(8 + 7, size_z, stride=8), :] = plane

    low, high = grid_ref[0], grid_ref[1]
    here = is_even("gx")
    even_ref[...] = jnp.where(here, high, low)
    odd_ref[...] = jnp.where(here, low, high)
    here = is_even("gz")
    lower, upper = odd_ref[pl.ds(0, 16), :], odd_ref[pl.ds(ROWS - 16, 16), :]
    diagonal_ref[0] = jnp.where(here, upper, lower)
    if diagonal_ref.shape[0] > 1:
        diagonal_ref[1] = jnp.where(here, lower, upper)


def interior_kernel(window_ref, meta_ref, top_ref, drag_ref, grid_ref, hot_ref, all_ref):
    brick, size_z, _ = drag_ref.shape
    fill_one_hot(hot_ref, meta_ref[0], inner_tiles(brick), brick)
    deposit_windows(grid_ref, window_ref, hot_ref, all_ref)
    depth = iota((size_z, brick), 0) + lax.axis_index("gz") * size_z
    lane = iota((size_z, LANES), 1)
    ends = [jnp.zeros((size_z, LANES), F32)] * 2
    layers = []
    for x in range(brick):
        layer = jnp.where(depth < top_ref[pl.ds(x, 1), :], drag_ref[x], 0.0)
        layers.append(layer)
        ends[0] = jnp.where(lane == 2 * (x + 1) + 1, layer[:, 0:1], ends[0])
        ends[1] = jnp.where(lane == 2 * (x + 1), layer[:, brick - 1 : brick], ends[1])
    planes = ends + [jnp.concatenate(layers[4 * t : 4 * t + 4], axis=1) for t in range(brick // 4)]
    for at, plane in enumerate(planes):
        grid_ref[at, pl.ds(8 + 7, size_z, stride=8), :] = plane


def own_tile(slab_ref, grid_ref, tile):
    return grid_ref[tile] if tile < 2 else slab_ref[tile - 2] if tile < SLABS else grid_ref[tile - 2]


def pack_z_kernel(slab_ref, grid_ref, xe_ref, even_ref, *odd_refs):
    here = is_even("gz")
    ends = []
    for first in (0, ROWS - 16):
        rows = pl.ds(first, 16)
        received = xe_ref[rows, :]
        extra = x_additions(*low_high(received, jnp.zeros_like(received), "gx"))
        ends.append([own_tile(slab_ref, grid_ref, t)[first : first + 16] + extra[t] for t in range(SLABS)])
        ends[-1] += [grid_ref[t, rows, :] for t in range(2, grid_ref.shape[0])]
    for tile, (lower, upper) in enumerate(zip(*ends)):
        even_ref[tile] = jnp.where(here, upper, lower)
        for odd_ref in odd_refs:
            odd_ref[tile] = jnp.where(here, lower, upper)


def x_additions(low, high):
    lower, upper = corners(low, high)
    planar = iota(low.shape, 1) < 64
    return [lower, upper, jnp.where(planar, low, 0.0), jnp.where(planar, high, 0.0)]


def xz_additions(xe_ref, xo_ref, diagonals, layers, tiles):
    odd = xo_ref[...] + diagonal_rows([ref[...] for ref in diagonals])
    extra = x_additions(*low_high(xe_ref[...], odd, "gx"))
    return [extra[t] + diagonal_rows([ref[t] for ref in layers]) for t in range(tiles)]


def pack_y_kernel(ends, *refs):
    grid_ref, xe_ref, xo_ref, *received = refs[:-2]
    even_ref, odd_ref = refs[-2:]
    extra = xz_additions(xe_ref, xo_ref, received[:ends], received[ends:], 2)
    lower, upper = grid_ref[0] + extra[0], grid_ref[1] + extra[1]
    here = is_even("gy")
    even_ref[...] = jnp.where(here, upper, lower)
    odd_ref[...] = jnp.where(here, lower, upper)


def node_gradients(counts, brick, size_z, tiles, totals, total_ref, push_ref, drag_ref):
    place = [lax.axis_index(axis) for axis in ("gx", "gy", "gz")]
    row = iota((8, LANES), 0)
    blank = jnp.zeros((8, LANES), F32)
    for at, (tile, total) in enumerate(zip(tiles, totals)):
        total_ref[at, pl.ds(0, ROWS), :] = total
        total_ref[at, pl.ds(ROWS, 16), :] = jnp.zeros((16, LANES), F32)
        lanes = pl.ds(at * LANES, LANES)
        node_x, node_y, _ = tile_nodes(tile, 8, brick)
        node_x = node_x + (place[0] * brick - 1)
        node_y = node_y + (place[1] * brick - 1)
        drags = []
        for side in range(2):
            c = [total_ref[at, pl.ds(32 * side + k, 8, stride=8), :] for k in range(CHANNELS)]
            node_z = row + (4 * side - 1) + place[2] * size_z
            inside = (node_z >= 0) & (node_z < counts[2] * size_z)
            if tile in (2, 3):
                inside = inside & (iota((8, LANES), 1) < 64)
            if tile < SLABS:
                inside = inside & (node_x >= 0) & (node_x < counts[0] * brick)
                inside = inside & (node_y >= 0) & (node_y < counts[1] * brick)
            inverse = 1.0 / jnp.maximum(c[0], 1.0)
            scale = jnp.where(inside, (1.0 - c[7]) * inverse, 0.0)
            high, low = split(jnp.concatenate([c[4 + a] * scale for a in range(3)] + [blank], axis=0))
            push_ref[pl.ds(64 * side, 32), lanes] = high
            push_ref[pl.ds(64 * side + 32, 32), lanes] = low
            drags.append(
                c[4] * (c[1] * inverse) + c[5] * (c[2] * inverse) + c[6] * (c[3] * inverse - gravity_step)
            )
        drag_ref[at] = jnp.where(row < 7, pltpu.roll(drags[0], 7, 0), pltpu.roll(drags[1], 3, 0))


def gather(hot, push_ref):
    return lax.dot_general(hot, push_ref[...], (((1,), (1,)), ((), ())), preferred_element_type=F32)


def early_kernel(counts, ends, size_z, *refs):
    inputs, refs = refs[:-7], refs[-7:]
    hot_slab_ref, hot_ref, slab_ref, grid_ref, xe_ref, xo_ref, *received = inputs
    gathered_ref, drag_slab_ref, drag_ref, total_ref, push_slab_ref, push_ref, _ = refs
    brick = 4 * (grid_ref.shape[0] - 2)
    extra = xz_additions(xe_ref, xo_ref, received[:ends], received[ends:], SLABS)
    totals = [slab_ref[tile - 2] + extra[tile] for tile in (2, 3)]
    node_gradients(counts, brick, size_z, (2, 3), totals, total_ref, push_slab_ref, drag_slab_ref)
    tiles = inner_tiles(brick)[2:]
    totals = [grid_ref[t - 2] + diagonal_rows([ref[t] for ref in received[ends:]]) for t in tiles]
    node_gradients(counts, brick, size_z, tiles, totals, total_ref, push_ref, drag_ref)
    gathered_ref[...] = gather(hot_slab_ref[...], push_slab_ref) + gather(
        hot_ref[:, pl.ds(2 * LANES, push_ref.shape[1])], push_ref
    )


def collect_kernel(counts, ends, *refs):
    inputs, refs = refs[:-10], refs[-10:]
    meta_ref, shape_ref, hot_ref, take_spread_ref, top_ref, gathered_ref, drag_slab_ref, drag_ref = inputs[:8]
    grid_ref, xe_ref, xo_ref, ye_ref, yo_ref, *received = inputs[8:]
    gvel_ref, gaff_ref, gvol_ref, gdrag_ref = refs[:4]
    total_ref, push_ref, drag_ends_ref, take_ref, pulled_ref, flat_ref = refs[4:]
    blocks = gvol_ref.shape[0]
    brick, size_z = gdrag_ref.shape[0], gdrag_ref.shape[1]
    saved = [shape_ref[pl.ds(k * blocks, blocks), :] for k in range(12)]
    weight, frac = [saved[3 * k : 3 * k + 3] for k in range(3)], saved[9:]

    extra = xz_additions(xe_ref, xo_ref, received[:ends], received[ends:], 2)
    low, high = low_high(ye_ref[...], yo_ref[...], "gy")
    totals = [grid_ref[0] + extra[0] + low, grid_ref[1] + extra[1] + high]
    node_gradients(counts, brick, size_z, (0, 1), totals, total_ref, push_ref, drag_ends_ref)
    gathered = gathered_ref[...] + gather(hot_ref[:, pl.ds(0, 2 * LANES)], push_ref)

    edges = [drag_ends_ref[t] for t in range(2)]
    depth = iota((size_z, brick), 0) + lax.axis_index("gz") * size_z
    lane = iota((size_z, LANES), 1)
    for x in range(brick):
        if x == 0:
            plane = pltpu.roll(drag_slab_ref[0], 96, 1)
        elif x == brick - 1:
            plane = drag_slab_ref[1]
        else:
            plane = drag_ref[x // 4]
            if x % 4:
                plane = pltpu.roll(plane, LANES - 32 * (x % 4), 1)
        at = 2 * (x + 1)
        plane = jnp.where(lane == 0, edges[0][:, at + 1 : at + 2], plane)
        plane = jnp.where(lane == brick - 1, edges[1][:, at : at + 1], plane)
        gdrag_ref[x] = jnp.where(depth < top_ref[pl.ds(x, 1), :], -plane[:, :brick], 0.0)

    lane = iota((blocks, LANES), 1)
    low_half = lane < 64
    upper = meta_ref[1] == 1
    lows, highs = [], []
    for node in range(16):
        value = gathered[node * blocks : (node + 1) * blocks]
        rolled = pltpu.roll(value, 64, 1)
        lows.append(jnp.where(upper, rolled, value))
        highs.append(jnp.where(upper, value, rolled))
    for ox in range(3):
        for oy in range(3):
            for cx in range(2):
                value = jnp.where(low_half, lows[4 * (cx + ox) + oy], highs[4 * (cx + ox) + oy + 1])
                take_ref[pl.ds((3 * ox + oy) * blocks, blocks), pl.ds(cx * LANES, LANES)] = value.astype(BF16)

    pulled_ref[...] = jnp.dot(take_ref[...], take_spread_ref[...], preferred_element_type=F32)

    live = meta_ref[2].astype(F32)
    planar = [[live * weight[0][ox] * weight[1][oy] for oy in range(3)] for ox in range(3)]
    trace = None
    for a in range(3):
        sums_x, sums_y, sums_z = [], [None] * 3, None
        for ox in range(3):
            column = None
            for oy in range(3):
                rows = pl.ds((3 * ox + oy) * blocks, blocks)
                g = [pulled_ref[rows, pl.ds((3 * a + oz) * LANES, LANES)] for oz in range(3)]
                below, above = weight[2][0] * g[0], weight[2][2] * g[2]
                sum_z = planar[ox][oy] * (weight[2][1] * g[1] + (below + above))
                slope = planar[ox][oy] * (above - below)
                column = sum_z if column is None else column + sum_z
                sums_y[oy] = sum_z if sums_y[oy] is None else sums_y[oy] + sum_z
                sums_z = slope if sums_z is None else sums_z + slope
            sums_x.append(column)
        whole = sums_x[0] + sums_x[1] + sums_x[2]
        moments = [sums_x[2] - sums_x[0], sums_y[2] - sums_y[0], sums_z]
        flat_ref[pl.ds(a * blocks, blocks), :] = whole
        for b in range(3):
            value = moments[b] - frac[b] * whole
            flat_ref[pl.ds((3 + 3 * a + b) * blocks, blocks), :] = value
            if a == b:
                trace = value if trace is None else trace + value
    gvol_ref[...] = -stiffness * trace
    from_rows(gvel_ref, flat_ref, 0, blocks)
    from_rows(gaff_ref, flat_ref, 3, blocks)


def paired(index, count, first):
    partner = index + 1 if (index - first) % 2 == 0 else index - 1
    return partner if 0 <= partner < count else None


def exchange(array, counts, pair):
    names = ("gx", "gy", "gz")
    links = []
    for x in range(counts[0]):
        for y in range(counts[1]):
            for z in range(counts[2]):
                target = pair(x, y, z)
                if None not in target:
                    links.append(((x * counts[1] + y) * counts[2] + z, (target[0] * counts[1] + target[1]) * counts[2] + target[2]))
    return lax.ppermute(array, names, links) if links else jnp.zeros_like(array)


def shards(
    offsets, velocity, affine, volume, cot_velocity, cot_affine, block_cells, fill_counts, baffle_top, drag
):
    brick, _, size_z = drag.shape
    blocks = block_cells.shape[0]
    counts = tuple(lax.axis_size(axis) for axis in ("gx", "gy", "gz"))
    interior = brick // 4
    vmem = pl.BlockSpec(memory_space=pltpu.VMEM)

    def f32(*shape):
        return jax.ShapeDtypeStruct(shape, F32)

    def bf16(*shape):
        return jax.ShapeDtypeStruct(shape, BF16)

    def call(kernel, name, out_shape, operands, scratch=(), megabytes=4, flops=0):
        return pl.pallas_call(
            kernel,
            out_shape=out_shape,
            in_specs=[vmem] * len(operands),
            out_specs=(vmem,) * len(out_shape),
            scratch_shapes=scratch,
            compiler_params=pltpu.CompilerParams(vmem_limit_bytes=megabytes * 1024 * 1024),
            cost_estimate=pl.CostEstimate(flops=flops, bytes_accessed=1024, transcendentals=0),
            name=name,
        )(*operands)

    operands = (
        block_cells.reshape(1, blocks), fill_counts.reshape(1, 1), offsets, velocity, affine, volume.reshape(blocks, LANES), cot_velocity, cot_affine,
        baffle_top, drag.transpose(0, 2, 1),
    )
    slab = f32(ROWS, LANES)
    ends = 2 if counts[2] > 2 else 1
    spread, take = call(
        spread_kernel, "spread", (bf16(21 * LANES, 2 * LANES), bf16(2 * LANES, 9 * LANES)), (), flops=20_000_000_000
    )
    edge, send_xe, send_xo, send_xz, meta, shape, window, hot_edge = call(
        deposit_kernel,
        "deposit",
        (
            f32(2, ROWS, LANES), slab, slab, f32(ends, 16, LANES),
            jax.ShapeDtypeStruct((3, blocks, LANES), jnp.int32), f32(12 * blocks, LANES),
            bf16(16 * blocks, 2 * LANES), bf16(16 * blocks, 2 * LANES),
        ),
        operands + (spread,),
        scratch=[
            pltpu.VMEM((27 * blocks, LANES), F32),
            pltpu.VMEM((18 * blocks, 21 * LANES), BF16),
            pltpu.VMEM((18 * blocks, 2 * LANES), F32),
            pltpu.VMEM((2 * LANES, 2 * LANES), F32),
        ],
        megabytes=16,
    )

    def even_x(x):
        return paired(x, counts[0], 0)

    def odd_x(x):
        partner = paired(x, counts[0], 1)
        return counts[0] - 1 - x if partner is None and counts[0] % 2 == 0 else partner

    def odd_y(x, y, z):
        partner = paired(y, counts[1], 1)
        return (even_x(x), y, z) if partner is None else (x, partner, z)

    xe = exchange(send_xe, counts, lambda x, y, z: (even_x(x), y, z))
    xo = exchange(send_xo, counts, lambda x, y, z: (odd_x(x), y, z))
    xz = [
        exchange(send_xz[first], counts, lambda x, y, z: (odd_x(x), y, paired(z, counts[2], first)))
        for first in range(ends)
    ]
    grid, hot = call(
        interior_kernel,
        "interior",
        (f32(2 + interior, ROWS, LANES), bf16(16 * blocks, (2 + interior) * LANES)),
        (window, meta, *operands[-2:]),
        scratch=[pltpu.VMEM((2 * LANES, (2 + interior) * LANES), F32)],
        megabytes=8,
        flops=1_000_000_000,
    )
    send_z = call(pack_z_kernel, "pack_z", (f32(SLABS + interior, 16, LANES),) * ends, (edge, grid, xe))
    layers = [
        exchange(array, counts, lambda x, y, z: (x, y, paired(z, counts[2], first)))
        for first, array in enumerate(send_z)
    ]
    send_ye, send_yo = call(
        functools.partial(pack_y_kernel, ends), "pack_y", (slab, slab), (grid, xe, xo, *xz, *layers)
    )
    yo = exchange(send_yo, counts, odd_y)
    ye = exchange(send_ye, counts, lambda x, y, z: (x, paired(y, counts[1], 0), z))
    gathered, drag_slab, drag_rows = call(
        functools.partial(early_kernel, counts, ends, size_z),
        "early",
        (f32(16 * blocks, LANES), f32(2, size_z, LANES), f32(interior, size_z, LANES)),
        (hot_edge, hot, edge, grid, xe, xo, *xz, *layers),
        scratch=[
            pltpu.VMEM((interior, ROWS + 16, LANES), F32),
            pltpu.VMEM((LANES, 2 * LANES), BF16),
            pltpu.VMEM((LANES, interior * LANES), BF16),
            pltpu.VMEM((8, LANES), F32),
        ],
        megabytes=8,
        flops=1_000_000_000,
    )
    grad_velocity, grad_affine, grad_volume, grad_drag = call(
        functools.partial(collect_kernel, counts, ends),
        "collect",
        (f32(3, blocks * LANES), f32(9, blocks * LANES), f32(blocks, LANES), f32(brick, size_z, brick)),
        (meta, shape, hot, take, baffle_top, gathered, drag_slab, drag_rows, grid, xe, xo, ye, yo, *xz, *layers),
        scratch=[
            pltpu.VMEM((2, ROWS + 16, LANES), F32),
            pltpu.VMEM((LANES, 2 * LANES), BF16),
            pltpu.VMEM((2, size_z, LANES), F32),
            pltpu.VMEM((9 * blocks, 2 * LANES), BF16),
            pltpu.VMEM((9 * blocks, 9 * LANES), F32),
            pltpu.VMEM((12 * blocks, LANES), F32),
        ],
        megabytes=12,
    )
    return grad_velocity, grad_affine, grad_volume.reshape(-1), grad_drag.transpose(0, 2, 1)


def solution(mesh):
    everywhere = ("gx", "gy", "gz")
    rows, flat = P(None, everywhere), P(everywhere)
    in_specs = (rows, rows, rows, flat, rows, rows, flat, flat, P("gx", "gy"), P("gx", "gy", "gz"))
    out_specs = (rows, rows, flat, P("gx", "gy", "gz"))
    return jax.shard_map(shards, mesh=mesh, in_specs=in_specs, out_specs=out_specs, check_vma=False)
```

```python
import functools

import jax
import jax.numpy as jnp
from jax import lax
from jax.experimental import pallas as pl
from jax.experimental.pallas import tpu as pltpu
from jax.sharding import PartitionSpec as P

stiffness = 2.0
gravity_step = 0.3

LANES = 128
SLABS = 4
ZROWS = 10
CHANNELS = 8
ROWS = ZROWS * CHANNELS
F32 = jnp.float32
BF16 = jnp.bfloat16


def iota(shape, dim):
    return lax.broadcasted_iota(jnp.int32, shape, dim)


def tile_nodes(tile, rows, brick):
    lane = iota((rows, LANES), 1)
    if tile < 2:
        x, y = lane >> 1, (lane & 1) + tile * brick
        valid = lane < 2 * (brick + 2)
    elif tile < SLABS:
        plane, corner = lane < 64, lane - 64
        x = jnp.where(plane, lane >> 5, (corner & 3) >> 1) + (tile - 2) * brick
        y = jnp.where(plane, (lane & 31) + 1, (corner >> 2) * brick + (corner & 1))
        valid = jnp.where(plane, ((y >= 2) & (y < brick)).astype(jnp.int32), (corner < 8).astype(jnp.int32)) == 1
    else:
        x = (lane >> 5) + 4 * (tile - SLABS) + 1
        y = (lane & 31) + 1
        valid = (x >= 2) & (x < brick) & (y >= 2) & (y < brick)
    return x, y, valid


def tile_code(tile, rows, brick):
    x, y, valid = tile_nodes(tile, rows, brick)
    return jnp.where(valid, x * 64 + y, -1)


def block_columns(cells_ref):
    blocks = cells_ref.shape[1]
    same = iota((blocks, blocks), 0) == iota((blocks, blocks), 1)
    column = jnp.sum(jnp.where(same, cells_ref[...].astype(F32), 0.0), axis=1, keepdims=True)
    cells = jnp.broadcast_to(column, (blocks, LANES)).astype(jnp.int32)
    return (cells >> 5) * 128 + ((cells >> 1) & 15) * 2, cells & 1


def fill_one_hot(hot_ref, code, tiles, brick, masks=(None,)):
    blocks = code.shape[0]
    for at, (mask, tile) in enumerate((mask, tile) for mask in masks for tile in tiles):
        lane_code = tile_code(tile, blocks, brick) - code
        if mask is not None:
            lane_code = jnp.where(mask, lane_code, -1)
        for node in range(16):
            hit = lane_code == (node // 4) * 64 + node % 4
            hot_ref[pl.ds(node * blocks, blocks), pl.ds(at * LANES, LANES)] = jnp.where(hit, 1.0, 0.0).astype(BF16)


def deposit_windows(grid_ref, window_ref, hot_ref, all_ref):
    all_ref[...] = lax.dot_general(
        window_ref[...], hot_ref[...], (((0,), (0,)), ((), ())), preferred_element_type=F32
    )
    for z in range(ZROWS):
        piece = None
        for tz in range(2):
            wz = z - 4 * tz
            if 0 <= wz < 6:
                row = 64 * tz + 8 * wz
                part = all_ref[pl.ds(row, 8), :] + all_ref[pl.ds(128 + row, 8), :]
                piece = part if piece is None else piece + part
        for tile in range(grid_ref.shape[0]):
            grid_ref[tile, pl.ds(8 * z, 8), :] = piece[:, tile * LANES : (tile + 1) * LANES]


def inner_tiles(brick):
    return (0, 1) + tuple(range(SLABS, SLABS + brick // 4))


def spline(frac):
    return [0.5 * (0.5 - frac) ** 2, 0.75 - frac * frac, 0.5 * (0.5 + frac) ** 2]


def split(value):
    high = value.astype(BF16)
    return high, (value - high.astype(F32)).astype(BF16)


def is_even(axis):
    return lax.rem(lax.axis_index(axis), 2) == 0


def low_high(even, odd, axis):
    here = is_even(axis)
    place = lax.axis_index(axis)
    low, high = jnp.where(here, odd, even), jnp.where(here, even, odd)
    return jnp.where(place > 0, low, 0.0), jnp.where(place < lax.axis_size(axis) - 1, high, 0.0)


def diagonal_rows(ends):
    even = ends[0]
    low, high = low_high(even, ends[1] if len(ends) > 1 else jnp.zeros_like(even), "gz")
    return jnp.concatenate([low, jnp.zeros((ROWS - 32, LANES), F32), high], axis=0)


def to_rows(flat_ref, first, array_ref, blocks):
    channels = array_ref.shape[0]
    if channels > 8:
        tiles = jnp.stack([array_ref[pl.ds(0, 8), pl.ds(b * LANES, LANES)] for b in range(blocks)])
        flat_ref[pl.ds(first * blocks, 8 * blocks), :] = jnp.swapaxes(tiles, 0, 1).reshape(8 * blocks, LANES)
        for b in range(blocks):
            flat_ref[pl.ds((first + 8) * blocks + b, 1), :] = array_ref[pl.ds(8, 1), pl.ds(b * LANES, LANES)]
        return
    for b in range(blocks):
        flat_ref[pl.ds(first * blocks + b, channels, stride=blocks), :] = array_ref[:, pl.ds(b * LANES, LANES)]


def from_rows(array_ref, flat_ref, first, blocks):
    channels = array_ref.shape[0]
    if channels > 8:
        tiles = flat_ref[pl.ds(first * blocks, 8 * blocks), :].reshape(8, blocks, LANES)
        tiles = jnp.swapaxes(tiles, 0, 1)
        for b in range(blocks):
            array_ref[pl.ds(0, 8), pl.ds(b * LANES, LANES)] = tiles[b]
            array_ref[pl.ds(8, 1), pl.ds(b * LANES, LANES)] = flat_ref[pl.ds((first + 8) * blocks + b, 1), :]
        return
    for b in range(blocks):
        array_ref[:, pl.ds(b * LANES, LANES)] = flat_ref[pl.ds(first * blocks + b, channels, stride=blocks), :]


def corners(low, high):
    lane = iota(low.shape, 1)
    first, last = lane < 4, (lane >= 64) & (lane < 68)
    zero = jnp.zeros_like(low)
    lower = jnp.where(first, pltpu.roll(low, 64, 1), jnp.where(last, high, zero))
    upper = jnp.where(first, pltpu.roll(low, 60, 1), jnp.where(last, pltpu.roll(high, 124, 1), zero))
    return lower, upper


def spread_kernel(spread_ref, take_ref):
    particle = iota((LANES, 2 * LANES), 0)
    shift = iota((LANES, 2 * LANES), 1) - ((particle >> 5) * 64 + ((particle >> 3) & 3) * 8)
    for c in range(7):
        for oz in range(3):
            hit = shift == oz * 8 + c
            spread_ref[pl.ds((3 * c + oz) * LANES, LANES), :] = jnp.where(hit, 1.0, 0.0).astype(BF16)
    key = iota((2 * LANES, LANES), 0)
    particle = iota((2 * LANES, LANES), 1)
    shift = jnp.where((key >> 6) == (particle >> 5), (key & 31) - ((particle >> 3) & 3), -64)
    for a in range(3):
        for oz in range(3):
            hit = shift == 8 * a + oz
            take_ref[:, pl.ds((3 * a + oz) * LANES, LANES)] = jnp.where(hit, 1.0, 0.0).astype(BF16)


def deposit_kernel(*refs):
    cells_ref, count_ref, pos_ref, vel_ref, aff_ref, vol_ref, cvel_ref, caff_ref, top_ref, drag_ref = refs[:10]
    spread_ref, refs = refs[10], refs[11:]
    grid_ref, even_ref, odd_ref, diagonal_ref, meta_ref, shape_ref, window_ref, hot_ref = refs[:8]
    flat_ref, terms_ref, sums_ref, all_ref = refs[8:]
    blocks = vol_ref.shape[0]
    brick = drag_ref.shape[0]
    size_z = drag_ref.shape[1]
    code, upper_tile = block_columns(cells_ref)
    live_rows = iota((blocks, LANES), 0) < count_ref[...]
    meta_ref[0], meta_ref[1], meta_ref[2] = code, upper_tile, live_rows.astype(jnp.int32)
    fill_one_hot(hot_ref, code, (2, 3), brick)
    for first, ref in ((0, pos_ref), (3, vel_ref), (6, aff_ref), (15, cvel_ref), (18, caff_ref)):
        to_rows(flat_ref, first, ref, blocks)

    def channel(c):
        return flat_ref[pl.ds(c * blocks, blocks), :]

    live = live_rows.astype(F32)
    frac = [channel(k) for k in range(3)]
    weight = [spline(f) for f in frac]
    for k, value in enumerate(weight[0] + weight[1] + weight[2] + frac):
        shape_ref[pl.ds(k * blocks, blocks), :] = value
    stretch = stiffness * (vol_ref[...] - 1.0)
    linear, matrix = [live], [None]
    for a in range(3):
        row = [live * (channel(6 + 3 * a + b) - (stretch if a == b else 0.0)) for b in range(3)]
        matrix.append(row)
        linear.append(live * channel(3 + a) - sum(row[b] * frac[b] for b in range(3)))
    for a in range(3):
        row = [(4.0 * live) * channel(18 + 3 * a + b) for b in range(3)]
        matrix.append(row)
        linear.append(live * channel(15 + a) - sum(row[b] * frac[b] for b in range(3)))

    def put(row, slot, value):
        high, low = split(value)
        lanes = pl.ds(slot * LANES, LANES)
        terms_ref[pl.ds(row * blocks, blocks), lanes] = high
        terms_ref[pl.ds((9 + row) * blocks, blocks), lanes] = low

    for ox in range(3):
        for oy in range(3):
            planar = weight[0][ox] * weight[1][oy]
            weights = [planar * weight[2][oz] for oz in range(3)]
            for c in range(7):
                base = linear[c]
                if c:
                    if ox != 1:
                        base = base + matrix[c][0] if ox else base - matrix[c][0]
                    if oy != 1:
                        base = base + matrix[c][1] if oy else base - matrix[c][1]
                for oz in range(3):
                    value = base
                    if c and oz != 1:
                        value = base + matrix[c][2] if oz else base - matrix[c][2]
                    put(3 * ox + oy, 3 * c + oz, weights[oz] * value)

    sums_ref[...] = jnp.dot(terms_ref[...], spread_ref[...], preferred_element_type=F32)

    lane = iota((blocks, LANES), 1)
    low_half = lane < 64
    own_half = low_half == (upper_tile == 0)

    def partial(wx, oy):
        total = None
        for cx in range(2):
            ox = wx - cx
            if 0 <= ox < 3:
                lanes = pl.ds(cx * LANES, LANES)
                row = 3 * ox + oy
                piece = sums_ref[pl.ds(row * blocks, blocks), lanes] + sums_ref[pl.ds((9 + row) * blocks, blocks), lanes]
                total = piece if total is None else total + piece
        return total

    for wx in range(4):
        columns = [partial(wx, oy) for oy in range(3)]
        zero = jnp.zeros_like(columns[0])
        for wy in range(4):
            both = jnp.where(low_half, columns[wy] if wy < 3 else zero, columns[wy - 1] if wy else zero)
            node = jnp.where(own_half, both + pltpu.roll(both, 64, 1), 0.0)
            high, low = split(node)
            rows = pl.ds((4 * wx + wy) * blocks, blocks)
            window_ref[rows, pl.ds(0, LANES)] = high
            window_ref[rows, pl.ds(LANES, LANES)] = low

    deposit_windows(grid_ref, window_ref, hot_ref, all_ref)

    depth = iota((size_z, brick), 0) + lax.axis_index("gz") * size_z
    lane = iota((size_z, LANES), 1)
    blank = jnp.zeros((size_z, 32), F32)
    for side, x in enumerate((0, brick - 1)):
        layer = jnp.where(depth < top_ref[pl.ds(x, 1), :], drag_ref[x], 0.0)
        plane = jnp.concatenate([blank, layer, blank, blank] if side == 0 else [layer, blank, blank, blank], axis=1)
        plane = jnp.where(lane == 67 - 2 * side, layer[:, 0:1], plane)
        plane = jnp.where(lane == 70 - 2 * side, layer[:, brick - 1 : brick], plane)
        grid_ref[side, pl.ds(8 + 7, size_z, stride=8), :] = plane

    low, high = grid_ref[0], grid_ref[1]
    here = is_even("gx")
    even_ref[...] = jnp.where(here, high, low)
    odd_ref[...] = jnp.where(here, low, high)
    here = is_even("gz")
    lower, upper = odd_ref[pl.ds(0, 16), :], odd_ref[pl.ds(ROWS - 16, 16), :]
    diagonal_ref[0] = jnp.where(here, upper, lower)
    if diagonal_ref.shape[0] > 1:
        diagonal_ref[1] = jnp.where(here, lower, upper)


def interior_kernel(window_ref, meta_ref, top_ref, drag_ref, grid_ref, hot_ref, all_ref):
    brick, size_z, _ = drag_ref.shape
    fill_one_hot(hot_ref, meta_ref[0], inner_tiles(brick), brick)
    deposit_windows(grid_ref, window_ref, hot_ref, all_ref)
    depth = iota((size_z, brick), 0) + lax.axis_index("gz") * size_z
    lane = iota((size_z, LANES), 1)
    ends = [jnp.zeros((size_z, LANES), F32)] * 2
    layers = []
    for x in range(brick):
        layer = jnp.where(depth < top_ref[pl.ds(x, 1), :], drag_ref[x], 0.0)
        layers.append(layer)
        ends[0] = jnp.where(lane == 2 * (x + 1) + 1, layer[:, 0:1], ends[0])
        ends[1] = jnp.where(lane == 2 * (x + 1), layer[:, brick - 1 : brick], ends[1])
    planes = ends + [jnp.concatenate(layers[4 * t : 4 * t + 4], axis=1) for t in range(brick // 4)]
    for at, plane in enumerate(planes):
        grid_ref[at, pl.ds(8 + 7, size_z, stride=8), :] = plane


def own_tile(slab_ref, grid_ref, tile):
    return grid_ref[tile] if tile < 2 else slab_ref[tile - 2] if tile < SLABS else grid_ref[tile - 2]


def pack_z_kernel(slab_ref, grid_ref, xe_ref, even_ref, *odd_refs):
    here = is_even("gz")
    ends = []
    for first in (0, ROWS - 16):
        rows = pl.ds(first, 16)
        received = xe_ref[rows, :]
        extra = x_additions(*low_high(received, jnp.zeros_like(received), "gx"))
        ends.append([own_tile(slab_ref, grid_ref, t)[first : first + 16] + extra[t] for t in range(SLABS)])
        ends[-1] += [grid_ref[t, rows, :] for t in range(2, grid_ref.shape[0])]
    for tile, (lower, upper) in enumerate(zip(*ends)):
        even_ref[tile] = jnp.where(here, upper, lower)
        for odd_ref in odd_refs:
            odd_ref[tile] = jnp.where(here, lower, upper)


def x_additions(low, high):
    lower, upper = corners(low, high)
    planar = iota(low.shape, 1) < 64
    return [lower, upper, jnp.where(planar, low, 0.0), jnp.where(planar, high, 0.0)]


def xz_additions(xe_ref, xo_ref, diagonals, layers, tiles):
    odd = xo_ref[...] + diagonal_rows([ref[...] for ref in diagonals])
    extra = x_additions(*low_high(xe_ref[...], odd, "gx"))
    return [extra[t] + diagonal_rows([ref[t] for ref in layers]) for t in range(tiles)]


def pack_y_kernel(ends, *refs):
    grid_ref, xe_ref, xo_ref, *received = refs[:-3]
    even_ref, odd_ref, sums_ref = refs[-3:]
    extra = xz_additions(xe_ref, xo_ref, received[:ends], received[ends:], 2)
    lower, upper = grid_ref[0] + extra[0], grid_ref[1] + extra[1]
    sums_ref[0], sums_ref[1] = lower, upper
    here = is_even("gy")
    even_ref[...] = jnp.where(here, upper, lower)
    odd_ref[...] = jnp.where(here, lower, upper)


def node_gradients(counts, brick, size_z, tiles, totals, total_ref, push_ref, drag_ref, apart=0):
    place = [lax.axis_index(axis) for axis in ("gx", "gy", "gz")]
    row = iota((8, LANES), 0)
    blank = jnp.zeros((8, LANES), F32)
    for at, (tile, total) in enumerate(zip(tiles, totals)):
        total_ref[at, pl.ds(0, ROWS), :] = total
        total_ref[at, pl.ds(ROWS, 16), :] = jnp.zeros((16, LANES), F32)
        lanes = pl.ds(at * LANES, LANES)
        node_x, node_y, _ = tile_nodes(tile, 8, brick)
        node_x = node_x + (place[0] * brick - 1)
        node_y = node_y + (place[1] * brick - 1)
        drags = []
        for side in range(2):
            c = [total_ref[at, pl.ds(32 * side + k, 8, stride=8), :] for k in range(CHANNELS)]
            node_z = row + (4 * side - 1) + place[2] * size_z
            inside = (node_z >= 0) & (node_z < counts[2] * size_z)
            if tile in (2, 3):
                inside = inside & (iota((8, LANES), 1) < 64)
            if tile < SLABS:
                inside = inside & (node_x >= 0) & (node_x < counts[0] * brick)
                inside = inside & (node_y >= 0) & (node_y < counts[1] * brick)
            inverse = 1.0 / jnp.maximum(c[0], 1.0)
            scale = jnp.where(inside, (1.0 - c[7]) * inverse, 0.0)
            high, low = split(jnp.concatenate([c[4 + a] * scale for a in range(3)] + [blank], axis=0))
            if apart:
                lanes = pl.ds((apart * side + at) * LANES, LANES)
            for first in (0, 64) if apart else (64 * side,):
                push_ref[pl.ds(first, 32), lanes] = high
                push_ref[pl.ds(first + 32, 32), lanes] = low
            drags.append(
                c[4] * (c[1] * inverse) + c[5] * (c[2] * inverse) + c[6] * (c[3] * inverse - gravity_step)
            )
        drag_ref[at] = jnp.where(row < 7, pltpu.roll(drags[0], 7, 0), pltpu.roll(drags[1], 3, 0))


def gather(hot, push_ref):
    return lax.dot_general(hot, push_ref[...], (((1,), (1,)), ((), ())), preferred_element_type=F32)


def early_kernel(counts, ends, size_z, *refs):
    inputs, refs = refs[:-7], refs[-7:]
    meta_ref, hot_slab_ref, hot_ref, slab_ref, grid_ref, xe_ref, xo_ref, *received = inputs
    gathered_ref, drag_slab_ref, drag_ref, masked_ref, total_ref, push_slab_ref, push_ref = refs
    brick = 4 * (grid_ref.shape[0] - 2)
    extra = xz_additions(xe_ref, xo_ref, received[:ends], received[ends:], SLABS)
    totals = [slab_ref[tile - 2] + extra[tile] for tile in (2, 3)]
    node_gradients(counts, brick, size_z, (2, 3), totals, total_ref, push_slab_ref, drag_slab_ref)
    tiles = inner_tiles(brick)[2:]
    totals = [grid_ref[t - 2] + diagonal_rows([ref[t] for ref in received[ends:]]) for t in tiles]
    node_gradients(counts, brick, size_z, tiles, totals, total_ref, push_ref, drag_ref)
    gathered = gather(hot_slab_ref[...], push_slab_ref) + gather(
        hot_ref[:, pl.ds(2 * LANES, push_ref.shape[1])], push_ref
    )
    upper = meta_ref[1] == 1
    blocks = upper.shape[0]
    keep = (iota((blocks, LANES), 1) < 64) != upper
    for node in range(16):
        value = gathered[node * blocks : (node + 1) * blocks]
        gathered_ref[pl.ds(node * blocks, blocks), :] = jnp.where(keep, value, pltpu.roll(value, 64, 1))
    fill_one_hot(masked_ref, meta_ref[0], (0, 1), brick, (jnp.logical_not(upper), upper))


def collect_kernel(counts, *refs):
    inputs, refs = refs[:-10], refs[-10:]
    meta_ref, shape_ref, masked_ref, take_spread_ref, top_ref, gathered_ref, drag_slab_ref, drag_ref = inputs[:8]
    near_ref, ye_ref, yo_ref = inputs[8:]
    gvel_ref, gaff_ref, gvol_ref, gdrag_ref = refs[:4]
    total_ref, push_ref, drag_ends_ref, take_ref, pulled_ref, flat_ref = refs[4:]
    blocks = gvol_ref.shape[0]
    brick, size_z = gdrag_ref.shape[0], gdrag_ref.shape[1]
    saved = [shape_ref[pl.ds(k * blocks, blocks), :] for k in range(12)]
    weight, frac = [saved[3 * k : 3 * k + 3] for k in range(3)], saved[9:]

    low, high = low_high(ye_ref[...], yo_ref[...], "gy")
    totals = [near_ref[0] + low, near_ref[1] + high]
    node_gradients(counts, brick, size_z, (0, 1), totals, total_ref, push_ref, drag_ends_ref, 2)
    gathered = gathered_ref[...] + gather(masked_ref[...], push_ref)

    edges = [drag_ends_ref[t] for t in range(2)]
    depth = iota((size_z, brick), 0) + lax.axis_index("gz") * size_z
    lane = iota((size_z, LANES), 1)
    for x in range(brick):
        if x == 0:
            plane = pltpu.roll(drag_slab_ref[0], 96, 1)
        elif x == brick - 1:
            plane = drag_slab_ref[1]
        else:
            plane = drag_ref[x // 4]
            if x % 4:
                plane = pltpu.roll(plane, LANES - 32 * (x % 4), 1)
        at = 2 * (x + 1)
        plane = jnp.where(lane == 0, edges[0][:, at + 1 : at + 2], plane)
        plane = jnp.where(lane == brick - 1, edges[1][:, at : at + 1], plane)
        gdrag_ref[x] = jnp.where(depth < top_ref[pl.ds(x, 1), :], -plane[:, :brick], 0.0)

    lane = iota((blocks, LANES), 1)
    low_half = lane < 64
    nodes = [gathered[node * blocks : (node + 1) * blocks] for node in range(16)]
    for ox in range(3):
        for oy in range(3):
            for cx in range(2):
                value = jnp.where(low_half, nodes[4 * (cx + ox) + oy], nodes[4 * (cx + ox) + oy + 1])
                take_ref[pl.ds((3 * ox + oy) * blocks, blocks), pl.ds(cx * LANES, LANES)] = value.astype(BF16)

    pulled_ref[...] = jnp.dot(take_ref[...], take_spread_ref[...], preferred_element_type=F32)

    live = meta_ref[2].astype(F32)
    planar = [[live * weight[0][ox] * weight[1][oy] for oy in range(3)] for ox in range(3)]
    trace = None
    for a in range(3):
        sums_x, sums_y, sums_z = [], [None] * 3, None
        for ox in range(3):
            column = None
            for oy in range(3):
                rows = pl.ds((3 * ox + oy) * blocks, blocks)
                g = [pulled_ref[rows, pl.ds((3 * a + oz) * LANES, LANES)] for oz in range(3)]
                below, above = weight[2][0] * g[0], weight[2][2] * g[2]
                sum_z = planar[ox][oy] * (weight[2][1] * g[1] + (below + above))
                slope = planar[ox][oy] * (above - below)
                column = sum_z if column is None else column + sum_z
                sums_y[oy] = sum_z if sums_y[oy] is None else sums_y[oy] + sum_z
                sums_z = slope if sums_z is None else sums_z + slope
            sums_x.append(column)
        whole = sums_x[0] + sums_x[1] + sums_x[2]
        moments = [sums_x[2] - sums_x[0], sums_y[2] - sums_y[0], sums_z]
        flat_ref[pl.ds(a * blocks, blocks), :] = whole
        for b in range(3):
            value = moments[b] - frac[b] * whole
            flat_ref[pl.ds((3 + 3 * a + b) * blocks, blocks), :] = value
            if a == b:
                trace = value if trace is None else trace + value
    gvol_ref[...] = -stiffness * trace
    from_rows(gvel_ref, flat_ref, 0, blocks)
    from_rows(gaff_ref, flat_ref, 3, blocks)


def paired(index, count, first):
    partner = index + 1 if (index - first) % 2 == 0 else index - 1
    return partner if 0 <= partner < count else None


def exchange(array, counts, pair):
    names = ("gx", "gy", "gz")
    links = []
    for x in range(counts[0]):
        for y in range(counts[1]):
            for z in range(counts[2]):
                target = pair(x, y, z)
                if None not in target:
                    links.append(((x * counts[1] + y) * counts[2] + z, (target[0] * counts[1] + target[1]) * counts[2] + target[2]))
    return lax.ppermute(array, names, links) if links else jnp.zeros_like(array)


def shards(
    offsets, velocity, affine, volume, cot_velocity, cot_affine, block_cells, fill_counts, baffle_top, drag
):
    brick, _, size_z = drag.shape
    blocks = block_cells.shape[0]
    counts = tuple(lax.axis_size(axis) for axis in ("gx", "gy", "gz"))
    interior = brick // 4
    vmem = pl.BlockSpec(memory_space=pltpu.VMEM)

    def f32(*shape):
        return jax.ShapeDtypeStruct(shape, F32)

    def bf16(*shape):
        return jax.ShapeDtypeStruct(shape, BF16)

    def call(kernel, name, out_shape, operands, scratch=(), megabytes=4, flops=0):
        return pl.pallas_call(
            kernel,
            out_shape=out_shape,
            in_specs=[vmem] * len(operands),
            out_specs=(vmem,) * len(out_shape),
            scratch_shapes=scratch,
            compiler_params=pltpu.CompilerParams(vmem_limit_bytes=megabytes * 1024 * 1024),
            cost_estimate=pl.CostEstimate(flops=flops, bytes_accessed=1024, transcendentals=0),
            name=name,
        )(*operands)

    operands = (
        block_cells.reshape(1, blocks), fill_counts.reshape(1, 1), offsets, velocity, affine, volume.reshape(blocks, LANES), cot_velocity, cot_affine,
        baffle_top, drag.transpose(0, 2, 1),
    )
    slab = f32(ROWS, LANES)
    ends = 2 if counts[2] > 2 else 1
    spread, take = call(
        spread_kernel, "spread", (bf16(21 * LANES, 2 * LANES), bf16(2 * LANES, 9 * LANES)), (), flops=20_000_000_000
    )
    edge, send_xe, send_xo, send_xz, meta, shape, window, hot_edge = call(
        deposit_kernel,
        "deposit",
        (
            f32(2, ROWS, LANES), slab, slab, f32(ends, 16, LANES),
            jax.ShapeDtypeStruct((3, blocks, LANES), jnp.int32), f32(12 * blocks, LANES),
            bf16(16 * blocks, 2 * LANES), bf16(16 * blocks, 2 * LANES),
        ),
        operands + (spread,),
        scratch=[
            pltpu.VMEM((27 * blocks, LANES), F32),
            pltpu.VMEM((18 * blocks, 21 * LANES), BF16),
            pltpu.VMEM((18 * blocks, 2 * LANES), F32),
            pltpu.VMEM((2 * LANES, 2 * LANES), F32),
        ],
        megabytes=16,
    )

    def even_x(x):
        return paired(x, counts[0], 0)

    def odd_x(x):
        partner = paired(x, counts[0], 1)
        return counts[0] - 1 - x if partner is None and counts[0] % 2 == 0 else partner

    def odd_y(x, y, z):
        partner = paired(y, counts[1], 1)
        return (even_x(x), y, z) if partner is None else (x, partner, z)

    xe = exchange(send_xe, counts, lambda x, y, z: (even_x(x), y, z))
    xo = exchange(send_xo, counts, lambda x, y, z: (odd_x(x), y, z))
    xz = [
        exchange(send_xz[first], counts, lambda x, y, z: (odd_x(x), y, paired(z, counts[2], first)))
        for first in range(ends)
    ]
    grid, hot = call(
        interior_kernel,
        "interior",
        (f32(2 + interior, ROWS, LANES), bf16(16 * blocks, (2 + interior) * LANES)),
        (window, meta, *operands[-2:]),
        scratch=[pltpu.VMEM((2 * LANES, (2 + interior) * LANES), F32)],
        megabytes=8,
        flops=1_000_000_000,
    )
    send_z = call(pack_z_kernel, "pack_z", (f32(SLABS + interior, 16, LANES),) * ends, (edge, grid, xe))
    layers = [
        exchange(array, counts, lambda x, y, z: (x, y, paired(z, counts[2], first)))
        for first, array in enumerate(send_z)
    ]
    send_ye, send_yo, near_y = call(
        functools.partial(pack_y_kernel, ends), "pack_y", (slab, slab, f32(2, ROWS, LANES)), (grid, xe, xo, *xz, *layers)
    )
    yo = exchange(send_yo, counts, odd_y)
    ye = exchange(send_ye, counts, lambda x, y, z: (x, paired(y, counts[1], 0), z))
    gathered, drag_slab, drag_rows, masked = call(
        functools.partial(early_kernel, counts, ends, size_z),
        "early",
        (
            f32(16 * blocks, LANES), f32(2, size_z, LANES), f32(interior, size_z, LANES),
            bf16(16 * blocks, 4 * LANES),
        ),
        (meta, hot_edge, hot, edge, grid, xe, xo, *xz, *layers),
        scratch=[
            pltpu.VMEM((interior, ROWS + 16, LANES), F32),
            pltpu.VMEM((LANES, 2 * LANES), BF16),
            pltpu.VMEM((LANES, interior * LANES), BF16),
        ],
        megabytes=8,
        flops=1_000_000_000,
    )
    grad_velocity, grad_affine, grad_volume, grad_drag = call(
        functools.partial(collect_kernel, counts),
        "collect",
        (f32(3, blocks * LANES), f32(9, blocks * LANES), f32(blocks, LANES), f32(brick, size_z, brick)),
        (meta, shape, masked, take, baffle_top, gathered, drag_slab, drag_rows, near_y, ye, yo),
        scratch=[
            pltpu.VMEM((2, ROWS + 16, LANES), F32),
            pltpu.VMEM((LANES, 4 * LANES), BF16),
            pltpu.VMEM((2, size_z, LANES), F32),
            pltpu.VMEM((9 * blocks, 2 * LANES), BF16),
            pltpu.VMEM((9 * blocks, 9 * LANES), F32),
            pltpu.VMEM((12 * blocks, LANES), F32),
        ],
        megabytes=12,
    )
    return grad_velocity, grad_affine, grad_volume.reshape(-1), grad_drag.transpose(0, 2, 1)


def solution(mesh):
    everywhere = ("gx", "gy", "gz")
    rows, flat = P(None, everywhere), P(everywhere)
    in_specs = (rows, rows, rows, flat, rows, rows, flat, flat, P("gx", "gy"), P("gx", "gy", "gz"))
    out_specs = (rows, rows, flat, P("gx", "gy", "gz"))
    return jax.shard_map(shards, mesh=mesh, in_specs=in_specs, out_specs=out_specs, check_vma=False)
```

```python
import functools

import jax
import jax.numpy as jnp
from jax import lax
from jax.experimental import pallas as pl
from jax.experimental.pallas import tpu as pltpu
from jax.sharding import PartitionSpec as P

stiffness = 2.0
gravity_step = 0.3

LANES = 128
SLABS = 4
ZROWS = 10
CHANNELS = 8
ROWS = ZROWS * CHANNELS
F32 = jnp.float32
BF16 = jnp.bfloat16


def iota(shape, dim):
    return lax.broadcasted_iota(jnp.int32, shape, dim)


def tile_nodes(tile, rows, brick):
    lane = iota((rows, LANES), 1)
    if tile < 2:
        x, y = lane >> 1, (lane & 1) + tile * brick
        valid = lane < 2 * (brick + 2)
    elif tile < SLABS:
        plane, corner = lane < 64, lane - 64
        x = jnp.where(plane, lane >> 5, (corner & 3) >> 1) + (tile - 2) * brick
        y = jnp.where(plane, (lane & 31) + 1, (corner >> 2) * brick + (corner & 1))
        valid = jnp.where(plane, ((y >= 2) & (y < brick)).astype(jnp.int32), (corner < 8).astype(jnp.int32)) == 1
    else:
        x = (lane >> 5) + 4 * (tile - SLABS) + 1
        y = (lane & 31) + 1
        valid = (x >= 2) & (x < brick) & (y >= 2) & (y < brick)
    return x, y, valid


def tile_code(tile, rows, brick):
    x, y, valid = tile_nodes(tile, rows, brick)
    return jnp.where(valid, x * 64 + y, -1)


def block_columns(cells_ref):
    blocks = cells_ref.shape[1]
    same = iota((blocks, blocks), 0) == iota((blocks, blocks), 1)
    column = jnp.sum(jnp.where(same, cells_ref[...].astype(F32), 0.0), axis=1, keepdims=True)
    cells = jnp.broadcast_to(column, (blocks, LANES)).astype(jnp.int32)
    return (cells >> 5) * 128 + ((cells >> 1) & 15) * 2, cells & 1


def fill_one_hot(hot_ref, code, tiles, brick, masks=(None,)):
    blocks = code.shape[0]
    for at, (mask, tile) in enumerate((mask, tile) for mask in masks for tile in tiles):
        lane_code = tile_code(tile, blocks, brick) - code
        if mask is not None:
            lane_code = jnp.where(mask, lane_code, -1)
        for node in range(16):
            hit = lane_code == (node // 4) * 64 + node % 4
            hot_ref[pl.ds(node * blocks, blocks), pl.ds(at * LANES, LANES)] = jnp.where(hit, 1.0, 0.0).astype(BF16)


def deposit_windows(grid_ref, window_ref, hot_ref, all_ref):
    all_ref[...] = lax.dot_general(
        window_ref[...], hot_ref[...], (((0,), (0,)), ((), ())), preferred_element_type=F32
    )
    for z in range(ZROWS):
        piece = None
        for tz in range(2):
            wz = z - 4 * tz
            if 0 <= wz < 6:
                row = 64 * tz + 8 * wz
                part = all_ref[pl.ds(row, 8), :] + all_ref[pl.ds(128 + row, 8), :]
                piece = part if piece is None else piece + part
        for tile in range(grid_ref.shape[0]):
            grid_ref[tile, pl.ds(8 * z, 8), :] = piece[:, tile * LANES : (tile + 1) * LANES]


def inner_tiles(brick):
    return (0, 1) + tuple(range(SLABS, SLABS + brick // 4))


def spline(frac):
    return [0.5 * (0.5 - frac) ** 2, 0.75 - frac * frac, 0.5 * (0.5 + frac) ** 2]


def split(value):
    high = value.astype(BF16)
    return high, (value - high.astype(F32)).astype(BF16)


def is_even(axis):
    return lax.rem(lax.axis_index(axis), 2) == 0


def low_high(even, odd, axis):
    here = is_even(axis)
    place = lax.axis_index(axis)
    low, high = jnp.where(here, odd, even), jnp.where(here, even, odd)
    return jnp.where(place > 0, low, 0.0), jnp.where(place < lax.axis_size(axis) - 1, high, 0.0)


def diagonal_rows(ends):
    even = ends[0]
    low, high = low_high(even, ends[1] if len(ends) > 1 else jnp.zeros_like(even), "gz")
    return jnp.concatenate([low, jnp.zeros((ROWS - 32, LANES), F32), high], axis=0)


def to_rows(flat_ref, first, array_ref, blocks):
    channels = array_ref.shape[0]
    if channels > 8:
        tiles = jnp.stack([array_ref[pl.ds(0, 8), pl.ds(b * LANES, LANES)] for b in range(blocks)])
        flat_ref[pl.ds(first * blocks, 8 * blocks), :] = jnp.swapaxes(tiles, 0, 1).reshape(8 * blocks, LANES)
        for b in range(blocks):
            flat_ref[pl.ds((first + 8) * blocks + b, 1), :] = array_ref[pl.ds(8, 1), pl.ds(b * LANES, LANES)]
        return
    for b in range(blocks):
        flat_ref[pl.ds(first * blocks + b, channels, stride=blocks), :] = array_ref[:, pl.ds(b * LANES, LANES)]


def from_rows(array_ref, flat_ref, first, blocks):
    channels = array_ref.shape[0]
    if channels > 8:
        tiles = flat_ref[pl.ds(first * blocks, 8 * blocks), :].reshape(8, blocks, LANES)
        tiles = jnp.swapaxes(tiles, 0, 1)
        for b in range(blocks):
            array_ref[pl.ds(0, 8), pl.ds(b * LANES, LANES)] = tiles[b]
            array_ref[pl.ds(8, 1), pl.ds(b * LANES, LANES)] = flat_ref[pl.ds((first + 8) * blocks + b, 1), :]
        return
    for b in range(blocks):
        array_ref[:, pl.ds(b * LANES, LANES)] = flat_ref[pl.ds(first * blocks + b, channels, stride=blocks), :]


def corners(low, high):
    lane = iota(low.shape, 1)
    first, last = lane < 4, (lane >= 64) & (lane < 68)
    zero = jnp.zeros_like(low)
    lower = jnp.where(first, pltpu.roll(low, 64, 1), jnp.where(last, high, zero))
    upper = jnp.where(first, pltpu.roll(low, 60, 1), jnp.where(last, pltpu.roll(high, 124, 1), zero))
    return lower, upper


def spread_kernel(spread_ref, take_ref):
    particle = iota((LANES, 2 * LANES), 0)
    shift = iota((LANES, 2 * LANES), 1) - ((particle >> 5) * 64 + ((particle >> 3) & 3) * 8)
    for c in range(7):
        for oz in range(3):
            hit = shift == oz * 8 + c
            spread_ref[pl.ds((3 * c + oz) * LANES, LANES), :] = jnp.where(hit, 1.0, 0.0).astype(BF16)
    key = iota((2 * LANES, LANES), 0)
    particle = iota((2 * LANES, LANES), 1)
    shift = jnp.where((key >> 6) == (particle >> 5), (key & 31) - ((particle >> 3) & 3), -64)
    for a in range(3):
        for oz in range(3):
            hit = shift == 8 * a + oz
            take_ref[:, pl.ds((3 * a + oz) * LANES, LANES)] = jnp.where(hit, 1.0, 0.0).astype(BF16)


def deposit_kernel(*refs):
    cells_ref, count_ref, pos_ref, vel_ref, aff_ref, vol_ref, cvel_ref, caff_ref, top_ref, drag_ref = refs[:10]
    spread_ref, refs = refs[10], refs[11:]
    grid_ref, even_ref, odd_ref, diagonal_ref, meta_ref, shape_ref, window_ref, hot_ref = refs[:8]
    flat_ref, terms_ref, sums_ref, all_ref = refs[8:]
    blocks = vol_ref.shape[0]
    brick = drag_ref.shape[0]
    size_z = drag_ref.shape[1]
    code, upper_tile = block_columns(cells_ref)
    live_rows = iota((blocks, LANES), 0) < count_ref[...]
    meta_ref[0], meta_ref[1], meta_ref[2] = code, upper_tile, live_rows.astype(jnp.int32)
    fill_one_hot(hot_ref, code, (2, 3), brick)
    for first, ref in ((0, pos_ref), (3, vel_ref), (6, aff_ref), (15, cvel_ref), (18, caff_ref)):
        to_rows(flat_ref, first, ref, blocks)

    def channel(c):
        return flat_ref[pl.ds(c * blocks, blocks), :]

    live = live_rows.astype(F32)
    frac = [channel(k) for k in range(3)]
    weight = [spline(f) for f in frac]
    for k, value in enumerate(weight[0] + weight[1] + weight[2] + frac):
        shape_ref[pl.ds(k * blocks, blocks), :] = value
    stretch = stiffness * (vol_ref[...] - 1.0)
    linear, matrix = [live], [None]
    for a in range(3):
        row = [live * (channel(6 + 3 * a + b) - (stretch if a == b else 0.0)) for b in range(3)]
        matrix.append(row)
        linear.append(live * channel(3 + a) - sum(row[b] * frac[b] for b in range(3)))
    for a in range(3):
        row = [(4.0 * live) * channel(18 + 3 * a + b) for b in range(3)]
        matrix.append(row)
        linear.append(live * channel(15 + a) - sum(row[b] * frac[b] for b in range(3)))

    def put(row, slot, value):
        high, low = split(value)
        lanes = pl.ds(slot * LANES, LANES)
        terms_ref[pl.ds(row * blocks, blocks), lanes] = high
        terms_ref[pl.ds((9 + row) * blocks, blocks), lanes] = low

    for ox in range(3):
        for oy in range(3):
            planar = weight[0][ox] * weight[1][oy]
            weights = [planar * weight[2][oz] for oz in range(3)]
            for c in range(7):
                base = linear[c]
                if c:
                    if ox != 1:
                        base = base + matrix[c][0] if ox else base - matrix[c][0]
                    if oy != 1:
                        base = base + matrix[c][1] if oy else base - matrix[c][1]
                for oz in range(3):
                    value = base
                    if c and oz != 1:
                        value = base + matrix[c][2] if oz else base - matrix[c][2]
                    put(3 * ox + oy, 3 * c + oz, weights[oz] * value)

    sums_ref[...] = jnp.dot(terms_ref[...], spread_ref[...], preferred_element_type=F32)

    lane = iota((blocks, LANES), 1)
    low_half = lane < 64
    own_half = low_half == (upper_tile == 0)

    def partial(wx, oy):
        total = None
        for cx in range(2):
            ox = wx - cx
            if 0 <= ox < 3:
                lanes = pl.ds(cx * LANES, LANES)
                row = 3 * ox + oy
                piece = sums_ref[pl.ds(row * blocks, blocks), lanes] + sums_ref[pl.ds((9 + row) * blocks, blocks), lanes]
                total = piece if total is None else total + piece
        return total

    for wx in range(4):
        columns = [partial(wx, oy) for oy in range(3)]
        zero = jnp.zeros_like(columns[0])
        for wy in range(4):
            both = jnp.where(low_half, columns[wy] if wy < 3 else zero, columns[wy - 1] if wy else zero)
            node = jnp.where(own_half, both + pltpu.roll(both, 64, 1), 0.0)
            high, low = split(node)
            rows = pl.ds((4 * wx + wy) * blocks, blocks)
            window_ref[rows, pl.ds(0, LANES)] = high
            window_ref[rows, pl.ds(LANES, LANES)] = low

    deposit_windows(grid_ref, window_ref, hot_ref, all_ref)

    depth = iota((size_z, brick), 0) + lax.axis_index("gz") * size_z
    lane = iota((size_z, LANES), 1)
    blank = jnp.zeros((size_z, 32), F32)
    for side, x in enumerate((0, brick - 1)):
        layer = jnp.where(depth < top_ref[pl.ds(x, 1), :], drag_ref[x], 0.0)
        plane = jnp.concatenate([blank, layer, blank, blank] if side == 0 else [layer, blank, blank, blank], axis=1)
        plane = jnp.where(lane == 67 - 2 * side, layer[:, 0:1], plane)
        plane = jnp.where(lane == 70 - 2 * side, layer[:, brick - 1 : brick], plane)
        grid_ref[side, pl.ds(8 + 7, size_z, stride=8), :] = plane

    low, high = grid_ref[0], grid_ref[1]
    here = is_even("gx")
    even_ref[pl.ds(0, ROWS), :] = jnp.where(here, high, low)
    even_ref[pl.ds(ROWS, even_ref.shape[0] - ROWS), :] = jnp.zeros((even_ref.shape[0] - ROWS, LANES), F32)
    odd_ref[...] = jnp.where(here, low, high)
    here = is_even("gz")
    lower, upper = odd_ref[pl.ds(0, 16), :], odd_ref[pl.ds(ROWS - 16, 16), :]
    diagonal_ref[0] = jnp.where(here, upper, lower)
    if diagonal_ref.shape[0] > 1:
        diagonal_ref[1] = jnp.where(here, lower, upper)


def interior_kernel(window_ref, meta_ref, top_ref, drag_ref, grid_ref, hot_ref, all_ref):
    brick, size_z, _ = drag_ref.shape
    fill_one_hot(hot_ref, meta_ref[0], inner_tiles(brick), brick)
    deposit_windows(grid_ref, window_ref, hot_ref, all_ref)
    depth = iota((size_z, brick), 0) + lax.axis_index("gz") * size_z
    lane = iota((size_z, LANES), 1)
    ends = [jnp.zeros((size_z, LANES), F32)] * 2
    layers = []
    for x in range(brick):
        layer = jnp.where(depth < top_ref[pl.ds(x, 1), :], drag_ref[x], 0.0)
        layers.append(layer)
        ends[0] = jnp.where(lane == 2 * (x + 1) + 1, layer[:, 0:1], ends[0])
        ends[1] = jnp.where(lane == 2 * (x + 1), layer[:, brick - 1 : brick], ends[1])
    planes = ends + [jnp.concatenate(layers[4 * t : 4 * t + 4], axis=1) for t in range(brick // 4)]
    for at, plane in enumerate(planes):
        grid_ref[at, pl.ds(8 + 7, size_z, stride=8), :] = plane


def join_columns(near_y, near_x):
    lane = iota(near_y.shape, 1)
    near_x = jnp.where(lane < 98, pltpu.roll(near_x, 67, 1), pltpu.roll(near_x, 65, 1))
    return jnp.where(lane < 68, near_y, near_x)


def joined_columns(joined, near_x):
    lane = iota(joined.shape, 1)
    if not near_x:
        return jnp.where(lane < 68, joined, 0.0)
    first, second = (lane >= 1) & (lane <= 30), (lane >= 33) & (lane <= 62)
    return jnp.where(first, pltpu.roll(joined, 61, 1), jnp.where(second, pltpu.roll(joined, 63, 1), 0.0))


def own_tile(slab_ref, grid_ref, tile):
    return grid_ref[tile] if tile < 2 else slab_ref[tile - 2] if tile < SLABS else grid_ref[tile - 2]


def pack_z_kernel(slab_ref, grid_ref, xe_ref, even_ref, *odd_refs):
    here = is_even("gz")
    ends = []
    for first in (0, ROWS - 16):
        rows = pl.ds(first, 16)
        received = xe_ref[rows, :]
        extra = x_additions(*low_high(received, jnp.zeros_like(received), "gx"))
        tiles = [own_tile(slab_ref, grid_ref, t)[first : first + 16] + extra[t] for t in range(SLABS)]
        ends.append([join_columns(tiles[t], tiles[t + 2]) for t in range(2)])
        ends[-1] += [grid_ref[t, rows, :] for t in range(2, grid_ref.shape[0])]
    for tile, (lower, upper) in enumerate(zip(*ends)):
        even_ref[tile] = jnp.where(here, upper, lower)
        for odd_ref in odd_refs:
            odd_ref[tile] = jnp.where(here, lower, upper)


def x_additions(low, high):
    lower, upper = corners(low, high)
    planar = iota(low.shape, 1) < 64
    return [lower, upper, jnp.where(planar, low, 0.0), jnp.where(planar, high, 0.0)]


def keep_kernel(received_ref, kept_ref):
    kept_ref[...] = received_ref[...]


def xz_additions(xe_ref, xo_ref, diagonals, layers, tiles):
    odd = xo_ref[...] + diagonal_rows([ref[...] for ref in diagonals])
    extra = x_additions(*low_high(xe_ref[pl.ds(0, ROWS), :], odd, "gx"))
    joined = [diagonal_rows([ref[t] for ref in layers]) for t in range(2)]
    return [extra[t] + joined_columns(joined[t % 2], t >= 2) for t in range(tiles)]


def pack_y_kernel(ends, *refs):
    grid_ref, xe_ref, xo_ref, *received = refs[:-3]
    even_ref, odd_ref, sums_ref = refs[-3:]
    extra = xz_additions(xe_ref, xo_ref, received[:ends], received[ends:], 2)
    lower, upper = grid_ref[0] + extra[0], grid_ref[1] + extra[1]
    sums_ref[0], sums_ref[1] = lower, upper
    here = is_even("gy")
    even_ref[...] = jnp.where(here, upper, lower)
    odd_ref[...] = jnp.where(here, lower, upper)


def node_gradients(counts, brick, size_z, tiles, totals, total_ref, push_ref, drag_ref, apart=0):
    place = [lax.axis_index(axis) for axis in ("gx", "gy", "gz")]
    row = iota((8, LANES), 0)
    blank = jnp.zeros((8, LANES), F32)
    for at, (tile, total) in enumerate(zip(tiles, totals)):
        total_ref[at, pl.ds(0, ROWS), :] = total
        total_ref[at, pl.ds(ROWS, 16), :] = jnp.zeros((16, LANES), F32)
        lanes = pl.ds(at * LANES, LANES)
        node_x, node_y, _ = tile_nodes(tile, 8, brick)
        node_x = node_x + (place[0] * brick - 1)
        node_y = node_y + (place[1] * brick - 1)
        drags = []
        for side in range(2):
            c = [total_ref[at, pl.ds(32 * side + k, 8, stride=8), :] for k in range(CHANNELS)]
            node_z = row + (4 * side - 1) + place[2] * size_z
            inside = (node_z >= 0) & (node_z < counts[2] * size_z)
            if tile in (2, 3):
                inside = inside & (iota((8, LANES), 1) < 64)
            if tile < SLABS:
                inside = inside & (node_x >= 0) & (node_x < counts[0] * brick)
                inside = inside & (node_y >= 0) & (node_y < counts[1] * brick)
            inverse = 1.0 / jnp.maximum(c[0], 1.0)
            scale = jnp.where(inside, (1.0 - c[7]) * inverse, 0.0)
            high, low = split(jnp.concatenate([c[4 + a] * scale for a in range(3)] + [blank], axis=0))
            if apart:
                lanes = pl.ds((apart * side + at) * LANES, LANES)
            for first in (0, 64) if apart else (64 * side,):
                push_ref[pl.ds(first, 32), lanes] = high
                push_ref[pl.ds(first + 32, 32), lanes] = low
            drags.append(
                c[4] * (c[1] * inverse) + c[5] * (c[2] * inverse) + c[6] * (c[3] * inverse - gravity_step)
            )
        drag_ref[at] = jnp.where(row < 7, pltpu.roll(drags[0], 7, 0), pltpu.roll(drags[1], 3, 0))


def gather(hot, push_ref):
    return lax.dot_general(hot, push_ref[...], (((1,), (1,)), ((), ())), preferred_element_type=F32)


def early_kernel(counts, ends, size_z, *refs):
    inputs, refs = refs[:-7], refs[-7:]
    meta_ref, hot_slab_ref, hot_ref, slab_ref, grid_ref, xe_ref, xo_ref, *received = inputs
    gathered_ref, drag_slab_ref, drag_ref, masked_ref, total_ref, push_slab_ref, push_ref = refs
    brick = 4 * (grid_ref.shape[0] - 2)
    extra = xz_additions(xe_ref, xo_ref, received[:ends], received[ends:], SLABS)
    totals = [slab_ref[tile - 2] + extra[tile] for tile in (2, 3)]
    node_gradients(counts, brick, size_z, (2, 3), totals, total_ref, push_slab_ref, drag_slab_ref)
    tiles = inner_tiles(brick)[2:]
    totals = [grid_ref[t - 2] + diagonal_rows([ref[t - 2] for ref in received[ends:]]) for t in tiles]
    node_gradients(counts, brick, size_z, tiles, totals, total_ref, push_ref, drag_ref)
    gathered = gather(hot_slab_ref[...], push_slab_ref) + gather(
        hot_ref[:, pl.ds(2 * LANES, push_ref.shape[1])], push_ref
    )
    upper = meta_ref[1] == 1
    blocks = upper.shape[0]
    keep = (iota((blocks, LANES), 1) < 64) != upper
    for node in range(16):
        value = gathered[node * blocks : (node + 1) * blocks]
        gathered_ref[pl.ds(node * blocks, blocks), :] = jnp.where(keep, value, pltpu.roll(value, 64, 1))
    fill_one_hot(masked_ref, meta_ref[0], (0, 1), brick, (jnp.logical_not(upper), upper))


def collect_kernel(counts, *refs):
    inputs, refs = refs[:-10], refs[-10:]
    meta_ref, shape_ref, masked_ref, take_spread_ref, top_ref, gathered_ref, drag_slab_ref, drag_ref = inputs[:8]
    near_ref, ye_ref, yo_ref = inputs[8:]
    gvel_ref, gaff_ref, gvol_ref, gdrag_ref = refs[:4]
    total_ref, push_ref, drag_ends_ref, take_ref, pulled_ref, flat_ref = refs[4:]
    blocks = gvol_ref.shape[0]
    brick, size_z = gdrag_ref.shape[0], gdrag_ref.shape[1]
    saved = [shape_ref[pl.ds(k * blocks, blocks), :] for k in range(12)]
    weight, frac = [saved[3 * k : 3 * k + 3] for k in range(3)], saved[9:]

    low, high = low_high(ye_ref[...], yo_ref[...], "gy")
    totals = [near_ref[0] + low, near_ref[1] + high]
    node_gradients(counts, brick, size_z, (0, 1), totals, total_ref, push_ref, drag_ends_ref, 2)
    gathered = gathered_ref[...] + gather(masked_ref[...], push_ref)

    edges = [drag_ends_ref[t] for t in range(2)]
    depth = iota((size_z, brick), 0) + lax.axis_index("gz") * size_z
    lane = iota((size_z, LANES), 1)
    for x in range(brick):
        if x == 0:
            plane = pltpu.roll(drag_slab_ref[0], 96, 1)
        elif x == brick - 1:
            plane = drag_slab_ref[1]
        else:
            plane = drag_ref[x // 4]
            if x % 4:
                plane = pltpu.roll(plane, LANES - 32 * (x % 4), 1)
        at = 2 * (x + 1)
        plane = jnp.where(lane == 0, edges[0][:, at + 1 : at + 2], plane)
        plane = jnp.where(lane == brick - 1, edges[1][:, at : at + 1], plane)
        gdrag_ref[x] = jnp.where(depth < top_ref[pl.ds(x, 1), :], -plane[:, :brick], 0.0)

    lane = iota((blocks, LANES), 1)
    low_half = lane < 64
    nodes = [gathered[node * blocks : (node + 1) * blocks] for node in range(16)]
    for ox in range(3):
        for oy in range(3):
            for cx in range(2):
                value = jnp.where(low_half, nodes[4 * (cx + ox) + oy], nodes[4 * (cx + ox) + oy + 1])
                take_ref[pl.ds((3 * ox + oy) * blocks, blocks), pl.ds(cx * LANES, LANES)] = value.astype(BF16)

    pulled_ref[...] = jnp.dot(take_ref[...], take_spread_ref[...], preferred_element_type=F32)

    live = meta_ref[2].astype(F32)
    planar = [[live * weight[0][ox] * weight[1][oy] for oy in range(3)] for ox in range(3)]
    trace = None
    for a in range(3):
        sums_x, sums_y, sums_z = [], [None] * 3, None
        for ox in range(3):
            column = None
            for oy in range(3):
                rows = pl.ds((3 * ox + oy) * blocks, blocks)
                g = [pulled_ref[rows, pl.ds((3 * a + oz) * LANES, LANES)] for oz in range(3)]
                below, above = weight[2][0] * g[0], weight[2][2] * g[2]
                sum_z = planar[ox][oy] * (weight[2][1] * g[1] + (below + above))
                slope = planar[ox][oy] * (above - below)
                column = sum_z if column is None else column + sum_z
                sums_y[oy] = sum_z if sums_y[oy] is None else sums_y[oy] + sum_z
                sums_z = slope if sums_z is None else sums_z + slope
            sums_x.append(column)
        whole = sums_x[0] + sums_x[1] + sums_x[2]
        moments = [sums_x[2] - sums_x[0], sums_y[2] - sums_y[0], sums_z]
        flat_ref[pl.ds(a * blocks, blocks), :] = whole
        for b in range(3):
            value = moments[b] - frac[b] * whole
            flat_ref[pl.ds((3 + 3 * a + b) * blocks, blocks), :] = value
            if a == b:
                trace = value if trace is None else trace + value
    gvol_ref[...] = -stiffness * trace
    from_rows(gvel_ref, flat_ref, 0, blocks)
    from_rows(gaff_ref, flat_ref, 3, blocks)


def paired(index, count, first):
    partner = index + 1 if (index - first) % 2 == 0 else index - 1
    return partner if 0 <= partner < count else None


def exchange(array, counts, pair):
    names = ("gx", "gy", "gz")
    links = []
    for x in range(counts[0]):
        for y in range(counts[1]):
            for z in range(counts[2]):
                target = pair(x, y, z)
                if None not in target:
                    links.append(((x * counts[1] + y) * counts[2] + z, (target[0] * counts[1] + target[1]) * counts[2] + target[2]))
    return lax.ppermute(array, names, links) if links else jnp.zeros_like(array)


def shards(
    offsets, velocity, affine, volume, cot_velocity, cot_affine, block_cells, fill_counts, baffle_top, drag
):
    brick, _, size_z = drag.shape
    blocks = block_cells.shape[0]
    counts = tuple(lax.axis_size(axis) for axis in ("gx", "gy", "gz"))
    interior = brick // 4
    vmem = pl.BlockSpec(memory_space=pltpu.VMEM)

    def f32(*shape):
        return jax.ShapeDtypeStruct(shape, F32)

    def bf16(*shape):
        return jax.ShapeDtypeStruct(shape, BF16)

    def call(kernel, name, out_shape, operands, scratch=(), megabytes=4, flops=0):
        return pl.pallas_call(
            kernel,
            out_shape=out_shape,
            in_specs=[vmem] * len(operands),
            out_specs=(vmem,) * len(out_shape),
            scratch_shapes=scratch,
            compiler_params=pltpu.CompilerParams(vmem_limit_bytes=megabytes * 1024 * 1024),
            cost_estimate=pl.CostEstimate(flops=flops, bytes_accessed=1024, transcendentals=0),
            name=name,
        )(*operands)

    operands = (
        block_cells.reshape(1, blocks), fill_counts.reshape(1, 1), offsets, velocity, affine, volume.reshape(blocks, LANES), cot_velocity, cot_affine,
        baffle_top, drag.transpose(0, 2, 1),
    )
    slab = f32(ROWS, LANES)
    ends = 2 if counts[2] > 2 else 1
    spread, take = call(
        spread_kernel, "spread", (bf16(21 * LANES, 2 * LANES), bf16(2 * LANES, 9 * LANES)), (), flops=20_000_000_000
    )
    edge, send_xe, send_xo, send_xz, meta, shape, window, hot_edge = call(
        deposit_kernel,
        "deposit",
        (
            f32(2, ROWS, LANES), f32(256, LANES), slab, f32(ends, 16, LANES),
            jax.ShapeDtypeStruct((3, blocks, LANES), jnp.int32), f32(12 * blocks, LANES),
            bf16(16 * blocks, 2 * LANES), bf16(16 * blocks, 2 * LANES),
        ),
        operands + (spread,),
        scratch=[
            pltpu.VMEM((27 * blocks, LANES), F32),
            pltpu.VMEM((18 * blocks, 21 * LANES), BF16),
            pltpu.VMEM((18 * blocks, 2 * LANES), F32),
            pltpu.VMEM((2 * LANES, 2 * LANES), F32),
        ],
        megabytes=16,
    )

    def even_x(x):
        return paired(x, counts[0], 0)

    def odd_x(x, y, z):
        partner = paired(x, counts[0], 1)
        return (x, y, paired(z, counts[2], 0)) if partner is None else (partner, y, z)

    def odd_xz(x, y, z, first):
        partner = paired(x, counts[0], 1)
        return x if partner is None else partner, y, paired(z, counts[2], first)

    def odd_y(x, y, z):
        partner = paired(y, counts[1], 1)
        return (even_x(x), y, z) if partner is None else (x, partner, z)

    xe = exchange(send_xe, counts, lambda x, y, z: (even_x(x), y, z))
    xo = exchange(send_xo, counts, odd_x)
    xz = [
        exchange(send_xz[first], counts, lambda x, y, z: odd_xz(x, y, z, first))
        for first in range(ends)
    ]
    grid, hot = call(
        interior_kernel,
        "interior",
        (f32(2 + interior, ROWS, LANES), bf16(16 * blocks, (2 + interior) * LANES)),
        (window, meta, *operands[-2:]),
        scratch=[pltpu.VMEM((2 * LANES, (2 + interior) * LANES), F32)],
        megabytes=8,
        flops=1_000_000_000,
    )
    (xo,) = call(keep_kernel, "keep", (slab,), (xo,), flops=700_000_000)
    send_z = call(pack_z_kernel, "pack_z", (f32(2 + interior, 16, LANES),) * ends, (edge, grid, xe))
    layers = [
        exchange(array, counts, lambda x, y, z: (x, y, paired(z, counts[2], first)))
        for first, array in enumerate(send_z)
    ]
    send_ye, send_yo, near_y = call(
        functools.partial(pack_y_kernel, ends), "pack_y", (slab, slab, f32(2, ROWS, LANES)), (grid, xe, xo, *xz, *layers)
    )
    yo = exchange(send_yo, counts, odd_y)
    ye = exchange(send_ye, counts, lambda x, y, z: (x, paired(y, counts[1], 0), z))
    gathered, drag_slab, drag_rows, masked = call(
        functools.partial(early_kernel, counts, ends, size_z),
        "early",
        (
            f32(16 * blocks, LANES), f32(2, size_z, LANES), f32(interior, size_z, LANES),
            bf16(16 * blocks, 4 * LANES),
        ),
        (meta, hot_edge, hot, edge, grid, xe, xo, *xz, *layers),
        scratch=[
            pltpu.VMEM((interior, ROWS + 16, LANES), F32),
            pltpu.VMEM((LANES, 2 * LANES), BF16),
            pltpu.VMEM((LANES, interior * LANES), BF16),
        ],
        megabytes=8,
        flops=1_000_000_000,
    )
    grad_velocity, grad_affine, grad_volume, grad_drag = call(
        functools.partial(collect_kernel, counts),
        "collect",
        (f32(3, blocks * LANES), f32(9, blocks * LANES), f32(blocks, LANES), f32(brick, size_z, brick)),
        (meta, shape, masked, take, baffle_top, gathered, drag_slab, drag_rows, near_y, ye, yo),
        scratch=[
            pltpu.VMEM((2, ROWS + 16, LANES), F32),
            pltpu.VMEM((LANES, 4 * LANES), BF16),
            pltpu.VMEM((2, size_z, LANES), F32),
            pltpu.VMEM((9 * blocks, 2 * LANES), BF16),
            pltpu.VMEM((9 * blocks, 9 * LANES), F32),
            pltpu.VMEM((12 * blocks, LANES), F32),
        ],
        megabytes=12,
    )
    return grad_velocity, grad_affine, grad_volume.reshape(-1), grad_drag.transpose(0, 2, 1)


def solution(mesh):
    everywhere = ("gx", "gy", "gz")
    rows, flat = P(None, everywhere), P(everywhere)
    in_specs = (rows, rows, rows, flat, rows, rows, flat, flat, P("gx", "gy"), P("gx", "gy", "gz"))
    out_specs = (rows, rows, flat, P("gx", "gy", "gz"))
    return jax.shard_map(shards, mesh=mesh, in_specs=in_specs, out_specs=out_specs, check_vma=False)
```

```python
import functools

import jax
import jax.numpy as jnp
from jax import lax
from jax.experimental import pallas as pl
from jax.experimental.pallas import tpu as pltpu
from jax.sharding import PartitionSpec as P

stiffness = 2.0
gravity_step = 0.3

LANES = 128
SLABS = 4
ZROWS = 10
CHANNELS = 8
ROWS = ZROWS * CHANNELS
F32 = jnp.float32
BF16 = jnp.bfloat16


def iota(shape, dim):
    return lax.broadcasted_iota(jnp.int32, shape, dim)


def tile_nodes(tile, rows, brick):
    lane = iota((rows, LANES), 1)
    if tile < 2:
        x, y = lane >> 1, (lane & 1) + tile * brick
        valid = lane < 2 * (brick + 2)
    elif tile < SLABS:
        plane, corner = lane < 64, lane - 64
        x = jnp.where(plane, lane >> 5, (corner & 3) >> 1) + (tile - 2) * brick
        y = jnp.where(plane, (lane & 31) + 1, (corner >> 2) * brick + (corner & 1))
        valid = jnp.where(plane, ((y >= 2) & (y < brick)).astype(jnp.int32), (corner < 8).astype(jnp.int32)) == 1
    else:
        x = (lane >> 5) + 4 * (tile - SLABS) + 1
        y = (lane & 31) + 1
        valid = (x >= 2) & (x < brick) & (y >= 2) & (y < brick)
    return x, y, valid


def tile_code(tile, rows, brick):
    x, y, valid = tile_nodes(tile, rows, brick)
    return jnp.where(valid, x * 64 + y, -1)


def block_columns(cells_ref):
    blocks = cells_ref.shape[1]
    same = iota((blocks, blocks), 0) == iota((blocks, blocks), 1)
    column = jnp.sum(jnp.where(same, cells_ref[...].astype(F32), 0.0), axis=1, keepdims=True)
    cells = jnp.broadcast_to(column, (blocks, LANES)).astype(jnp.int32)
    return (cells >> 5) * 128 + ((cells >> 1) & 15) * 2, cells & 1


def fill_one_hot(hot_ref, code, tiles, brick, masks=(None,)):
    blocks = code.shape[0]
    for at, (mask, tile) in enumerate((mask, tile) for mask in masks for tile in tiles):
        lane_code = tile_code(tile, blocks, brick) - code
        if mask is not None:
            lane_code = jnp.where(mask, lane_code, -1)
        for node in range(16):
            hit = lane_code == (node // 4) * 64 + node % 4
            hot_ref[pl.ds(node * blocks, blocks), pl.ds(at * LANES, LANES)] = jnp.where(hit, 1.0, 0.0).astype(BF16)


def deposit_windows(grid_ref, window_ref, hot_ref, all_ref):
    all_ref[...] = lax.dot_general(
        window_ref[...], hot_ref[...], (((0,), (0,)), ((), ())), preferred_element_type=F32
    )
    for z in range(ZROWS):
        piece = None
        for tz in range(2):
            wz = z - 4 * tz
            if 0 <= wz < 6:
                row = 64 * tz + 8 * wz
                part = all_ref[pl.ds(row, 8), :] + all_ref[pl.ds(128 + row, 8), :]
                piece = part if piece is None else piece + part
        for tile in range(grid_ref.shape[0]):
            grid_ref[tile, pl.ds(8 * z, 8), :] = piece[:, tile * LANES : (tile + 1) * LANES]


def inner_tiles(brick):
    return (0, 1) + tuple(range(SLABS, SLABS + brick // 4))


def spline(frac):
    return [0.5 * (0.5 - frac) ** 2, 0.75 - frac * frac, 0.5 * (0.5 + frac) ** 2]


def split(value):
    high = value.astype(BF16)
    return high, (value - high.astype(F32)).astype(BF16)


def is_even(axis):
    return lax.rem(lax.axis_index(axis), 2) == 0


def low_high(even, odd, axis):
    here = is_even(axis)
    place = lax.axis_index(axis)
    low, high = jnp.where(here, odd, even), jnp.where(here, even, odd)
    return jnp.where(place > 0, low, 0.0), jnp.where(place < lax.axis_size(axis) - 1, high, 0.0)


def diagonal_rows(ends):
    even = ends[0]
    low, high = low_high(even, ends[1] if len(ends) > 1 else jnp.zeros_like(even), "gz")
    return jnp.concatenate([low, jnp.zeros((ROWS - 32, LANES), F32), high], axis=0)


def pack_layers(tiles):
    row = iota((8, LANES), 0)
    firsts = [jnp.where(row == 7, pltpu.roll(mine, 7, 0), theirs) for theirs, mine in tiles]
    pairs = [
        jnp.where(row < 4, pltpu.roll(odd[1], 4, 0), even[1]) for even, odd in zip(tiles[0::2], tiles[1::2])
    ]
    return firsts + pairs


def layer_rows(refs, tile):
    row = iota((8, LANES), 0)
    planes = []
    for ref in refs:
        first, pair = ref[tile], ref[2 * ref.shape[0] // 3 + tile // 2]
        half = pltpu.roll(pair, 4, 0) if tile % 2 else pair
        own = jnp.where(row < 7, first, 0.0)
        halo = jnp.where(row >= 4, half, jnp.where(row == 0, pltpu.roll(first, 1, 0), 0.0))
        planes.append(jnp.concatenate([own, halo], axis=0))
    low, high = low_high(planes[0], planes[1] if len(planes) > 1 else jnp.zeros_like(planes[0]), "gz")
    return jnp.concatenate([low[8:], low[:8], jnp.zeros((ROWS - 32, LANES), F32), high], axis=0)


def to_rows(flat_ref, first, array_ref, blocks):
    channels = array_ref.shape[0]
    if channels > 8:
        tiles = jnp.stack([array_ref[pl.ds(0, 8), pl.ds(b * LANES, LANES)] for b in range(blocks)])
        flat_ref[pl.ds(first * blocks, 8 * blocks), :] = jnp.swapaxes(tiles, 0, 1).reshape(8 * blocks, LANES)
        for b in range(blocks):
            flat_ref[pl.ds((first + 8) * blocks + b, 1), :] = array_ref[pl.ds(8, 1), pl.ds(b * LANES, LANES)]
        return
    for b in range(blocks):
        flat_ref[pl.ds(first * blocks + b, channels, stride=blocks), :] = array_ref[:, pl.ds(b * LANES, LANES)]


def from_rows(array_ref, flat_ref, first, blocks):
    channels = array_ref.shape[0]
    if channels > 8:
        tiles = flat_ref[pl.ds(first * blocks, 8 * blocks), :].reshape(8, blocks, LANES)
        tiles = jnp.swapaxes(tiles, 0, 1)
        for b in range(blocks):
            array_ref[pl.ds(0, 8), pl.ds(b * LANES, LANES)] = tiles[b]
            array_ref[pl.ds(8, 1), pl.ds(b * LANES, LANES)] = flat_ref[pl.ds((first + 8) * blocks + b, 1), :]
        return
    for b in range(blocks):
        array_ref[:, pl.ds(b * LANES, LANES)] = flat_ref[pl.ds(first * blocks + b, channels, stride=blocks), :]


def corners(low, high):
    lane = iota(low.shape, 1)
    first, last = lane < 4, (lane >= 64) & (lane < 68)
    zero = jnp.zeros_like(low)
    lower = jnp.where(first, pltpu.roll(low, 64, 1), jnp.where(last, high, zero))
    upper = jnp.where(first, pltpu.roll(low, 60, 1), jnp.where(last, pltpu.roll(high, 124, 1), zero))
    return lower, upper


def spread_kernel(spread_ref, take_ref):
    particle = iota((LANES, 2 * LANES), 0)
    shift = iota((LANES, 2 * LANES), 1) - ((particle >> 5) * 64 + ((particle >> 3) & 3) * 8)
    for c in range(7):
        for oz in range(3):
            hit = shift == oz * 8 + c
            spread_ref[pl.ds((3 * c + oz) * LANES, LANES), :] = jnp.where(hit, 1.0, 0.0).astype(BF16)
    key = iota((2 * LANES, LANES), 0)
    particle = iota((2 * LANES, LANES), 1)
    shift = jnp.where((key >> 6) == (particle >> 5), (key & 31) - ((particle >> 3) & 3), -64)
    for a in range(3):
        for oz in range(3):
            hit = shift == 8 * a + oz
            take_ref[:, pl.ds((3 * a + oz) * LANES, LANES)] = jnp.where(hit, 1.0, 0.0).astype(BF16)


def deposit_kernel(*refs):
    cells_ref, count_ref, pos_ref, vel_ref, aff_ref, vol_ref, cvel_ref, caff_ref, top_ref, drag_ref = refs[:10]
    spread_ref, refs = refs[10], refs[11:]
    grid_ref, even_ref, odd_ref, diagonal_ref, meta_ref, shape_ref, window_ref, hot_ref = refs[:8]
    flat_ref, terms_ref, sums_ref, all_ref = refs[8:]
    blocks = vol_ref.shape[0]
    brick = drag_ref.shape[0]
    size_z = drag_ref.shape[1]
    code, upper_tile = block_columns(cells_ref)
    live_rows = iota((blocks, LANES), 0) < count_ref[...]
    meta_ref[0], meta_ref[1], meta_ref[2] = code, upper_tile, live_rows.astype(jnp.int32)
    fill_one_hot(hot_ref, code, (2, 3), brick)
    for first, ref in ((0, pos_ref), (3, vel_ref), (6, aff_ref), (15, cvel_ref), (18, caff_ref)):
        to_rows(flat_ref, first, ref, blocks)

    def channel(c):
        return flat_ref[pl.ds(c * blocks, blocks), :]

    live = live_rows.astype(F32)
    frac = [channel(k) for k in range(3)]
    weight = [spline(f) for f in frac]
    for k, value in enumerate(weight[0] + weight[1] + weight[2] + frac):
        shape_ref[pl.ds(k * blocks, blocks), :] = value
    stretch = stiffness * (vol_ref[...] - 1.0)
    linear, matrix = [live], [None]
    for a in range(3):
        row = [live * (channel(6 + 3 * a + b) - (stretch if a == b else 0.0)) for b in range(3)]
        matrix.append(row)
        linear.append(live * channel(3 + a) - sum(row[b] * frac[b] for b in range(3)))
    for a in range(3):
        row = [(4.0 * live) * channel(18 + 3 * a + b) for b in range(3)]
        matrix.append(row)
        linear.append(live * channel(15 + a) - sum(row[b] * frac[b] for b in range(3)))

    def put(row, slot, value):
        high, low = split(value)
        lanes = pl.ds(slot * LANES, LANES)
        terms_ref[pl.ds(row * blocks, blocks), lanes] = high
        terms_ref[pl.ds((9 + row) * blocks, blocks), lanes] = low

    for ox in range(3):
        for oy in range(3):
            planar = weight[0][ox] * weight[1][oy]
            weights = [planar * weight[2][oz] for oz in range(3)]
            for c in range(7):
                base = linear[c]
                if c:
                    if ox != 1:
                        base = base + matrix[c][0] if ox else base - matrix[c][0]
                    if oy != 1:
                        base = base + matrix[c][1] if oy else base - matrix[c][1]
                for oz in range(3):
                    value = base
                    if c and oz != 1:
                        value = base + matrix[c][2] if oz else base - matrix[c][2]
                    put(3 * ox + oy, 3 * c + oz, weights[oz] * value)

    sums_ref[...] = jnp.dot(terms_ref[...], spread_ref[...], preferred_element_type=F32)

    lane = iota((blocks, LANES), 1)
    low_half = lane < 64
    own_half = low_half == (upper_tile == 0)

    def partial(wx, oy):
        total = None
        for cx in range(2):
            ox = wx - cx
            if 0 <= ox < 3:
                lanes = pl.ds(cx * LANES, LANES)
                row = 3 * ox + oy
                piece = sums_ref[pl.ds(row * blocks, blocks), lanes] + sums_ref[pl.ds((9 + row) * blocks, blocks), lanes]
                total = piece if total is None else total + piece
        return total

    for wx in range(4):
        columns = [partial(wx, oy) for oy in range(3)]
        zero = jnp.zeros_like(columns[0])
        for wy in range(4):
            both = jnp.where(low_half, columns[wy] if wy < 3 else zero, columns[wy - 1] if wy else zero)
            node = jnp.where(own_half, both + pltpu.roll(both, 64, 1), 0.0)
            high, low = split(node)
            rows = pl.ds((4 * wx + wy) * blocks, blocks)
            window_ref[rows, pl.ds(0, LANES)] = high
            window_ref[rows, pl.ds(LANES, LANES)] = low

    deposit_windows(grid_ref, window_ref, hot_ref, all_ref)

    depth = iota((size_z, brick), 0) + lax.axis_index("gz") * size_z
    lane = iota((size_z, LANES), 1)
    blank = jnp.zeros((size_z, 32), F32)
    for side, x in enumerate((0, brick - 1)):
        layer = jnp.where(depth < top_ref[pl.ds(x, 1), :], drag_ref[x], 0.0)
        plane = jnp.concatenate([blank, layer, blank, blank] if side == 0 else [layer, blank, blank, blank], axis=1)
        plane = jnp.where(lane == 67 - 2 * side, layer[:, 0:1], plane)
        plane = jnp.where(lane == 70 - 2 * side, layer[:, brick - 1 : brick], plane)
        grid_ref[side, pl.ds(8 + 7, size_z, stride=8), :] = plane

    low, high = grid_ref[0], grid_ref[1]
    here = is_even("gx")
    even_ref[pl.ds(0, ROWS), :] = jnp.where(here, high, low)
    even_ref[pl.ds(ROWS, even_ref.shape[0] - ROWS), :] = jnp.zeros((even_ref.shape[0] - ROWS, LANES), F32)
    odd_ref[...] = jnp.where(here, low, high)
    here = is_even("gz")
    lower, upper = odd_ref[pl.ds(0, 16), :], odd_ref[pl.ds(ROWS - 16, 16), :]
    diagonal_ref[0] = jnp.where(here, upper, lower)
    if diagonal_ref.shape[0] > 1:
        diagonal_ref[1] = jnp.where(here, lower, upper)


def interior_kernel(window_ref, meta_ref, top_ref, drag_ref, grid_ref, hot_ref, all_ref):
    brick, size_z, _ = drag_ref.shape
    fill_one_hot(hot_ref, meta_ref[0], inner_tiles(brick), brick)
    deposit_windows(grid_ref, window_ref, hot_ref, all_ref)
    depth = iota((size_z, brick), 0) + lax.axis_index("gz") * size_z
    lane = iota((size_z, LANES), 1)
    ends = [jnp.zeros((size_z, LANES), F32)] * 2
    layers = []
    for x in range(brick):
        layer = jnp.where(depth < top_ref[pl.ds(x, 1), :], drag_ref[x], 0.0)
        layers.append(layer)
        ends[0] = jnp.where(lane == 2 * (x + 1) + 1, layer[:, 0:1], ends[0])
        ends[1] = jnp.where(lane == 2 * (x + 1), layer[:, brick - 1 : brick], ends[1])
    planes = ends + [jnp.concatenate(layers[4 * t : 4 * t + 4], axis=1) for t in range(brick // 4)]
    for at, plane in enumerate(planes):
        grid_ref[at, pl.ds(8 + 7, size_z, stride=8), :] = plane


def join_columns(near_y, near_x):
    lane = iota(near_y.shape, 1)
    near_x = jnp.where(lane < 98, pltpu.roll(near_x, 67, 1), pltpu.roll(near_x, 65, 1))
    return jnp.where(lane < 68, near_y, near_x)


def joined_columns(joined, near_x):
    lane = iota(joined.shape, 1)
    if not near_x:
        return jnp.where(lane < 68, joined, 0.0)
    first, second = (lane >= 1) & (lane <= 30), (lane >= 33) & (lane <= 62)
    return jnp.where(first, pltpu.roll(joined, 61, 1), jnp.where(second, pltpu.roll(joined, 63, 1), 0.0))


def own_tile(slab_ref, grid_ref, tile):
    return grid_ref[tile] if tile < 2 else slab_ref[tile - 2] if tile < SLABS else grid_ref[tile - 2]


def pack_z_kernel(slab_ref, grid_ref, xe_ref, even_ref, *odd_refs):
    here = is_even("gz")
    ends = []
    for first in (0, ROWS - 16):
        rows = pl.ds(first, 16)
        received = xe_ref[rows, :]
        extra = x_additions(*low_high(received, jnp.zeros_like(received), "gx"))
        tiles = [own_tile(slab_ref, grid_ref, t)[first : first + 16] + extra[t] for t in range(SLABS)]
        ends.append([join_columns(tiles[t], tiles[t + 2]) for t in range(2)])
        ends[-1] += [grid_ref[t, rows, :] for t in range(2, grid_ref.shape[0])]
    for up, refs in ((here, (even_ref,)), (jnp.logical_not(here), odd_refs)):
        for ref in refs:
            tiles = [
                (jnp.where(up, upper[8:], lower[:8]), jnp.where(up, upper[:8], lower[8:]))
                for lower, upper in zip(*ends)
            ]
            for at, rows in enumerate(pack_layers(tiles)):
                ref[at] = rows


def x_additions(low, high):
    lower, upper = corners(low, high)
    planar = iota(low.shape, 1) < 64
    return [lower, upper, jnp.where(planar, low, 0.0), jnp.where(planar, high, 0.0)]


def keep_kernel(received_ref, kept_ref):
    kept_ref[...] = received_ref[...]


def xz_additions(xe_ref, xo_ref, diagonals, layers, tiles):
    odd = xo_ref[...] + diagonal_rows([ref[...] for ref in diagonals])
    extra = x_additions(*low_high(xe_ref[pl.ds(0, ROWS), :], odd, "gx"))
    joined = [layer_rows(layers, t) for t in range(2)]
    return [extra[t] + joined_columns(joined[t % 2], t >= 2) for t in range(tiles)]


def pack_y_kernel(ends, *refs):
    grid_ref, xe_ref, xo_ref, *received = refs[:-3]
    even_ref, odd_ref, sums_ref = refs[-3:]
    extra = xz_additions(xe_ref, xo_ref, received[:ends], received[ends:], 2)
    lower, upper = grid_ref[0] + extra[0], grid_ref[1] + extra[1]
    sums_ref[0], sums_ref[1] = lower, upper
    here = is_even("gy")
    even_ref[...] = jnp.where(here, upper, lower)
    odd_ref[...] = jnp.where(here, lower, upper)


def node_gradients(counts, brick, size_z, tiles, totals, total_ref, push_ref, drag_ref, apart=0):
    place = [lax.axis_index(axis) for axis in ("gx", "gy", "gz")]
    row = iota((8, LANES), 0)
    blank = jnp.zeros((8, LANES), F32)
    for at, (tile, total) in enumerate(zip(tiles, totals)):
        total_ref[at, pl.ds(0, ROWS), :] = total
        total_ref[at, pl.ds(ROWS, 16), :] = jnp.zeros((16, LANES), F32)
        lanes = pl.ds(at * LANES, LANES)
        node_x, node_y, _ = tile_nodes(tile, 8, brick)
        node_x = node_x + (place[0] * brick - 1)
        node_y = node_y + (place[1] * brick - 1)
        drags = []
        for side in range(2):
            c = [total_ref[at, pl.ds(32 * side + k, 8, stride=8), :] for k in range(CHANNELS)]
            node_z = row + (4 * side - 1) + place[2] * size_z
            inside = (node_z >= 0) & (node_z < counts[2] * size_z)
            if tile in (2, 3):
                inside = inside & (iota((8, LANES), 1) < 64)
            if tile < SLABS:
                inside = inside & (node_x >= 0) & (node_x < counts[0] * brick)
                inside = inside & (node_y >= 0) & (node_y < counts[1] * brick)
            inverse = 1.0 / jnp.maximum(c[0], 1.0)
            scale = jnp.where(inside, (1.0 - c[7]) * inverse, 0.0)
            high, low = split(jnp.concatenate([c[4 + a] * scale for a in range(3)] + [blank], axis=0))
            if apart:
                lanes = pl.ds((apart * side + at) * LANES, LANES)
            for first in (0, 64) if apart else (64 * side,):
                push_ref[pl.ds(first, 32), lanes] = high
                push_ref[pl.ds(first + 32, 32), lanes] = low
            drags.append(
                c[4] * (c[1] * inverse) + c[5] * (c[2] * inverse) + c[6] * (c[3] * inverse - gravity_step)
            )
        drag_ref[at] = jnp.where(row < 7, pltpu.roll(drags[0], 7, 0), pltpu.roll(drags[1], 3, 0))


def gather(hot, push_ref):
    return lax.dot_general(hot, push_ref[...], (((1,), (1,)), ((), ())), preferred_element_type=F32)


def early_kernel(counts, ends, size_z, *refs):
    inputs, refs = refs[:-7], refs[-7:]
    meta_ref, hot_slab_ref, hot_ref, slab_ref, grid_ref, xe_ref, xo_ref, *received = inputs
    gathered_ref, drag_slab_ref, drag_ref, masked_ref, total_ref, push_slab_ref, push_ref = refs
    brick = 4 * (grid_ref.shape[0] - 2)
    extra = xz_additions(xe_ref, xo_ref, received[:ends], received[ends:], SLABS)
    totals = [slab_ref[tile - 2] + extra[tile] for tile in (2, 3)]
    node_gradients(counts, brick, size_z, (2, 3), totals, total_ref, push_slab_ref, drag_slab_ref)
    tiles = inner_tiles(brick)[2:]
    totals = [grid_ref[t - 2] + layer_rows(received[ends:], t - 2) for t in tiles]
    node_gradients(counts, brick, size_z, tiles, totals, total_ref, push_ref, drag_ref)
    gathered = gather(hot_slab_ref[...], push_slab_ref) + gather(
        hot_ref[:, pl.ds(2 * LANES, push_ref.shape[1])], push_ref
    )
    upper = meta_ref[1] == 1
    blocks = upper.shape[0]
    keep = (iota((blocks, LANES), 1) < 64) != upper
    for node in range(16):
        value = gathered[node * blocks : (node + 1) * blocks]
        gathered_ref[pl.ds(node * blocks, blocks), :] = jnp.where(keep, value, pltpu.roll(value, 64, 1))
    fill_one_hot(masked_ref, meta_ref[0], (0, 1), brick, (jnp.logical_not(upper), upper))


def collect_kernel(counts, *refs):
    inputs, refs = refs[:-10], refs[-10:]
    meta_ref, shape_ref, masked_ref, take_spread_ref, top_ref, gathered_ref, drag_slab_ref, drag_ref = inputs[:8]
    near_ref, ye_ref, yo_ref = inputs[8:]
    gvel_ref, gaff_ref, gvol_ref, gdrag_ref = refs[:4]
    total_ref, push_ref, drag_ends_ref, take_ref, pulled_ref, flat_ref = refs[4:]
    blocks = gvol_ref.shape[0]
    brick, size_z = gdrag_ref.shape[0], gdrag_ref.shape[1]
    saved = [shape_ref[pl.ds(k * blocks, blocks), :] for k in range(12)]
    weight, frac = [saved[3 * k : 3 * k + 3] for k in range(3)], saved[9:]

    low, high = low_high(ye_ref[...], yo_ref[...], "gy")
    totals = [near_ref[0] + low, near_ref[1] + high]
    node_gradients(counts, brick, size_z, (0, 1), totals, total_ref, push_ref, drag_ends_ref, 2)
    gathered = gathered_ref[...] + gather(masked_ref[...], push_ref)

    edges = [drag_ends_ref[t] for t in range(2)]
    depth = iota((size_z, brick), 0) + lax.axis_index("gz") * size_z
    lane = iota((size_z, LANES), 1)
    for x in range(brick):
        if x == 0:
            plane = pltpu.roll(drag_slab_ref[0], 96, 1)
        elif x == brick - 1:
            plane = drag_slab_ref[1]
        else:
            plane = drag_ref[x // 4]
            if x % 4:
                plane = pltpu.roll(plane, LANES - 32 * (x % 4), 1)
        at = 2 * (x + 1)
        plane = jnp.where(lane == 0, edges[0][:, at + 1 : at + 2], plane)
        plane = jnp.where(lane == brick - 1, edges[1][:, at : at + 1], plane)
        gdrag_ref[x] = jnp.where(depth < top_ref[pl.ds(x, 1), :], -plane[:, :brick], 0.0)

    lane = iota((blocks, LANES), 1)
    low_half = lane < 64
    nodes = [gathered[node * blocks : (node + 1) * blocks] for node in range(16)]
    for ox in range(3):
        for oy in range(3):
            for cx in range(2):
                value = jnp.where(low_half, nodes[4 * (cx + ox) + oy], nodes[4 * (cx + ox) + oy + 1])
                take_ref[pl.ds((3 * ox + oy) * blocks, blocks), pl.ds(cx * LANES, LANES)] = value.astype(BF16)

    pulled_ref[...] = jnp.dot(take_ref[...], take_spread_ref[...], preferred_element_type=F32)

    live = meta_ref[2].astype(F32)
    planar = [[live * weight[0][ox] * weight[1][oy] for oy in range(3)] for ox in range(3)]
    trace = None
    for a in range(3):
        sums_x, sums_y, sums_z = [], [None] * 3, None
        for ox in range(3):
            column = None
            for oy in range(3):
                rows = pl.ds((3 * ox + oy) * blocks, blocks)
                g = [pulled_ref[rows, pl.ds((3 * a + oz) * LANES, LANES)] for oz in range(3)]
                below, above = weight[2][0] * g[0], weight[2][2] * g[2]
                sum_z = planar[ox][oy] * (weight[2][1] * g[1] + (below + above))
                slope = planar[ox][oy] * (above - below)
                column = sum_z if column is None else column + sum_z
                sums_y[oy] = sum_z if sums_y[oy] is None else sums_y[oy] + sum_z
                sums_z = slope if sums_z is None else sums_z + slope
            sums_x.append(column)
        whole = sums_x[0] + sums_x[1] + sums_x[2]
        moments = [sums_x[2] - sums_x[0], sums_y[2] - sums_y[0], sums_z]
        flat_ref[pl.ds(a * blocks, blocks), :] = whole
        for b in range(3):
            value = moments[b] - frac[b] * whole
            flat_ref[pl.ds((3 + 3 * a + b) * blocks, blocks), :] = value
            if a == b:
                trace = value if trace is None else trace + value
    gvol_ref[...] = -stiffness * trace
    from_rows(gvel_ref, flat_ref, 0, blocks)
    from_rows(gaff_ref, flat_ref, 3, blocks)


def paired(index, count, first):
    partner = index + 1 if (index - first) % 2 == 0 else index - 1
    return partner if 0 <= partner < count else None


def exchange(array, counts, pair):
    names = ("gx", "gy", "gz")
    links = []
    for x in range(counts[0]):
        for y in range(counts[1]):
            for z in range(counts[2]):
                target = pair(x, y, z)
                if None not in target:
                    links.append(((x * counts[1] + y) * counts[2] + z, (target[0] * counts[1] + target[1]) * counts[2] + target[2]))
    return lax.ppermute(array, names, links) if links else jnp.zeros_like(array)


def shards(
    offsets, velocity, affine, volume, cot_velocity, cot_affine, block_cells, fill_counts, baffle_top, drag
):
    brick, _, size_z = drag.shape
    blocks = block_cells.shape[0]
    counts = tuple(lax.axis_size(axis) for axis in ("gx", "gy", "gz"))
    interior = brick // 4
    vmem = pl.BlockSpec(memory_space=pltpu.VMEM)

    def f32(*shape):
        return jax.ShapeDtypeStruct(shape, F32)

    def bf16(*shape):
        return jax.ShapeDtypeStruct(shape, BF16)

    def call(kernel, name, out_shape, operands, scratch=(), megabytes=4, flops=0):
        return pl.pallas_call(
            kernel,
            out_shape=out_shape,
            in_specs=[vmem] * len(operands),
            out_specs=(vmem,) * len(out_shape),
            scratch_shapes=scratch,
            compiler_params=pltpu.CompilerParams(vmem_limit_bytes=megabytes * 1024 * 1024),
            cost_estimate=pl.CostEstimate(flops=flops, bytes_accessed=1024, transcendentals=0),
            name=name,
        )(*operands)

    operands = (
        block_cells.reshape(1, blocks), fill_counts.reshape(1, 1), offsets, velocity, affine, volume.reshape(blocks, LANES), cot_velocity, cot_affine,
        baffle_top, drag.transpose(0, 2, 1),
    )
    slab = f32(ROWS, LANES)
    ends = 2 if counts[2] > 2 else 1
    spread, take = call(
        spread_kernel, "spread", (bf16(21 * LANES, 2 * LANES), bf16(2 * LANES, 9 * LANES)), (), flops=20_000_000_000
    )
    edge, send_xe, send_xo, send_xz, meta, shape, window, hot_edge = call(
        deposit_kernel,
        "deposit",
        (
            f32(2, ROWS, LANES), f32(192, LANES), slab, f32(ends, 16, LANES),
            jax.ShapeDtypeStruct((3, blocks, LANES), jnp.int32), f32(12 * blocks, LANES),
            bf16(16 * blocks, 2 * LANES), bf16(16 * blocks, 2 * LANES),
        ),
        operands + (spread,),
        scratch=[
            pltpu.VMEM((27 * blocks, LANES), F32),
            pltpu.VMEM((18 * blocks, 21 * LANES), BF16),
            pltpu.VMEM((18 * blocks, 2 * LANES), F32),
            pltpu.VMEM((2 * LANES, 2 * LANES), F32),
        ],
        megabytes=16,
    )

    def even_x(x):
        return paired(x, counts[0], 0)

    def odd_x(x, y, z):
        partner = paired(x, counts[0], 1)
        return (x, y, paired(z, counts[2], 0)) if partner is None else (partner, y, z)

    def odd_xz(x, y, z, first):
        partner = paired(x, counts[0], 1)
        return x if partner is None else partner, y, paired(z, counts[2], first)

    def odd_y(x, y, z):
        partner = paired(y, counts[1], 1)
        return (even_x(x), y, z) if partner is None else (x, partner, z)

    xe = exchange(send_xe, counts, lambda x, y, z: (even_x(x), y, z))
    xo = exchange(send_xo, counts, odd_x)
    xz = [
        exchange(send_xz[first], counts, lambda x, y, z: odd_xz(x, y, z, first))
        for first in range(ends)
    ]
    grid, hot = call(
        interior_kernel,
        "interior",
        (f32(2 + interior, ROWS, LANES), bf16(16 * blocks, (2 + interior) * LANES)),
        (window, meta, *operands[-2:]),
        scratch=[pltpu.VMEM((2 * LANES, (2 + interior) * LANES), F32)],
        megabytes=8,
        flops=1_000_000_000,
    )
    (xo,) = call(keep_kernel, "keep", (slab,), (xo,), flops=400_000_000)
    send_z = call(pack_z_kernel, "pack_z", (f32(3 * (2 + interior) // 2, 8, LANES),) * ends, (edge, grid, xe))
    layers = [
        exchange(array, counts, lambda x, y, z: (x, y, paired(z, counts[2], first)))
        for first, array in enumerate(send_z)
    ]
    send_ye, send_yo, near_y = call(
        functools.partial(pack_y_kernel, ends), "pack_y", (slab, slab, f32(2, ROWS, LANES)), (grid, xe, xo, *xz, *layers)
    )
    yo = exchange(send_yo, counts, odd_y)
    ye = exchange(send_ye, counts, lambda x, y, z: (x, paired(y, counts[1], 0), z))
    gathered, drag_slab, drag_rows, masked = call(
        functools.partial(early_kernel, counts, ends, size_z),
        "early",
        (
            f32(16 * blocks, LANES), f32(2, size_z, LANES), f32(interior, size_z, LANES),
            bf16(16 * blocks, 4 * LANES),
        ),
        (meta, hot_edge, hot, edge, grid, xe, xo, *xz, *layers),
        scratch=[
            pltpu.VMEM((interior, ROWS + 16, LANES), F32),
            pltpu.VMEM((LANES, 2 * LANES), BF16),
            pltpu.VMEM((LANES, interior * LANES), BF16),
        ],
        megabytes=8,
        flops=1_000_000_000,
    )
    grad_velocity, grad_affine, grad_volume, grad_drag = call(
        functools.partial(collect_kernel, counts),
        "collect",
        (f32(3, blocks * LANES), f32(9, blocks * LANES), f32(blocks, LANES), f32(brick, size_z, brick)),
        (meta, shape, masked, take, baffle_top, gathered, drag_slab, drag_rows, near_y, ye, yo),
        scratch=[
            pltpu.VMEM((2, ROWS + 16, LANES), F32),
            pltpu.VMEM((LANES, 4 * LANES), BF16),
            pltpu.VMEM((2, size_z, LANES), F32),
            pltpu.VMEM((9 * blocks, 2 * LANES), BF16),
            pltpu.VMEM((9 * blocks, 9 * LANES), F32),
            pltpu.VMEM((12 * blocks, LANES), F32),
        ],
        megabytes=12,
    )
    return grad_velocity, grad_affine, grad_volume.reshape(-1), grad_drag.transpose(0, 2, 1)


def solution(mesh):
    everywhere = ("gx", "gy", "gz")
    rows, flat = P(None, everywhere), P(everywhere)
    in_specs = (rows, rows, rows, flat, rows, rows, flat, flat, P("gx", "gy"), P("gx", "gy", "gz"))
    out_specs = (rows, rows, flat, P("gx", "gy", "gz"))
    return jax.shard_map(shards, mesh=mesh, in_specs=in_specs, out_specs=out_specs, check_vma=False)
```

```python
import functools

import jax
import jax.numpy as jnp
from jax import lax
from jax.experimental import pallas as pl
from jax.experimental.pallas import tpu as pltpu
from jax.sharding import PartitionSpec as P

stiffness = 2.0
gravity_step = 0.3

LANES = 128
SLABS = 4
ZROWS = 10
CHANNELS = 8
ROWS = ZROWS * CHANNELS
F32 = jnp.float32
BF16 = jnp.bfloat16


def iota(shape, dim):
    return lax.broadcasted_iota(jnp.int32, shape, dim)


def tile_nodes(tile, rows, brick):
    lane = iota((rows, LANES), 1)
    if tile < 2:
        x, y = lane >> 1, (lane & 1) + tile * brick
        valid = lane < 2 * (brick + 2)
    elif tile < SLABS:
        plane, corner = lane < 64, lane - 64
        x = jnp.where(plane, lane >> 5, (corner & 3) >> 1) + (tile - 2) * brick
        y = jnp.where(plane, (lane & 31) + 1, (corner >> 2) * brick + (corner & 1))
        valid = jnp.where(plane, ((y >= 2) & (y < brick)).astype(jnp.int32), (corner < 8).astype(jnp.int32)) == 1
    else:
        x = (lane >> 5) + 4 * (tile - SLABS) + 1
        y = (lane & 31) + 1
        valid = (x >= 2) & (x < brick) & (y >= 2) & (y < brick)
    return x, y, valid


def tile_code(tile, rows, brick):
    x, y, valid = tile_nodes(tile, rows, brick)
    return jnp.where(valid, x * 64 + y, -1)


def block_columns(cells_ref):
    blocks = cells_ref.shape[1]
    same = iota((blocks, blocks), 0) == iota((blocks, blocks), 1)
    column = jnp.sum(jnp.where(same, cells_ref[...].astype(F32), 0.0), axis=1, keepdims=True)
    cells = jnp.broadcast_to(column, (blocks, LANES)).astype(jnp.int32)
    return (cells >> 5) * 128 + ((cells >> 1) & 15) * 2, cells & 1


def fill_one_hot(hot_ref, code, tiles, brick, masks=(None,)):
    blocks = code.shape[0]
    for at, (mask, tile) in enumerate((mask, tile) for mask in masks for tile in tiles):
        lane_code = tile_code(tile, blocks, brick) - code
        if mask is not None:
            lane_code = jnp.where(mask, lane_code, -1)
        for node in range(16):
            hit = lane_code == (node // 4) * 64 + node % 4
            hot_ref[pl.ds(node * blocks, blocks), pl.ds(at * LANES, LANES)] = jnp.where(hit, 1.0, 0.0).astype(BF16)


def deposit_windows(grid_ref, window_ref, hot_ref, all_ref):
    all_ref[...] = lax.dot_general(
        window_ref[...], hot_ref[...], (((0,), (0,)), ((), ())), preferred_element_type=F32
    )
    for z in range(ZROWS):
        piece = None
        for tz in range(2):
            wz = z - 4 * tz
            if 0 <= wz < 6:
                row = 64 * tz + 8 * wz
                part = all_ref[pl.ds(row, 8), :] + all_ref[pl.ds(128 + row, 8), :]
                piece = part if piece is None else piece + part
        for tile in range(grid_ref.shape[0]):
            grid_ref[tile, pl.ds(8 * z, 8), :] = piece[:, tile * LANES : (tile + 1) * LANES]


def inner_tiles(brick):
    return (0, 1) + tuple(range(SLABS, SLABS + brick // 4))


def spline(frac):
    return [0.5 * (0.5 - frac) ** 2, 0.75 - frac * frac, 0.5 * (0.5 + frac) ** 2]


def split(value):
    high = value.astype(BF16)
    return high, (value - high.astype(F32)).astype(BF16)


def is_even(axis):
    return lax.rem(lax.axis_index(axis), 2) == 0


def low_high(even, odd, axis):
    here = is_even(axis)
    place = lax.axis_index(axis)
    low, high = jnp.where(here, odd, even), jnp.where(here, even, odd)
    return jnp.where(place > 0, low, 0.0), jnp.where(place < lax.axis_size(axis) - 1, high, 0.0)


def diagonal_rows(ends):
    even = ends[0]
    low, high = low_high(even, ends[1] if len(ends) > 1 else jnp.zeros_like(even), "gz")
    return jnp.concatenate([low, jnp.zeros((ROWS - 32, LANES), F32), high], axis=0)


def pack_layers(tiles):
    row = iota((8, LANES), 0)
    firsts = [jnp.where(row == 7, pltpu.roll(mine, 7, 0), theirs) for theirs, mine in tiles]
    pairs = [
        jnp.where(row < 4, pltpu.roll(odd[1], 4, 0), even[1]) for even, odd in zip(tiles[0::2], tiles[1::2])
    ]
    return firsts + pairs


def layer_rows(refs, tile):
    row = iota((8, LANES), 0)
    planes = []
    for ref in refs:
        first, pair = ref[tile], ref[2 * ref.shape[0] // 3 + tile // 2]
        half = pltpu.roll(pair, 4, 0) if tile % 2 else pair
        own = jnp.where(row < 7, first, 0.0)
        halo = jnp.where(row >= 4, half, jnp.where(row == 0, pltpu.roll(first, 1, 0), 0.0))
        planes.append(jnp.concatenate([own, halo], axis=0))
    low, high = low_high(planes[0], planes[1] if len(planes) > 1 else jnp.zeros_like(planes[0]), "gz")
    return jnp.concatenate([low[8:], low[:8], jnp.zeros((ROWS - 32, LANES), F32), high], axis=0)


def to_rows(flat_ref, first, array_ref, blocks):
    channels = array_ref.shape[0]
    if channels > 8:
        tiles = jnp.stack([array_ref[pl.ds(0, 8), pl.ds(b * LANES, LANES)] for b in range(blocks)])
        flat_ref[pl.ds(first * blocks, 8 * blocks), :] = jnp.swapaxes(tiles, 0, 1).reshape(8 * blocks, LANES)
        for b in range(blocks):
            flat_ref[pl.ds((first + 8) * blocks + b, 1), :] = array_ref[pl.ds(8, 1), pl.ds(b * LANES, LANES)]
        return
    for b in range(blocks):
        flat_ref[pl.ds(first * blocks + b, channels, stride=blocks), :] = array_ref[:, pl.ds(b * LANES, LANES)]


def from_rows(array_ref, flat_ref, first, blocks):
    channels = array_ref.shape[0]
    if channels > 8:
        tiles = flat_ref[pl.ds(first * blocks, 8 * blocks), :].reshape(8, blocks, LANES)
        tiles = jnp.swapaxes(tiles, 0, 1)
        for b in range(blocks):
            array_ref[pl.ds(0, 8), pl.ds(b * LANES, LANES)] = tiles[b]
            array_ref[pl.ds(8, 1), pl.ds(b * LANES, LANES)] = flat_ref[pl.ds((first + 8) * blocks + b, 1), :]
        return
    for b in range(blocks):
        array_ref[:, pl.ds(b * LANES, LANES)] = flat_ref[pl.ds(first * blocks + b, channels, stride=blocks), :]


def corners(low, high):
    lane = iota(low.shape, 1)
    first, last = lane < 4, (lane >= 64) & (lane < 68)
    zero = jnp.zeros_like(low)
    lower = jnp.where(first, pltpu.roll(low, 64, 1), jnp.where(last, high, zero))
    upper = jnp.where(first, pltpu.roll(low, 60, 1), jnp.where(last, pltpu.roll(high, 124, 1), zero))
    return lower, upper


def spread_kernel(spread_ref, take_ref):
    particle = iota((LANES, 2 * LANES), 0)
    shift = iota((LANES, 2 * LANES), 1) - ((particle >> 5) * 64 + ((particle >> 3) & 3) * 8)
    for c in range(7):
        for oz in range(3):
            hit = shift == oz * 8 + c
            spread_ref[pl.ds((3 * c + oz) * LANES, LANES), :] = jnp.where(hit, 1.0, 0.0).astype(BF16)
    key = iota((2 * LANES, LANES), 0)
    particle = iota((2 * LANES, LANES), 1)
    shift = jnp.where((key >> 6) == (particle >> 5), (key & 31) - ((particle >> 3) & 3), -64)
    for a in range(3):
        for oz in range(3):
            hit = shift == 8 * a + oz
            take_ref[:, pl.ds((3 * a + oz) * LANES, LANES)] = jnp.where(hit, 1.0, 0.0).astype(BF16)


def deposit_kernel(*refs):
    cells_ref, count_ref, pos_ref, vel_ref, aff_ref, vol_ref, cvel_ref, caff_ref, top_ref, drag_ref = refs[:10]
    spread_ref, refs = refs[10], refs[11:]
    grid_ref, even_ref, odd_ref, diagonal_ref, meta_ref, shape_ref, window_ref, hot_ref = refs[:8]
    flat_ref, terms_ref, sums_ref, all_ref = refs[8:]
    blocks = vol_ref.shape[0]
    brick = drag_ref.shape[0]
    size_z = drag_ref.shape[1]
    code, upper_tile = block_columns(cells_ref)
    live_rows = iota((blocks, LANES), 0) < count_ref[...]
    meta_ref[0], meta_ref[1], meta_ref[2] = code, upper_tile, live_rows.astype(jnp.int32)
    fill_one_hot(hot_ref, code, (2, 3), brick)
    for first, ref in ((0, pos_ref), (3, vel_ref), (6, aff_ref), (15, cvel_ref), (18, caff_ref)):
        to_rows(flat_ref, first, ref, blocks)

    def channel(c):
        return flat_ref[pl.ds(c * blocks, blocks), :]

    live = live_rows.astype(F32)
    frac = [channel(k) for k in range(3)]
    weight = [spline(f) for f in frac]
    for k, value in enumerate(weight[0] + weight[1] + weight[2] + frac):
        shape_ref[pl.ds(k * blocks, blocks), :] = value
    stretch = stiffness * (vol_ref[...] - 1.0)
    linear, matrix = [live], [None]
    for a in range(3):
        row = [live * (channel(6 + 3 * a + b) - (stretch if a == b else 0.0)) for b in range(3)]
        matrix.append(row)
        linear.append(live * channel(3 + a) - sum(row[b] * frac[b] for b in range(3)))
    for a in range(3):
        row = [(4.0 * live) * channel(18 + 3 * a + b) for b in range(3)]
        matrix.append(row)
        linear.append(live * channel(15 + a) - sum(row[b] * frac[b] for b in range(3)))

    def put(row, slot, value):
        high, low = split(value)
        lanes = pl.ds(slot * LANES, LANES)
        terms_ref[pl.ds(row * blocks, blocks), lanes] = high
        terms_ref[pl.ds((9 + row) * blocks, blocks), lanes] = low

    for ox in range(3):
        for oy in range(3):
            planar = weight[0][ox] * weight[1][oy]
            weights = [planar * weight[2][oz] for oz in range(3)]
            for c in range(7):
                base = linear[c]
                if c:
                    if ox != 1:
                        base = base + matrix[c][0] if ox else base - matrix[c][0]
                    if oy != 1:
                        base = base + matrix[c][1] if oy else base - matrix[c][1]
                for oz in range(3):
                    value = base
                    if c and oz != 1:
                        value = base + matrix[c][2] if oz else base - matrix[c][2]
                    put(3 * ox + oy, 3 * c + oz, weights[oz] * value)

    sums_ref[...] = jnp.dot(terms_ref[...], spread_ref[...], preferred_element_type=F32)

    lane = iota((blocks, LANES), 1)
    low_half = lane < 64
    own_half = low_half == (upper_tile == 0)

    def partial(wx, oy):
        total = None
        for cx in range(2):
            ox = wx - cx
            if 0 <= ox < 3:
                lanes = pl.ds(cx * LANES, LANES)
                row = 3 * ox + oy
                piece = sums_ref[pl.ds(row * blocks, blocks), lanes] + sums_ref[pl.ds((9 + row) * blocks, blocks), lanes]
                total = piece if total is None else total + piece
        return total

    for wx in range(4):
        columns = [partial(wx, oy) for oy in range(3)]
        zero = jnp.zeros_like(columns[0])
        for wy in range(4):
            both = jnp.where(low_half, columns[wy] if wy < 3 else zero, columns[wy - 1] if wy else zero)
            node = jnp.where(own_half, both + pltpu.roll(both, 64, 1), 0.0)
            high, low = split(node)
            rows = pl.ds((4 * wx + wy) * blocks, blocks)
            window_ref[rows, pl.ds(0, LANES)] = high
            window_ref[rows, pl.ds(LANES, LANES)] = low

    deposit_windows(grid_ref, window_ref, hot_ref, all_ref)

    depth = iota((size_z, brick), 0) + lax.axis_index("gz") * size_z
    lane = iota((size_z, LANES), 1)
    blank = jnp.zeros((size_z, 32), F32)
    for side, x in enumerate((0, brick - 1)):
        layer = jnp.where(depth < top_ref[pl.ds(x, 1), :], drag_ref[x], 0.0)
        plane = jnp.concatenate([blank, layer, blank, blank] if side == 0 else [layer, blank, blank, blank], axis=1)
        plane = jnp.where(lane == 67 - 2 * side, layer[:, 0:1], plane)
        plane = jnp.where(lane == 70 - 2 * side, layer[:, brick - 1 : brick], plane)
        grid_ref[side, pl.ds(8 + 7, size_z, stride=8), :] = plane

    low, high = grid_ref[0], grid_ref[1]
    here = is_even("gx")
    even_ref[pl.ds(0, ROWS), :] = jnp.where(here, high, low)
    even_ref[pl.ds(ROWS, even_ref.shape[0] - ROWS), :] = jnp.zeros((even_ref.shape[0] - ROWS, LANES), F32)
    odd_ref[...] = jnp.where(here, low, high)
    here = is_even("gz")
    lower, upper = odd_ref[pl.ds(0, 16), :], odd_ref[pl.ds(ROWS - 16, 16), :]
    diagonal_ref[0] = jnp.where(here, upper, lower)
    if diagonal_ref.shape[0] > 1:
        diagonal_ref[1] = jnp.where(here, lower, upper)


def interior_kernel(window_ref, meta_ref, top_ref, drag_ref, grid_ref, hot_ref, all_ref):
    brick, size_z, _ = drag_ref.shape
    fill_one_hot(hot_ref, meta_ref[0], inner_tiles(brick), brick)
    deposit_windows(grid_ref, window_ref, hot_ref, all_ref)
    depth = iota((size_z, brick), 0) + lax.axis_index("gz") * size_z
    lane = iota((size_z, LANES), 1)
    ends = [jnp.zeros((size_z, LANES), F32)] * 2
    layers = []
    for x in range(brick):
        layer = jnp.where(depth < top_ref[pl.ds(x, 1), :], drag_ref[x], 0.0)
        layers.append(layer)
        ends[0] = jnp.where(lane == 2 * (x + 1) + 1, layer[:, 0:1], ends[0])
        ends[1] = jnp.where(lane == 2 * (x + 1), layer[:, brick - 1 : brick], ends[1])
    planes = ends + [jnp.concatenate(layers[4 * t : 4 * t + 4], axis=1) for t in range(brick // 4)]
    for at, plane in enumerate(planes):
        grid_ref[at, pl.ds(8 + 7, size_z, stride=8), :] = plane


def join_columns(near_y, near_x):
    lane = iota(near_y.shape, 1)
    near_x = jnp.where(lane < 98, pltpu.roll(near_x, 67, 1), pltpu.roll(near_x, 65, 1))
    return jnp.where(lane < 68, near_y, near_x)


def joined_columns(joined, near_x):
    lane = iota(joined.shape, 1)
    if not near_x:
        return jnp.where(lane < 68, joined, 0.0)
    first, second = (lane >= 1) & (lane <= 30), (lane >= 33) & (lane <= 62)
    return jnp.where(first, pltpu.roll(joined, 61, 1), jnp.where(second, pltpu.roll(joined, 63, 1), 0.0))


def own_tile(slab_ref, grid_ref, tile):
    return grid_ref[tile] if tile < 2 else slab_ref[tile - 2] if tile < SLABS else grid_ref[tile - 2]


def pack_z_kernel(slab_ref, grid_ref, xe_ref, even_ref, *odd_refs):
    here = is_even("gz")
    ends = []
    for first in (0, ROWS - 16):
        rows = pl.ds(first, 16)
        received = xe_ref[rows, :]
        extra = x_additions(*low_high(received, jnp.zeros_like(received), "gx"))
        tiles = [own_tile(slab_ref, grid_ref, t)[first : first + 16] + extra[t] for t in range(SLABS)]
        ends.append([join_columns(tiles[t], tiles[t + 2]) for t in range(2)])
        ends[-1] += [grid_ref[t, rows, :] for t in range(2, grid_ref.shape[0])]
    for up, refs in ((here, (even_ref,)), (jnp.logical_not(here), odd_refs)):
        for ref in refs:
            tiles = [
                (jnp.where(up, upper[8:], lower[:8]), jnp.where(up, upper[:8], lower[8:]))
                for lower, upper in zip(*ends)
            ]
            for at, rows in enumerate(pack_layers(tiles)):
                ref[at] = rows


def x_additions(low, high):
    lower, upper = corners(low, high)
    planar = iota(low.shape, 1) < 64
    return [lower, upper, jnp.where(planar, low, 0.0), jnp.where(planar, high, 0.0)]


def keep_kernel(received_ref, kept_ref):
    kept_ref[...] = received_ref[...]


def xz_additions(xe_ref, xo_ref, diagonals, layers, tiles):
    odd = xo_ref[...] + diagonal_rows([ref[...] for ref in diagonals])
    extra = x_additions(*low_high(xe_ref[pl.ds(0, ROWS), :], odd, "gx"))
    joined = [layer_rows(layers, t) for t in range(2)]
    return [extra[t] + joined_columns(joined[t % 2], t >= 2) for t in range(tiles)]


def pack_y_kernel(ends, *refs):
    grid_ref, xe_ref, xo_ref, *received = refs[:-3]
    even_ref, odd_ref, sums_ref = refs[-3:]
    extra = xz_additions(xe_ref, xo_ref, received[:ends], received[ends:], 2)
    lower, upper = grid_ref[0] + extra[0], grid_ref[1] + extra[1]
    sums_ref[0], sums_ref[1] = lower, upper
    here = is_even("gy")
    even_ref[...] = jnp.where(here, upper, lower)
    odd_ref[...] = jnp.where(here, lower, upper)


def node_gradients(counts, brick, size_z, tiles, totals, total_ref, push_ref, drag_ref, apart=0):
    place = [lax.axis_index(axis) for axis in ("gx", "gy", "gz")]
    row = iota((8, LANES), 0)
    blank = jnp.zeros((8, LANES), F32)
    for at, (tile, total) in enumerate(zip(tiles, totals)):
        total_ref[at, pl.ds(0, ROWS), :] = total
        total_ref[at, pl.ds(ROWS, 16), :] = jnp.zeros((16, LANES), F32)
        lanes = pl.ds(at * LANES, LANES)
        node_x, node_y, _ = tile_nodes(tile, 8, brick)
        node_x = node_x + (place[0] * brick - 1)
        node_y = node_y + (place[1] * brick - 1)
        drags = []
        for side in range(2):
            c = [total_ref[at, pl.ds(32 * side + k, 8, stride=8), :] for k in range(CHANNELS)]
            node_z = row + (4 * side - 1) + place[2] * size_z
            inside = (node_z >= 0) & (node_z < counts[2] * size_z)
            if tile in (2, 3):
                inside = inside & (iota((8, LANES), 1) < 64)
            if tile < SLABS:
                inside = inside & (node_x >= 0) & (node_x < counts[0] * brick)
                inside = inside & (node_y >= 0) & (node_y < counts[1] * brick)
            inverse = 1.0 / jnp.maximum(c[0], 1.0)
            scale = jnp.where(inside, (1.0 - c[7]) * inverse, 0.0)
            high, low = split(jnp.concatenate([c[4 + a] * scale for a in range(3)] + [blank], axis=0))
            if apart:
                lanes = pl.ds((apart * side + at) * LANES, LANES)
            for first in (0, 64) if apart else (64 * side,):
                push_ref[pl.ds(first, 32), lanes] = high
                push_ref[pl.ds(first + 32, 32), lanes] = low
            drags.append(
                c[4] * (c[1] * inverse) + c[5] * (c[2] * inverse) + c[6] * (c[3] * inverse - gravity_step)
            )
        drag_ref[at] = jnp.where(row < 7, pltpu.roll(drags[0], 7, 0), pltpu.roll(drags[1], 3, 0))


def gather(hot, push_ref):
    return lax.dot_general(hot, push_ref[...], (((1,), (1,)), ((), ())), preferred_element_type=F32)


def early_kernel(counts, ends, size_z, *refs):
    inputs, refs = refs[:-7], refs[-7:]
    meta_ref, hot_slab_ref, hot_ref, slab_ref, grid_ref, xe_ref, xo_ref, *received = inputs
    gathered_ref, drag_slab_ref, drag_ref, masked_ref, total_ref, push_slab_ref, push_ref = refs
    brick = 4 * (grid_ref.shape[0] - 2)
    extra = xz_additions(xe_ref, xo_ref, received[:ends], received[ends:], SLABS)
    totals = [slab_ref[tile - 2] + extra[tile] for tile in (2, 3)]
    node_gradients(counts, brick, size_z, (2, 3), totals, total_ref, push_slab_ref, drag_slab_ref)
    tiles = inner_tiles(brick)[2:]
    totals = [grid_ref[t - 2] + layer_rows(received[ends:], t - 2) for t in tiles]
    node_gradients(counts, brick, size_z, tiles, totals, total_ref, push_ref, drag_ref)
    gathered = gather(hot_slab_ref[...], push_slab_ref) + gather(
        hot_ref[:, pl.ds(2 * LANES, push_ref.shape[1])], push_ref
    )
    upper = meta_ref[1] == 1
    blocks = upper.shape[0]
    keep = (iota((blocks, LANES), 1) < 64) != upper
    for node in range(16):
        value = gathered[node * blocks : (node + 1) * blocks]
        gathered_ref[pl.ds(node * blocks, blocks), :] = jnp.where(keep, value, pltpu.roll(value, 64, 1))
    fill_one_hot(masked_ref, meta_ref[0], (0, 1), brick, (jnp.logical_not(upper), upper))


def collect_kernel(counts, *refs):
    inputs, refs = refs[:-10], refs[-10:]
    meta_ref, shape_ref, masked_ref, take_spread_ref, top_ref, gathered_ref, drag_slab_ref, drag_ref = inputs[:8]
    near_ref, ye_ref, yo_ref = inputs[8:]
    gvel_ref, gaff_ref, gvol_ref, gdrag_ref = refs[:4]
    total_ref, push_ref, drag_ends_ref, take_ref, pulled_ref, flat_ref = refs[4:]
    blocks = gvol_ref.shape[0]
    brick, size_z = gdrag_ref.shape[0], gdrag_ref.shape[1]
    saved = [shape_ref[pl.ds(k * blocks, blocks), :] for k in range(12)]
    weight, frac = [saved[3 * k : 3 * k + 3] for k in range(3)], saved[9:]

    low, high = low_high(ye_ref[...], yo_ref[...], "gy")
    totals = [near_ref[0] + low, near_ref[1] + high]
    node_gradients(counts, brick, size_z, (0, 1), totals, total_ref, push_ref, drag_ends_ref, 2)
    gathered = gathered_ref[...] + gather(masked_ref[...], push_ref)

    edges = [drag_ends_ref[t] for t in range(2)]
    depth = iota((size_z, brick), 0) + lax.axis_index("gz") * size_z
    lane = iota((size_z, LANES), 1)
    for x in range(brick):
        if x == 0:
            plane = pltpu.roll(drag_slab_ref[0], 96, 1)
        elif x == brick - 1:
            plane = drag_slab_ref[1]
        else:
            plane = drag_ref[x // 4]
            if x % 4:
                plane = pltpu.roll(plane, LANES - 32 * (x % 4), 1)
        at = 2 * (x + 1)
        plane = jnp.where(lane == 0, edges[0][:, at + 1 : at + 2], plane)
        plane = jnp.where(lane == brick - 1, edges[1][:, at : at + 1], plane)
        gdrag_ref[x] = jnp.where(depth < top_ref[pl.ds(x, 1), :], -plane[:, :brick], 0.0)

    lane = iota((blocks, LANES), 1)
    low_half = lane < 64
    nodes = [gathered[node * blocks : (node + 1) * blocks] for node in range(16)]
    for ox in range(3):
        for oy in range(3):
            for cx in range(2):
                value = jnp.where(low_half, nodes[4 * (cx + ox) + oy], nodes[4 * (cx + ox) + oy + 1])
                take_ref[pl.ds((3 * ox + oy) * blocks, blocks), pl.ds(cx * LANES, LANES)] = value.astype(BF16)

    pulled_ref[...] = jnp.dot(take_ref[...], take_spread_ref[...], preferred_element_type=F32)

    live = meta_ref[2].astype(F32)
    planar = [[live * weight[0][ox] * weight[1][oy] for oy in range(3)] for ox in range(3)]
    trace = None
    for a in range(3):
        sums_x, sums_y, sums_z = [], [None] * 3, None
        for ox in range(3):
            column = None
            for oy in range(3):
                rows = pl.ds((3 * ox + oy) * blocks, blocks)
                g = [pulled_ref[rows, pl.ds((3 * a + oz) * LANES, LANES)] for oz in range(3)]
                below, above = weight[2][0] * g[0], weight[2][2] * g[2]
                sum_z = planar[ox][oy] * (weight[2][1] * g[1] + (below + above))
                slope = planar[ox][oy] * (above - below)
                column = sum_z if column is None else column + sum_z
                sums_y[oy] = sum_z if sums_y[oy] is None else sums_y[oy] + sum_z
                sums_z = slope if sums_z is None else sums_z + slope
            sums_x.append(column)
        whole = sums_x[0] + sums_x[1] + sums_x[2]
        moments = [sums_x[2] - sums_x[0], sums_y[2] - sums_y[0], sums_z]
        flat_ref[pl.ds(a * blocks, blocks), :] = whole
        for b in range(3):
            value = moments[b] - frac[b] * whole
            flat_ref[pl.ds((3 + 3 * a + b) * blocks, blocks), :] = value
            if a == b:
                trace = value if trace is None else trace + value
    gvol_ref[...] = -stiffness * trace
    from_rows(gvel_ref, flat_ref, 0, blocks)
    from_rows(gaff_ref, flat_ref, 3, blocks)


def paired(index, count, first):
    partner = index + 1 if (index - first) % 2 == 0 else index - 1
    return partner if 0 <= partner < count else None


def exchange(array, counts, pair):
    names = ("gx", "gy", "gz")
    links = []
    for x in range(counts[0]):
        for y in range(counts[1]):
            for z in range(counts[2]):
                target = pair(x, y, z)
                if None not in target:
                    links.append(((x * counts[1] + y) * counts[2] + z, (target[0] * counts[1] + target[1]) * counts[2] + target[2]))
    return lax.ppermute(array, names, links) if links else jnp.zeros_like(array)


def shards(
    offsets, velocity, affine, volume, cot_velocity, cot_affine, block_cells, fill_counts, baffle_top, drag
):
    brick, _, size_z = drag.shape
    blocks = block_cells.shape[0]
    counts = tuple(lax.axis_size(axis) for axis in ("gx", "gy", "gz"))
    interior = brick // 4
    vmem = pl.BlockSpec(memory_space=pltpu.VMEM)

    def f32(*shape):
        return jax.ShapeDtypeStruct(shape, F32)

    def bf16(*shape):
        return jax.ShapeDtypeStruct(shape, BF16)

    def call(kernel, name, out_shape, operands, scratch=(), megabytes=4, flops=0):
        return pl.pallas_call(
            kernel,
            out_shape=out_shape,
            in_specs=[vmem] * len(operands),
            out_specs=(vmem,) * len(out_shape),
            scratch_shapes=scratch,
            compiler_params=pltpu.CompilerParams(vmem_limit_bytes=megabytes * 1024 * 1024),
            cost_estimate=pl.CostEstimate(flops=flops, bytes_accessed=1024, transcendentals=0),
            name=name,
        )(*operands)

    operands = (
        block_cells.reshape(1, blocks), fill_counts.reshape(1, 1), offsets, velocity, affine, volume.reshape(blocks, LANES), cot_velocity, cot_affine,
        baffle_top, drag.transpose(0, 2, 1),
    )
    slab = f32(ROWS, LANES)
    ends = 2 if counts[2] > 2 else 1
    spread, take = call(
        spread_kernel, "spread", (bf16(21 * LANES, 2 * LANES), bf16(2 * LANES, 9 * LANES)), (), flops=20_000_000_000
    )
    edge, send_xe, send_xo, send_xz, meta, shape, window, hot_edge = call(
        deposit_kernel,
        "deposit",
        (
            f32(2, ROWS, LANES), f32(192, LANES), slab, f32(ends, 16, LANES),
            jax.ShapeDtypeStruct((3, blocks, LANES), jnp.int32), f32(12 * blocks, LANES),
            bf16(16 * blocks, 2 * LANES), bf16(16 * blocks, 2 * LANES),
        ),
        operands + (spread,),
        scratch=[
            pltpu.VMEM((27 * blocks, LANES), F32),
            pltpu.VMEM((18 * blocks, 21 * LANES), BF16),
            pltpu.VMEM((18 * blocks, 2 * LANES), F32),
            pltpu.VMEM((2 * LANES, 2 * LANES), F32),
        ],
        megabytes=16,
    )

    def even_x(x):
        return paired(x, counts[0], 0)

    def odd_x(x, y, z):
        partner = paired(x, counts[0], 1)
        return (x, y, paired(z, counts[2], 0)) if partner is None else (partner, y, z)

    def odd_xz(x, y, z, first):
        partner = paired(x, counts[0], 1)
        return x if partner is None else partner, y, paired(z, counts[2], first)

    def odd_y(x, y, z):
        partner = paired(y, counts[1], 1)
        return (even_x(x), y, z) if partner is None else (x, partner, z)

    xe = exchange(send_xe, counts, lambda x, y, z: (even_x(x), y, z))
    xo = exchange(send_xo, counts, odd_x)
    xz = [
        exchange(send_xz[first], counts, lambda x, y, z: odd_xz(x, y, z, first))
        for first in range(ends)
    ]
    grid, hot = call(
        interior_kernel,
        "interior",
        (f32(2 + interior, ROWS, LANES), bf16(16 * blocks, (2 + interior) * LANES)),
        (window, meta, *operands[-2:]),
        scratch=[pltpu.VMEM((2 * LANES, (2 + interior) * LANES), F32)],
        megabytes=8,
        flops=1_000_000_000,
    )
    (xo,) = call(keep_kernel, "keep", (slab,), (xo,), flops=400_000_000)
    send_z = call(pack_z_kernel, "pack_z", (f32(3 * (2 + interior) // 2, 8, LANES),) * ends, (edge, grid, xe))
    layers = [
        exchange(array, counts, lambda x, y, z: (x, y, paired(z, counts[2], first)))
        for first, array in enumerate(send_z)
    ]
    send_ye, send_yo, near_y = call(
        functools.partial(pack_y_kernel, ends), "pack_y", (slab, slab, f32(2, ROWS, LANES)), (grid, xe, xo, *xz, *layers)
    )
    yo = exchange(send_yo, counts, odd_y)
    ye = exchange(send_ye, counts, lambda x, y, z: (x, paired(y, counts[1], 0), z))
    gathered, drag_slab, drag_rows, masked = call(
        functools.partial(early_kernel, counts, ends, size_z),
        "early",
        (
            f32(16 * blocks, LANES), f32(2, size_z, LANES), f32(interior, size_z, LANES),
            bf16(16 * blocks, 4 * LANES),
        ),
        (meta, hot_edge, hot, edge, grid, xe, xo, *xz, *layers),
        scratch=[
            pltpu.VMEM((interior, ROWS + 24, LANES), F32),
            pltpu.VMEM((LANES, 2 * LANES), BF16),
            pltpu.VMEM((LANES, interior * LANES), BF16),
        ],
        megabytes=8,
        flops=1_000_000_000,
    )
    grad_velocity, grad_affine, grad_volume, grad_drag = call(
        functools.partial(collect_kernel, counts),
        "collect",
        (f32(3, blocks * LANES), f32(9, blocks * LANES), f32(blocks, LANES), f32(brick, size_z, brick)),
        (meta, shape, masked, take, baffle_top, gathered, drag_slab, drag_rows, near_y, ye, yo),
        scratch=[
            pltpu.VMEM((2, ROWS + 24, LANES), F32),
            pltpu.VMEM((LANES, 4 * LANES), BF16),
            pltpu.VMEM((2, size_z, LANES), F32),
            pltpu.VMEM((9 * blocks, 2 * LANES), BF16),
            pltpu.VMEM((9 * blocks, 9 * LANES), F32),
            pltpu.VMEM((12 * blocks, LANES), F32),
        ],
        megabytes=12,
    )
    return grad_velocity, grad_affine, grad_volume.reshape(-1), grad_drag.transpose(0, 2, 1)


def solution(mesh):
    everywhere = ("gx", "gy", "gz")
    rows, flat = P(None, everywhere), P(everywhere)
    in_specs = (rows, rows, rows, flat, rows, rows, flat, flat, P("gx", "gy"), P("gx", "gy", "gz"))
    out_specs = (rows, rows, flat, P("gx", "gy", "gz"))
    return jax.shard_map(shards, mesh=mesh, in_specs=in_specs, out_specs=out_specs, check_vma=False)
```

```python
import functools

import jax
import jax.numpy as jnp
from jax import lax
from jax.experimental import pallas as pl
from jax.experimental.pallas import tpu as pltpu
from jax.sharding import PartitionSpec as P

stiffness = 2.0
gravity_step = 0.3

LANES = 128
SLABS = 4
ZROWS = 10
CHANNELS = 8
ROWS = ZROWS * CHANNELS
F32 = jnp.float32
BF16 = jnp.bfloat16


def iota(shape, dim):
    return lax.broadcasted_iota(jnp.int32, shape, dim)


def tile_nodes(tile, rows, brick):
    lane = iota((rows, LANES), 1)
    if tile < 2:
        x, y = lane >> 1, (lane & 1) + tile * brick
        valid = lane < 2 * (brick + 2)
    elif tile < SLABS:
        plane, corner = lane < 64, lane - 64
        x = jnp.where(plane, lane >> 5, (corner & 3) >> 1) + (tile - 2) * brick
        y = jnp.where(plane, (lane & 31) + 1, (corner >> 2) * brick + (corner & 1))
        valid = jnp.where(plane, ((y >= 2) & (y < brick)).astype(jnp.int32), (corner < 8).astype(jnp.int32)) == 1
    else:
        x = (lane >> 5) + 4 * (tile - SLABS) + 1
        y = (lane & 31) + 1
        valid = (x >= 2) & (x < brick) & (y >= 2) & (y < brick)
    return x, y, valid


def tile_code(tile, rows, brick):
    x, y, valid = tile_nodes(tile, rows, brick)
    return jnp.where(valid, x * 64 + y, -1)


def block_columns(cells_ref):
    blocks = cells_ref.shape[1]
    same = iota((blocks, blocks), 0) == iota((blocks, blocks), 1)
    column = jnp.sum(jnp.where(same, cells_ref[...].astype(F32), 0.0), axis=1, keepdims=True)
    cells = jnp.broadcast_to(column, (blocks, LANES)).astype(jnp.int32)
    return (cells >> 5) * 128 + ((cells >> 1) & 15) * 2, cells & 1


def fill_one_hot(hot_ref, code, tiles, brick, masks=(None,)):
    blocks = code.shape[0]
    for at, (mask, tile) in enumerate((mask, tile) for mask in masks for tile in tiles):
        lane_code = tile_code(tile, blocks, brick) - code
        if mask is not None:
            lane_code = jnp.where(mask, lane_code, -1)
        for node in range(16):
            hit = lane_code == (node // 4) * 64 + node % 4
            hot_ref[pl.ds(node * blocks, blocks), pl.ds(at * LANES, LANES)] = jnp.where(hit, 1.0, 0.0).astype(BF16)


def deposit_windows(grid_ref, window_ref, hot_ref, all_ref):
    all_ref[...] = lax.dot_general(
        window_ref[...], hot_ref[...], (((0,), (0,)), ((), ())), preferred_element_type=F32
    )
    for z in range(ZROWS):
        piece = None
        for tz in range(2):
            wz = z - 4 * tz
            if 0 <= wz < 6:
                row = 64 * tz + 8 * wz
                part = all_ref[pl.ds(row, 8), :] + all_ref[pl.ds(128 + row, 8), :]
                piece = part if piece is None else piece + part
        for tile in range(grid_ref.shape[0]):
            grid_ref[tile, pl.ds(8 * z, 8), :] = piece[:, tile * LANES : (tile + 1) * LANES]


def inner_tiles(brick):
    return (0, 1) + tuple(range(SLABS, SLABS + brick // 4))


def spline(frac):
    return [0.5 * (0.5 - frac) ** 2, 0.75 - frac * frac, 0.5 * (0.5 + frac) ** 2]


def split(value):
    high = value.astype(BF16)
    return high, (value - high.astype(F32)).astype(BF16)


def is_even(axis):
    return lax.rem(lax.axis_index(axis), 2) == 0


def low_high(even, odd, axis):
    here = is_even(axis)
    place = lax.axis_index(axis)
    low, high = jnp.where(here, odd, even), jnp.where(here, even, odd)
    return jnp.where(place > 0, low, 0.0), jnp.where(place < lax.axis_size(axis) - 1, high, 0.0)


def diagonal_rows(ends):
    even = ends[0]
    low, high = low_high(even, ends[1] if len(ends) > 1 else jnp.zeros_like(even), "gz")
    return jnp.concatenate([low, jnp.zeros((ROWS - 32, LANES), F32), high], axis=0)


def pack_layers(tiles):
    row = iota((8, LANES), 0)
    firsts = [jnp.where(row == 7, pltpu.roll(mine, 7, 0), theirs) for theirs, mine in tiles]
    pairs = [
        jnp.where(row < 4, pltpu.roll(odd[1], 4, 0), even[1]) for even, odd in zip(tiles[0::2], tiles[1::2])
    ]
    return firsts + pairs


def layer_rows(refs, tile):
    row = iota((8, LANES), 0)
    planes = []
    for ref in refs:
        first, pair = ref[tile], ref[2 * ref.shape[0] // 3 + tile // 2]
        half = pltpu.roll(pair, 4, 0) if tile % 2 else pair
        own = jnp.where(row < 7, first, 0.0)
        halo = jnp.where(row >= 4, half, jnp.where(row == 0, pltpu.roll(first, 1, 0), 0.0))
        planes.append(jnp.concatenate([own, halo], axis=0))
    low, high = low_high(planes[0], planes[1] if len(planes) > 1 else jnp.zeros_like(planes[0]), "gz")
    return jnp.concatenate([low[8:], low[:8], jnp.zeros((ROWS - 32, LANES), F32), high], axis=0)


def to_rows(flat_ref, first, array_ref, blocks):
    channels = array_ref.shape[0]
    if channels > 8:
        tiles = jnp.stack([array_ref[pl.ds(0, 8), pl.ds(b * LANES, LANES)] for b in range(blocks)])
        flat_ref[pl.ds(first * blocks, 8 * blocks), :] = jnp.swapaxes(tiles, 0, 1).reshape(8 * blocks, LANES)
        for b in range(blocks):
            flat_ref[pl.ds((first + 8) * blocks + b, 1), :] = array_ref[pl.ds(8, 1), pl.ds(b * LANES, LANES)]
        return
    for b in range(blocks):
        flat_ref[pl.ds(first * blocks + b, channels, stride=blocks), :] = array_ref[:, pl.ds(b * LANES, LANES)]


def from_rows(array_ref, flat_ref, first, blocks):
    channels = array_ref.shape[0]
    if channels > 8:
        tiles = flat_ref[pl.ds(first * blocks, 8 * blocks), :].reshape(8, blocks, LANES)
        tiles = jnp.swapaxes(tiles, 0, 1)
        for b in range(blocks):
            array_ref[pl.ds(0, 8), pl.ds(b * LANES, LANES)] = tiles[b]
            array_ref[pl.ds(8, 1), pl.ds(b * LANES, LANES)] = flat_ref[pl.ds((first + 8) * blocks + b, 1), :]
        return
    for b in range(blocks):
        array_ref[:, pl.ds(b * LANES, LANES)] = flat_ref[pl.ds(first * blocks + b, channels, stride=blocks), :]


def corners(low, high):
    lane = iota(low.shape, 1)
    first, last = lane < 4, (lane >= 64) & (lane < 68)
    zero = jnp.zeros_like(low)
    lower = jnp.where(first, pltpu.roll(low, 64, 1), jnp.where(last, high, zero))
    upper = jnp.where(first, pltpu.roll(low, 60, 1), jnp.where(last, pltpu.roll(high, 124, 1), zero))
    return lower, upper


def fill_take(take_ref):
    key = iota((2 * LANES, LANES), 0)
    particle = iota((2 * LANES, LANES), 1)
    shift = jnp.where((key >> 6) == (particle >> 5), (key & 31) - ((particle >> 3) & 3), -64)
    for a in range(3):
        for oz in range(3):
            hit = shift == 8 * a + oz
            take_ref[:, pl.ds((3 * a + oz) * LANES, LANES)] = jnp.where(hit, 1.0, 0.0).astype(BF16)


def spread_kernel(spread_ref):
    particle = iota((LANES, 2 * LANES), 0)
    shift = iota((LANES, 2 * LANES), 1) - ((particle >> 5) * 64 + ((particle >> 3) & 3) * 8)
    for c in range(7):
        for oz in range(3):
            hit = shift == oz * 8 + c
            spread_ref[pl.ds((3 * c + oz) * LANES, LANES), :] = jnp.where(hit, 1.0, 0.0).astype(BF16)


def deposit_kernel(*refs):
    cells_ref, count_ref, pos_ref, vel_ref, aff_ref, vol_ref, cvel_ref, caff_ref, top_ref, drag_ref = refs[:10]
    spread_ref, refs = refs[10], refs[11:]
    grid_ref, even_ref, odd_ref, diagonal_ref, meta_ref, shape_ref, window_ref, hot_ref = refs[:8]
    flat_ref, terms_ref, sums_ref, all_ref = refs[8:]
    blocks = vol_ref.shape[0]
    brick = drag_ref.shape[0]
    size_z = drag_ref.shape[1]
    code, upper_tile = block_columns(cells_ref)
    live_rows = iota((blocks, LANES), 0) < count_ref[...]
    meta_ref[0], meta_ref[1], meta_ref[2] = code, upper_tile, live_rows.astype(jnp.int32)
    fill_one_hot(hot_ref, code, (2, 3), brick)
    for first, ref in ((0, pos_ref), (3, vel_ref), (6, aff_ref), (15, cvel_ref), (18, caff_ref)):
        to_rows(flat_ref, first, ref, blocks)

    def channel(c):
        return flat_ref[pl.ds(c * blocks, blocks), :]

    live = live_rows.astype(F32)
    frac = [channel(k) for k in range(3)]
    weight = [spline(f) for f in frac]
    for k, value in enumerate(weight[0] + weight[1] + weight[2] + frac):
        shape_ref[pl.ds(k * blocks, blocks), :] = value
    stretch = stiffness * (vol_ref[...] - 1.0)
    linear, matrix = [live], [None]
    for a in range(3):
        row = [live * (channel(6 + 3 * a + b) - (stretch if a == b else 0.0)) for b in range(3)]
        matrix.append(row)
        linear.append(live * channel(3 + a) - sum(row[b] * frac[b] for b in range(3)))
    for a in range(3):
        row = [(4.0 * live) * channel(18 + 3 * a + b) for b in range(3)]
        matrix.append(row)
        linear.append(live * channel(15 + a) - sum(row[b] * frac[b] for b in range(3)))

    def put(row, slot, value):
        high, low = split(value)
        lanes = pl.ds(slot * LANES, LANES)
        terms_ref[pl.ds(row * blocks, blocks), lanes] = high
        terms_ref[pl.ds((9 + row) * blocks, blocks), lanes] = low

    for ox in range(3):
        for oy in range(3):
            planar = weight[0][ox] * weight[1][oy]
            weights = [planar * weight[2][oz] for oz in range(3)]
            for c in range(7):
                base = linear[c]
                if c:
                    if ox != 1:
                        base = base + matrix[c][0] if ox else base - matrix[c][0]
                    if oy != 1:
                        base = base + matrix[c][1] if oy else base - matrix[c][1]
                for oz in range(3):
                    value = base
                    if c and oz != 1:
                        value = base + matrix[c][2] if oz else base - matrix[c][2]
                    put(3 * ox + oy, 3 * c + oz, weights[oz] * value)

    sums_ref[...] = jnp.dot(terms_ref[...], spread_ref[...], preferred_element_type=F32)

    lane = iota((blocks, LANES), 1)
    low_half = lane < 64
    own_half = low_half == (upper_tile == 0)

    def partial(wx, oy):
        total = None
        for cx in range(2):
            ox = wx - cx
            if 0 <= ox < 3:
                lanes = pl.ds(cx * LANES, LANES)
                row = 3 * ox + oy
                piece = sums_ref[pl.ds(row * blocks, blocks), lanes] + sums_ref[pl.ds((9 + row) * blocks, blocks), lanes]
                total = piece if total is None else total + piece
        return total

    for wx in range(4):
        columns = [partial(wx, oy) for oy in range(3)]
        zero = jnp.zeros_like(columns[0])
        for wy in range(4):
            both = jnp.where(low_half, columns[wy] if wy < 3 else zero, columns[wy - 1] if wy else zero)
            node = jnp.where(own_half, both + pltpu.roll(both, 64, 1), 0.0)
            high, low = split(node)
            rows = pl.ds((4 * wx + wy) * blocks, blocks)
            window_ref[rows, pl.ds(0, LANES)] = high
            window_ref[rows, pl.ds(LANES, LANES)] = low

    deposit_windows(grid_ref, window_ref, hot_ref, all_ref)

    depth = iota((size_z, brick), 0) + lax.axis_index("gz") * size_z
    lane = iota((size_z, LANES), 1)
    blank = jnp.zeros((size_z, 32), F32)
    for side, x in enumerate((0, brick - 1)):
        layer = jnp.where(depth < top_ref[pl.ds(x, 1), :], drag_ref[x], 0.0)
        plane = jnp.concatenate([blank, layer, blank, blank] if side == 0 else [layer, blank, blank, blank], axis=1)
        plane = jnp.where(lane == 67 - 2 * side, layer[:, 0:1], plane)
        plane = jnp.where(lane == 70 - 2 * side, layer[:, brick - 1 : brick], plane)
        grid_ref[side, pl.ds(8 + 7, size_z, stride=8), :] = plane

    low, high = grid_ref[0], grid_ref[1]
    here = is_even("gx")
    even_ref[pl.ds(0, ROWS), :] = jnp.where(here, high, low)
    even_ref[pl.ds(ROWS, even_ref.shape[0] - ROWS), :] = jnp.zeros((even_ref.shape[0] - ROWS, LANES), F32)
    odd_ref[...] = jnp.where(here, low, high)
    here = is_even("gz")
    lower, upper = odd_ref[pl.ds(0, 16), :], odd_ref[pl.ds(ROWS - 16, 16), :]
    diagonal_ref[0] = jnp.where(here, upper, lower)
    if diagonal_ref.shape[0] > 1:
        diagonal_ref[1] = jnp.where(here, lower, upper)


def interior_kernel(window_ref, meta_ref, top_ref, drag_ref, grid_ref, hot_ref, all_ref):
    brick, size_z, _ = drag_ref.shape
    fill_one_hot(hot_ref, meta_ref[0], inner_tiles(brick), brick)
    deposit_windows(grid_ref, window_ref, hot_ref, all_ref)
    depth = iota((size_z, brick), 0) + lax.axis_index("gz") * size_z
    lane = iota((size_z, LANES), 1)
    ends = [jnp.zeros((size_z, LANES), F32)] * 2
    layers = []
    for x in range(brick):
        layer = jnp.where(depth < top_ref[pl.ds(x, 1), :], drag_ref[x], 0.0)
        layers.append(layer)
        ends[0] = jnp.where(lane == 2 * (x + 1) + 1, layer[:, 0:1], ends[0])
        ends[1] = jnp.where(lane == 2 * (x + 1), layer[:, brick - 1 : brick], ends[1])
    planes = ends + [jnp.concatenate(layers[4 * t : 4 * t + 4], axis=1) for t in range(brick // 4)]
    for at, plane in enumerate(planes):
        grid_ref[at, pl.ds(8 + 7, size_z, stride=8), :] = plane


def join_columns(near_y, near_x):
    lane = iota(near_y.shape, 1)
    near_x = jnp.where(lane < 98, pltpu.roll(near_x, 67, 1), pltpu.roll(near_x, 65, 1))
    return jnp.where(lane < 68, near_y, near_x)


def joined_columns(joined, near_x):
    lane = iota(joined.shape, 1)
    if not near_x:
        return jnp.where(lane < 68, joined, 0.0)
    first, second = (lane >= 1) & (lane <= 30), (lane >= 33) & (lane <= 62)
    return jnp.where(first, pltpu.roll(joined, 61, 1), jnp.where(second, pltpu.roll(joined, 63, 1), 0.0))


def own_tile(slab_ref, grid_ref, tile):
    return grid_ref[tile] if tile < 2 else slab_ref[tile - 2] if tile < SLABS else grid_ref[tile - 2]


def pack_z_kernel(slab_ref, grid_ref, xe_ref, even_ref, *odd_refs):
    here = is_even("gz")
    ends = []
    for first in (0, ROWS - 16):
        rows = pl.ds(first, 16)
        received = xe_ref[rows, :]
        extra = x_additions(*low_high(received, jnp.zeros_like(received), "gx"))
        tiles = [own_tile(slab_ref, grid_ref, t)[first : first + 16] + extra[t] for t in range(SLABS)]
        ends.append([join_columns(tiles[t], tiles[t + 2]) for t in range(2)])
        ends[-1] += [grid_ref[t, rows, :] for t in range(2, grid_ref.shape[0])]
    for up, refs in ((here, (even_ref,)), (jnp.logical_not(here), odd_refs)):
        for ref in refs:
            tiles = [
                (jnp.where(up, upper[8:], lower[:8]), jnp.where(up, upper[:8], lower[8:]))
                for lower, upper in zip(*ends)
            ]
            for at, rows in enumerate(pack_layers(tiles)):
                ref[at] = rows


def x_additions(low, high):
    lower, upper = corners(low, high)
    planar = iota(low.shape, 1) < 64
    return [lower, upper, jnp.where(planar, low, 0.0), jnp.where(planar, high, 0.0)]


def keep_kernel(received_ref, kept_ref):
    kept_ref[...] = received_ref[...]


def xz_additions(xe_ref, xo_ref, diagonals, layers, tiles):
    odd = xo_ref[...] + diagonal_rows([ref[...] for ref in diagonals])
    extra = x_additions(*low_high(xe_ref[pl.ds(0, ROWS), :], odd, "gx"))
    joined = [layer_rows(layers, t) for t in range(2)]
    return [extra[t] + joined_columns(joined[t % 2], t >= 2) for t in range(tiles)]


def pack_y_kernel(ends, *refs):
    grid_ref, xe_ref, xo_ref, *received = refs[:-3]
    even_ref, odd_ref, sums_ref = refs[-3:]
    extra = xz_additions(xe_ref, xo_ref, received[:ends], received[ends:], 2)
    lower, upper = grid_ref[0] + extra[0], grid_ref[1] + extra[1]
    sums_ref[0], sums_ref[1] = lower, upper
    here = is_even("gy")
    even_ref[...] = jnp.where(here, upper, lower)
    odd_ref[...] = jnp.where(here, lower, upper)


def node_gradients(counts, brick, size_z, tiles, totals, total_ref, push_ref, drag_ref, apart=0):
    place = [lax.axis_index(axis) for axis in ("gx", "gy", "gz")]
    row = iota((8, LANES), 0)
    blank = jnp.zeros((8, LANES), F32)
    for at, (tile, total) in enumerate(zip(tiles, totals)):
        total_ref[at, pl.ds(0, ROWS), :] = total
        total_ref[at, pl.ds(ROWS, 16), :] = jnp.zeros((16, LANES), F32)
        lanes = pl.ds(at * LANES, LANES)
        node_x, node_y, _ = tile_nodes(tile, 8, brick)
        node_x = node_x + (place[0] * brick - 1)
        node_y = node_y + (place[1] * brick - 1)
        drags = []
        for side in range(2):
            c = [total_ref[at, pl.ds(32 * side + k, 8, stride=8), :] for k in range(CHANNELS)]
            node_z = row + (4 * side - 1) + place[2] * size_z
            inside = (node_z >= 0) & (node_z < counts[2] * size_z)
            if tile in (2, 3):
                inside = inside & (iota((8, LANES), 1) < 64)
            if tile < SLABS:
                inside = inside & (node_x >= 0) & (node_x < counts[0] * brick)
                inside = inside & (node_y >= 0) & (node_y < counts[1] * brick)
            inverse = 1.0 / jnp.maximum(c[0], 1.0)
            scale = jnp.where(inside, (1.0 - c[7]) * inverse, 0.0)
            high, low = split(jnp.concatenate([c[4 + a] * scale for a in range(3)] + [blank], axis=0))
            if apart:
                lanes = pl.ds((apart * side + at) * LANES, LANES)
            for first in (0, 64) if apart else (64 * side,):
                push_ref[pl.ds(first, 32), lanes] = high
                push_ref[pl.ds(first + 32, 32), lanes] = low
            drags.append(
                c[4] * (c[1] * inverse) + c[5] * (c[2] * inverse) + c[6] * (c[3] * inverse - gravity_step)
            )
        drag_ref[at] = jnp.where(row < 7, pltpu.roll(drags[0], 7, 0), pltpu.roll(drags[1], 3, 0))


def gather(hot, push_ref):
    return lax.dot_general(hot, push_ref[...], (((1,), (1,)), ((), ())), preferred_element_type=F32)


def early_kernel(counts, ends, size_z, *refs):
    inputs, refs = refs[:-8], refs[-8:]
    meta_ref, hot_slab_ref, hot_ref, slab_ref, grid_ref, xe_ref, xo_ref, *received = inputs
    gathered_ref, drag_slab_ref, drag_ref, masked_ref, take_ref, total_ref, push_slab_ref, push_ref = refs
    fill_take(take_ref)
    brick = 4 * (grid_ref.shape[0] - 2)
    extra = xz_additions(xe_ref, xo_ref, received[:ends], received[ends:], SLABS)
    totals = [slab_ref[tile - 2] + extra[tile] for tile in (2, 3)]
    node_gradients(counts, brick, size_z, (2, 3), totals, total_ref, push_slab_ref, drag_slab_ref)
    tiles = inner_tiles(brick)[2:]
    totals = [grid_ref[t - 2] + layer_rows(received[ends:], t - 2) for t in tiles]
    node_gradients(counts, brick, size_z, tiles, totals, total_ref, push_ref, drag_ref)
    gathered = gather(hot_slab_ref[...], push_slab_ref) + gather(
        hot_ref[:, pl.ds(2 * LANES, push_ref.shape[1])], push_ref
    )
    upper = meta_ref[1] == 1
    blocks = upper.shape[0]
    keep = (iota((blocks, LANES), 1) < 64) != upper
    for node in range(16):
        value = gathered[node * blocks : (node + 1) * blocks]
        gathered_ref[pl.ds(node * blocks, blocks), :] = jnp.where(keep, value, pltpu.roll(value, 64, 1))
    fill_one_hot(masked_ref, meta_ref[0], (0, 1), brick, (jnp.logical_not(upper), upper))


def collect_kernel(counts, *refs):
    inputs, refs = refs[:-10], refs[-10:]
    meta_ref, shape_ref, masked_ref, take_spread_ref, top_ref, gathered_ref, drag_slab_ref, drag_ref = inputs[:8]
    near_ref, ye_ref, yo_ref = inputs[8:]
    gvel_ref, gaff_ref, gvol_ref, gdrag_ref = refs[:4]
    total_ref, push_ref, drag_ends_ref, take_ref, pulled_ref, flat_ref = refs[4:]
    blocks = gvol_ref.shape[0]
    brick, size_z = gdrag_ref.shape[0], gdrag_ref.shape[1]
    saved = [shape_ref[pl.ds(k * blocks, blocks), :] for k in range(12)]
    weight, frac = [saved[3 * k : 3 * k + 3] for k in range(3)], saved[9:]

    low, high = low_high(ye_ref[...], yo_ref[...], "gy")
    totals = [near_ref[0] + low, near_ref[1] + high]
    node_gradients(counts, brick, size_z, (0, 1), totals, total_ref, push_ref, drag_ends_ref, 2)
    gathered = gathered_ref[...] + gather(masked_ref[...], push_ref)

    edges = [drag_ends_ref[t] for t in range(2)]
    depth = iota((size_z, brick), 0) + lax.axis_index("gz") * size_z
    lane = iota((size_z, LANES), 1)
    for x in range(brick):
        if x == 0:
            plane = pltpu.roll(drag_slab_ref[0], 96, 1)
        elif x == brick - 1:
            plane = drag_slab_ref[1]
        else:
            plane = drag_ref[x // 4]
            if x % 4:
                plane = pltpu.roll(plane, LANES - 32 * (x % 4), 1)
        at = 2 * (x + 1)
        plane = jnp.where(lane == 0, edges[0][:, at + 1 : at + 2], plane)
        plane = jnp.where(lane == brick - 1, edges[1][:, at : at + 1], plane)
        gdrag_ref[x] = jnp.where(depth < top_ref[pl.ds(x, 1), :], -plane[:, :brick], 0.0)

    lane = iota((blocks, LANES), 1)
    low_half = lane < 64
    nodes = [gathered[node * blocks : (node + 1) * blocks] for node in range(16)]
    for ox in range(3):
        for oy in range(3):
            for cx in range(2):
                value = jnp.where(low_half, nodes[4 * (cx + ox) + oy], nodes[4 * (cx + ox) + oy + 1])
                take_ref[pl.ds((3 * ox + oy) * blocks, blocks), pl.ds(cx * LANES, LANES)] = value.astype(BF16)

    pulled_ref[...] = jnp.dot(take_ref[...], take_spread_ref[...], preferred_element_type=F32)

    live = meta_ref[2].astype(F32)
    planar = [[live * weight[0][ox] * weight[1][oy] for oy in range(3)] for ox in range(3)]
    trace = None
    for a in range(3):
        sums_x, sums_y, sums_z = [], [None] * 3, None
        for ox in range(3):
            column = None
            for oy in range(3):
                rows = pl.ds((3 * ox + oy) * blocks, blocks)
                g = [pulled_ref[rows, pl.ds((3 * a + oz) * LANES, LANES)] for oz in range(3)]
                below, above = weight[2][0] * g[0], weight[2][2] * g[2]
                sum_z = planar[ox][oy] * (weight[2][1] * g[1] + (below + above))
                slope = planar[ox][oy] * (above - below)
                column = sum_z if column is None else column + sum_z
                sums_y[oy] = sum_z if sums_y[oy] is None else sums_y[oy] + sum_z
                sums_z = slope if sums_z is None else sums_z + slope
            sums_x.append(column)
        whole = sums_x[0] + sums_x[1] + sums_x[2]
        moments = [sums_x[2] - sums_x[0], sums_y[2] - sums_y[0], sums_z]
        flat_ref[pl.ds(a * blocks, blocks), :] = whole
        for b in range(3):
            value = moments[b] - frac[b] * whole
            flat_ref[pl.ds((3 + 3 * a + b) * blocks, blocks), :] = value
            if a == b:
                trace = value if trace is None else trace + value
    gvol_ref[...] = -stiffness * trace
    from_rows(gvel_ref, flat_ref, 0, blocks)
    from_rows(gaff_ref, flat_ref, 3, blocks)


def paired(index, count, first):
    partner = index + 1 if (index - first) % 2 == 0 else index - 1
    return partner if 0 <= partner < count else None


def exchange(array, counts, pair):
    names = ("gx", "gy", "gz")
    links = []
    for x in range(counts[0]):
        for y in range(counts[1]):
            for z in range(counts[2]):
                target = pair(x, y, z)
                if None not in target:
                    links.append(((x * counts[1] + y) * counts[2] + z, (target[0] * counts[1] + target[1]) * counts[2] + target[2]))
    return lax.ppermute(array, names, links) if links else jnp.zeros_like(array)


def shards(
    offsets, velocity, affine, volume, cot_velocity, cot_affine, block_cells, fill_counts, baffle_top, drag
):
    brick, _, size_z = drag.shape
    blocks = block_cells.shape[0]
    counts = tuple(lax.axis_size(axis) for axis in ("gx", "gy", "gz"))
    interior = brick // 4
    vmem = pl.BlockSpec(memory_space=pltpu.VMEM)

    def f32(*shape):
        return jax.ShapeDtypeStruct(shape, F32)

    def bf16(*shape):
        return jax.ShapeDtypeStruct(shape, BF16)

    def call(kernel, name, out_shape, operands, scratch=(), megabytes=4, flops=0):
        return pl.pallas_call(
            kernel,
            out_shape=out_shape,
            in_specs=[vmem] * len(operands),
            out_specs=(vmem,) * len(out_shape),
            scratch_shapes=scratch,
            compiler_params=pltpu.CompilerParams(vmem_limit_bytes=megabytes * 1024 * 1024),
            cost_estimate=pl.CostEstimate(flops=flops, bytes_accessed=1024, transcendentals=0),
            name=name,
        )(*operands)

    operands = (
        block_cells.reshape(1, blocks), fill_counts.reshape(1, 1), offsets, velocity, affine, volume.reshape(blocks, LANES), cot_velocity, cot_affine,
        baffle_top, drag.transpose(0, 2, 1),
    )
    slab = f32(ROWS, LANES)
    ends = 2 if counts[2] > 2 else 1
    (spread,) = call(spread_kernel, "spread", (bf16(21 * LANES, 2 * LANES),), (), flops=20_000_000_000)
    edge, send_xe, send_xo, send_xz, meta, shape, window, hot_edge = call(
        deposit_kernel,
        "deposit",
        (
            f32(2, ROWS, LANES), f32(192, LANES), slab, f32(ends, 16, LANES),
            jax.ShapeDtypeStruct((3, blocks, LANES), jnp.int32), f32(12 * blocks, LANES),
            bf16(16 * blocks, 2 * LANES), bf16(16 * blocks, 2 * LANES),
        ),
        operands + (spread,),
        scratch=[
            pltpu.VMEM((27 * blocks, LANES), F32),
            pltpu.VMEM((18 * blocks, 21 * LANES), BF16),
            pltpu.VMEM((18 * blocks, 2 * LANES), F32),
            pltpu.VMEM((2 * LANES, 2 * LANES), F32),
        ],
        megabytes=16,
    )

    def even_x(x):
        return paired(x, counts[0], 0)

    def odd_x(x, y, z):
        partner = paired(x, counts[0], 1)
        return (x, y, paired(z, counts[2], 0)) if partner is None else (partner, y, z)

    def odd_xz(x, y, z, first):
        partner = paired(x, counts[0], 1)
        return x if partner is None else partner, y, paired(z, counts[2], first)

    def odd_y(x, y, z):
        partner = paired(y, counts[1], 1)
        return (even_x(x), y, z) if partner is None else (x, partner, z)

    xe = exchange(send_xe, counts, lambda x, y, z: (even_x(x), y, z))
    xo = exchange(send_xo, counts, odd_x)
    xz = [
        exchange(send_xz[first], counts, lambda x, y, z: odd_xz(x, y, z, first))
        for first in range(ends)
    ]
    grid, hot = call(
        interior_kernel,
        "interior",
        (f32(2 + interior, ROWS, LANES), bf16(16 * blocks, (2 + interior) * LANES)),
        (window, meta, *operands[-2:]),
        scratch=[pltpu.VMEM((2 * LANES, (2 + interior) * LANES), F32)],
        megabytes=8,
        flops=1_000_000_000,
    )
    (xo,) = call(keep_kernel, "keep", (slab,), (xo,), flops=400_000_000)
    send_z = call(pack_z_kernel, "pack_z", (f32(3 * (2 + interior) // 2, 8, LANES),) * ends, (edge, grid, xe))
    layers = [
        exchange(array, counts, lambda x, y, z: (x, y, paired(z, counts[2], first)))
        for first, array in enumerate(send_z)
    ]
    send_ye, send_yo, near_y = call(
        functools.partial(pack_y_kernel, ends), "pack_y", (slab, slab, f32(2, ROWS, LANES)), (grid, xe, xo, *xz, *layers)
    )
    yo = exchange(send_yo, counts, odd_y)
    ye = exchange(send_ye, counts, lambda x, y, z: (x, paired(y, counts[1], 0), z))
    gathered, drag_slab, drag_rows, masked, take = call(
        functools.partial(early_kernel, counts, ends, size_z),
        "early",
        (
            f32(16 * blocks, LANES), f32(2, size_z, LANES), f32(interior, size_z, LANES),
            bf16(16 * blocks, 4 * LANES), bf16(2 * LANES, 9 * LANES),
        ),
        (meta, hot_edge, hot, edge, grid, xe, xo, *xz, *layers),
        scratch=[
            pltpu.VMEM((interior, ROWS + 24, LANES), F32),
            pltpu.VMEM((LANES, 2 * LANES), BF16),
            pltpu.VMEM((LANES, interior * LANES), BF16),
        ],
        megabytes=8,
        flops=1_000_000_000,
    )
    grad_velocity, grad_affine, grad_volume, grad_drag = call(
        functools.partial(collect_kernel, counts),
        "collect",
        (f32(3, blocks * LANES), f32(9, blocks * LANES), f32(blocks, LANES), f32(brick, size_z, brick)),
        (meta, shape, masked, take, baffle_top, gathered, drag_slab, drag_rows, near_y, ye, yo),
        scratch=[
            pltpu.VMEM((2, ROWS + 24, LANES), F32),
            pltpu.VMEM((LANES, 4 * LANES), BF16),
            pltpu.VMEM((2, size_z, LANES), F32),
            pltpu.VMEM((9 * blocks, 2 * LANES), BF16),
            pltpu.VMEM((9 * blocks, 9 * LANES), F32),
            pltpu.VMEM((12 * blocks, LANES), F32),
        ],
        megabytes=12,
    )
    return grad_velocity, grad_affine, grad_volume.reshape(-1), grad_drag.transpose(0, 2, 1)


def solution(mesh):
    everywhere = ("gx", "gy", "gz")
    rows, flat = P(None, everywhere), P(everywhere)
    in_specs = (rows, rows, rows, flat, rows, rows, flat, flat, P("gx", "gy"), P("gx", "gy", "gz"))
    out_specs = (rows, rows, flat, P("gx", "gy", "gz"))
    return jax.shard_map(shards, mesh=mesh, in_specs=in_specs, out_specs=out_specs, check_vma=False)
```
